32 devices in a mesh: dp: 2 (over core), ctx: 4 (over z), mp: 4 (over y, x).
Axes of the slice: x: 2, y: 2, z: 4, core: 2. Of those that a mesh axis runs over, the one named last changes fastest.
Arguments:
- image_states: bfloat16 [2, 1024, 8192], P('dp', 'ctx', 'mp'), may hold values from -6 to 6
- place_index: int32 [2, 1024], P('dp'), may hold values from 0 to 2047, as said below
- doc_ids: int32 [2, 2048], P('dp'), may hold values from 0 to 15, never falling along the last dimension, each value on 1 to 512 neighbouring positions
- queries: bfloat16 [2, 2048, 4096], P('dp', 'ctx', 'mp'), may hold values from -160 to 160
- text_kv: bfloat16 [2, 2048, 1024], P('dp', 'ctx', 'mp'), may hold values from -5.5 to 5.5
- kv_weight: bfloat16 [4, 8192, 256], P('mp'), may hold values from -0.0625 to 0.0625
- d_out: bfloat16 [2, 2048, 4096], P('dp', 'ctx', 'mp'), may hold values from -6 to 6
Outputs:
- attn_out: bfloat16 [2, 2048, 4096], P('dp', 'ctx', 'mp')
- image_grad: bfloat16 [2, 1024, 8192], P('dp', 'ctx', 'mp')
- kv_weight_grad: float32 [4, 8192, 256], P('mp', 'ctx')
The draws below stay inside these ranges and needn't reach their ends.
Inputs may be any that keep to these rules, and one draw needn't show every extreme that they name: `place_index`: images are whole blocks of 16 image tokens, consecutive in a vision rank's order and placed on 16 consecutive positions aligned to 16; every context shard of 512 positions holds exactly 256 image tokens; no position gets two image tokens; at most 64 image tokens of one vision rank lie in one context shard, and in every draw some vision rank places exactly 64 in some shard.
All inputs are finite; a program needn't handle non-finite values.
Results may differ from the reference program's by a relative error of at most 0.0085.
Values may be sent and summed in bfloat16 or wider, within the bound.
No kernel may reach another device: no remote copies, remote signals or barrier semaphores. Data moves between devices by JAX's collectives and lax.ppermute only.
A program may use at most 128 MiB of HBM per device.

```python
import math
import jax
import jax.numpy as jnp
import numpy as np
from jax import lax

D = 8192
HD = 128
KV_HEADS = 4
GROUP = 8
QH = 32
CTX_DEV = 512
IMGTOK = 16
IMG_DEV = 256
LEN = 2048
NIMG = 1024
DOCS = 16
N_DP = 2
N_CTX = 4


def image_layout(key):
    per_rank = IMG_DEV // IMGTOK
    blocks = CTX_DEV // IMGTOK

    def one_replica(replica_key):
        perm_key, slot_key = jax.random.split(replica_key)
        offsets = jax.random.permutation(perm_key, N_CTX).astype(jnp.int32)
        half_way = N_CTX // 2
        first_offset = offsets[0]
        slot_ids = jnp.arange(N_CTX, dtype=jnp.int32)
        offsets = jnp.where(offsets == half_way, first_offset, offsets)
        offsets = jnp.where(slot_ids == 0, half_way, offsets).astype(jnp.int32)
        rank_ids = jnp.arange(N_CTX, dtype=jnp.int32)[:, None]
        images = jnp.arange(per_rank, dtype=jnp.int32)[None, :]
        target = (rank_ids + offsets[images % N_CTX]) % N_CTX
        scores = jax.random.randint(slot_key, (N_CTX, blocks), 0, 1 << 20) * blocks + jnp.arange(blocks, dtype=jnp.int32)[None, :]
        block_order = jnp.argsort(scores, axis=1).astype(jnp.int32)
        chosen_block = block_order[target, jnp.broadcast_to(images, target.shape)]
        starts = target * CTX_DEV + chosen_block * IMGTOK
        positions = starts[:, :, None] + jnp.arange(IMGTOK, dtype=jnp.int32)[None, None, :]
        return positions.reshape(NIMG).astype(jnp.int32)
    return jax.vmap(one_replica)(jax.random.split(key, N_DP))


def attention_inputs(key):
    query_key = jax.random.fold_in(key, 11)
    value_key = jax.random.fold_in(key, 13)
    query_vals = jnp.clip(jax.random.normal(query_key, (N_DP, LEN, QH * HD), jnp.float32), -5.5, 5.5)
    key_values = jnp.clip(jax.random.normal(value_key, (N_DP, LEN, KV_HEADS * 2 * HD), jnp.float32), -5.5, 5.5)
    return (query_vals, key_values)


def draw_place_index(key, part):
    return image_layout(jax.random.fold_in(key, 7))


def draw_queries(key, part):
    return attention_inputs(key)[0].astype(jnp.bfloat16)


def draw_text_kv(key, part):
    return attention_inputs(key)[1].astype(jnp.bfloat16)


def level_of(own_key, extent, shards, low, largest):
    gain = 1.0
    for dim, shards_of in shards:
        draws = jax.random.uniform(jax.random.fold_in(jax.random.fold_in(own_key, 6), dim), (shards_of,), jnp.float32, low / len(shards), largest / len(shards))
        gain = gain * jnp.repeat(jnp.exp(draws), extent[dim] // shards_of).reshape((-1,) + (1,) * (len(extent) - 1 - dim))
    return gain


def length_profile(amount, total, most, slope):
    portions = [(1 << 20) // math.isqrt(rank ** slope) + 1 for rank in range(2, amount + 1)]
    rest, counts = total - most - (amount - 1), [1] * (amount - 1)
    while rest > 0:
        candidates = [i for i in range(amount - 1) if counts[i] < most]
        whole, remaining = sum([portions[i] for i in candidates]), rest
        for i in candidates:
            extra = min(most - counts[i], max(1, remaining * portions[i] // whole), rest)
            counts[i] = counts[i] + extra
            rest = rest - extra
    return np.array([most] + counts)


def uneven(own_key, count, total, most, slope):
    if count == 2:
        one = jax.random.randint(own_key, (), max(1, total - most), min(most, total - 1) + 1)
        return jnp.stack([one, total - one])
    tallies = jnp.asarray(length_profile(count, total, most, slope), jnp.int32)
    twos = (count - 1) // 2
    donor, receiver = tallies[1:1 + 2 * twos:2], tallies[2:2 + 2 * twos:2]
    slack = jnp.minimum(donor - 1, most - receiver)
    passed = jax.random.randint(jax.random.fold_in(own_key, 1), (twos,), 0, 1 << 20) % (slack + 1)
    tallies = tallies.at[1:1 + 2 * twos:2].set(donor - passed).at[2:2 + 2 * twos:2].set(receiver + passed)
    return tallies[jax.random.permutation(jax.random.fold_in(own_key, 2), count)]


def noise(rng, extent, spread, bound, cuts=(), kind=jnp.bfloat16):
    gain = level_of(rng, extent, cuts, -0.22, 0.18) if cuts else 1.0
    result = jax.random.normal(rng, extent, jnp.float32) * spread * gain
    return jnp.minimum(jnp.maximum(result, -bound), bound).astype(kind)


def setup_inputs(seed: int = 0) -> dict:
    keys = jax.random.split(jax.random.key(seed), 8)
    return {
        "image_states": noise(keys[0], (N_DP, NIMG, D), 1.0, 6.0, ((0, 2), (1, 4), (2, 4))),
        "place_index": draw_place_index(jax.random.fold_in(keys[7], 71), 0),
        "doc_ids": jax.vmap(lambda own: jnp.searchsorted(jnp.cumsum(uneven(own, DOCS, LEN, CTX_DEV, 2)), jnp.arange(LEN), side="right"))(jax.random.split(keys[2], N_DP)).reshape((N_DP, LEN)).astype(jnp.int32),
        "queries": draw_queries(jax.random.fold_in(keys[7], 71), 0),
        "text_kv": draw_text_kv(jax.random.fold_in(keys[7], 71), 0),
        "kv_weight": noise(keys[5], (KV_HEADS, D, 2 * HD), D ** -0.5, 0.0625, ((0, 4),)),
        "d_out": noise(keys[6], (N_DP, LEN, QH * HD), 1.0, 6.0, ((0, 2), (1, 4), (2, 4))),
    }


def shard_pass(query_rows, grad_rows, key_window, key_docs, own_docs):
    score_scale = HD ** -0.5
    query_all = query_rows.reshape(CTX_DEV, KV_HEADS, GROUP, HD).astype(jnp.float32)
    grad_all = grad_rows.reshape(CTX_DEV, KV_HEADS, GROUP, HD).astype(jnp.float32)
    parted = key_window.reshape(2 * CTX_DEV, KV_HEADS, 2, HD).astype(jnp.float32)
    key_part = parted[:, :, 0, :]
    value_part = parted[:, :, 1, :]
    query_pos = jnp.arange(CTX_DEV, dtype=jnp.int32)
    key_pos = jnp.arange(2 * CTX_DEV, dtype=jnp.int32) - CTX_DEV
    allowed = (key_pos[None, :] <= query_pos[:, None]) & (key_docs[None, :] == own_docs[:, None])
    scores = jnp.einsum('qhgd,khd->hgqk', query_all, key_part) * score_scale
    scores = jnp.where(allowed[None, None], scores, -1e30)
    shifted = jnp.exp(scores - jnp.max(scores, axis=3, keepdims=True))
    shifted = jnp.where(allowed[None, None], shifted, 0.0)
    attention = shifted / jnp.sum(shifted, axis=3, keepdims=True)
    attention_low = lax.optimization_barrier(attention.astype(jnp.bfloat16)).astype(jnp.float32)
    context = jnp.einsum('hgqk,khd->qhgd', attention_low, value_part)
    grad_attention = jnp.einsum('qhgd,khd->hgqk', grad_all, value_part)
    row_delta = jnp.einsum('qhgd,qhgd->hgq', grad_all, context)[..., None]
    grad_scores = attention * (grad_attention - row_delta)
    grad_scores = lax.optimization_barrier(grad_scores.astype(jnp.bfloat16)).astype(jnp.float32)
    key_grad = score_scale * jnp.einsum('hgqk,qhgd->khd', grad_scores, query_all)
    value_grad = jnp.einsum('hgqk,qhgd->khd', attention_low, grad_all)
    kv_grad = jnp.stack([key_grad, value_grad], axis=2).reshape(2 * CTX_DEV, KV_HEADS * 2 * HD)
    return context.astype(jnp.bfloat16).reshape(CTX_DEV, QH * HD), kv_grad


def reference(image_states, place_index, doc_ids, queries, text_kv, kv_weight, d_out):
    heads_weight = kv_weight.transpose(1, 0, 2).reshape(D, KV_HEADS * 2 * HD)
    flat_states = image_states.reshape(N_DP * NIMG, D)
    image_kv = jnp.dot(flat_states, heads_weight, preferred_element_type=jnp.float32).astype(jnp.bfloat16)
    image_kv = image_kv.reshape(N_DP, NIMG, KV_HEADS * 2 * HD)
    out_list = []
    grad_list = []
    for replica in range(N_DP):
        kv_full = text_kv[replica].at[place_index[replica]].set(image_kv[replica])
        padded_kv = jnp.concatenate([jnp.zeros((CTX_DEV, KV_HEADS * 2 * HD), jnp.bfloat16), kv_full], axis=0)
        padded_docs = jnp.concatenate([jnp.full((CTX_DEV,), -1, jnp.int32), doc_ids[replica]], axis=0)
        replica_queries = queries[replica]
        replica_grads = d_out[replica]
        replica_docs = doc_ids[replica]

        def one_shard(running_sums, shard_index):
            first_row = shard_index * CTX_DEV
            key_window = lax.dynamic_slice_in_dim(padded_kv, first_row, 2 * CTX_DEV)
            key_docs = lax.dynamic_slice_in_dim(padded_docs, first_row, 2 * CTX_DEV)
            own_docs = lax.dynamic_slice_in_dim(replica_docs, first_row, CTX_DEV)
            query_rows = lax.dynamic_slice_in_dim(replica_queries, first_row, CTX_DEV)
            grad_rows = lax.dynamic_slice_in_dim(replica_grads, first_row, CTX_DEV)
            output, kv_grad = shard_pass(query_rows, grad_rows, key_window, key_docs, own_docs)
            current = lax.dynamic_slice_in_dim(running_sums, first_row, 2 * CTX_DEV)
            running_sums = lax.dynamic_update_slice_in_dim(running_sums, current + kv_grad, first_row, 0)
            return running_sums, output

        initial = jnp.zeros(((N_CTX + 1) * CTX_DEV, KV_HEADS * 2 * HD), jnp.float32)
        grad_padded, outputs = lax.scan(one_shard, initial, jnp.arange(N_CTX, dtype=jnp.int32))
        out_list.append(outputs.reshape(LEN, QH * HD))
        grad_list.append(grad_padded[CTX_DEV:][place_index[replica]].astype(jnp.bfloat16))
    attn_out = jnp.stack(out_list)
    flat_grad = jnp.stack(grad_list).reshape(N_DP * NIMG, KV_HEADS * 2 * HD)
    image_grad = lax.dot_general(flat_grad, heads_weight, (((1,), (1,)), ((), ())), preferred_element_type=jnp.float32)
    image_grad = image_grad.astype(jnp.bfloat16).reshape(N_DP, NIMG, D)
    weight_flat = lax.dot_general(flat_states, flat_grad, (((0,), (0,)), ((), ())), preferred_element_type=jnp.float32)
    kv_weight_grad = weight_flat.reshape(D, KV_HEADS, 2 * HD).transpose(1, 0, 2)
    return attn_out, image_grad, kv_weight_grad
```

```python
import functools

import jax
import jax.numpy as jnp
from jax import lax
from jax.experimental import pallas as pl
from jax.experimental.pallas import tpu as pltpu
from jax.sharding import PartitionSpec as P

IMGTOK = 16
QTILE = 128
LOG2E = 1.4426950408889634
VMEM = 56 * 1024 * 1024

NN = (((1,), (0,)), ((), ()))
NT = (((1,), (1,)), ((), ()))
TN = (((0,), (0,)), ((), ()))


def dot(a, b, dims):
    return lax.dot_general(a, b, dims, preferred_element_type=jnp.float32)


def params():
    return pltpu.CompilerParams(vmem_limit_bytes=VMEM)


def shift(block, axis, distance):
    devices = range(lax.axis_size(axis))
    route = [(i - distance, i) for i in devices if i - distance in devices]
    return lax.ppermute(block, axis, route)


def swap(block, axis):
    count = lax.axis_size(axis)
    return lax.ppermute(block, axis, [(i, count - 1 - i) for i in range(count)])


def exchange(blocks, axis):
    return lax.all_to_all(blocks, axis, split_axis=0, concat_axis=0, tiled=True)


def rows16(start):
    return pl.ds(pl.multiple_of(start * IMGTOK, IMGTOK), IMGTOK)


def project_body(d_ref, s_ref, near_ref, far_ref, out_ref):
    half = near_ref.shape[1]
    d = d_ref[0]
    near = s_ref[:, pl.ds(pl.multiple_of(d * half, half), half)]
    far = s_ref[:, pl.ds(pl.multiple_of((1 - d) * half, half), half)]
    out_ref[0] = dot(near, near_ref[0], NN) + dot(far, far_ref[0], NN)


def project(d, states, near, far):
    heads, half, width = near.shape
    rows = states.shape[0]
    return pl.pallas_call(
        project_body,
        grid_spec=pltpu.PrefetchScalarGridSpec(
            num_scalar_prefetch=1,
            grid=(heads,),
            in_specs=[
                pl.BlockSpec(states.shape, lambda h, d: (0, 0)),
                pl.BlockSpec((1, half, width), lambda h, d: (h, 0, 0)),
                pl.BlockSpec((1, half, width), lambda h, d: (h, 0, 0)),
            ],
            out_specs=pl.BlockSpec((1, rows, width), lambda h, d: (h, 0, 0)),
        ),
        out_shape=jax.ShapeDtypeStruct((heads, rows, width), jnp.float32),
        compiler_params=params(),
    )(d, states, near, far)


def pack_body(per_shard, c_ref, place_ref, part_ref, out_ref, rounded, count):
    shards = out_ref.shape[0]
    total = part_ref[0]
    for m in range(1, part_ref.shape[0]):
        total = total + part_ref[m]
    rounded[...] = total.astype(jnp.bfloat16)
    out_ref[...] = jnp.zeros_like(out_ref)
    for s in range(shards):
        count[s] = 0
    images = rounded.shape[0] // IMGTOK
    c = c_ref[0]

    def step(i, carry):
        dest = place_ref[c * images + i] // per_shard
        slot = count[dest]
        count[dest] = slot + 1
        block = rounded[rows16(i), :]
        out_ref[dest, 0, rows16(slot), :] = block

        @pl.when(dest + 1 < shards)
        def _():
            out_ref[dest + 1, 1, rows16(slot), :] = block

        return carry

    lax.fori_loop(0, images, step, 0)


def pack(c, place, parts, shards, capacity, per_shard):
    _, rows, width = parts.shape
    smem = pl.BlockSpec(memory_space=pltpu.SMEM)
    vmem = pl.BlockSpec(memory_space=pltpu.VMEM)
    return pl.pallas_call(
        functools.partial(pack_body, per_shard),
        in_specs=[smem, smem, vmem],
        out_specs=vmem,
        out_shape=jax.ShapeDtypeStruct((shards, 2, capacity, width), jnp.bfloat16),
        scratch_shapes=[
            pltpu.VMEM((rows, width), jnp.bfloat16),
            pltpu.SMEM((shards,), jnp.int32),
        ],
        compiler_params=params(),
    )(c, place, parts)


def attention_body(
    per_shard,
    images,
    c_ref,
    place_ref,
    start_ref,
    q_ref,
    g_ref,
    own_ref,
    prior_ref,
    image_ref,
    out_ref,
    own_grad_ref,
    prior_grad_ref,
    window,
    probs,
    grads,
    total,
):
    t = pl.program_id(0)
    c = c_ref[0]
    rows = own_ref.shape[0]
    hd = own_ref.shape[1] // 2
    blocks = place_ref.shape[0]
    span = rows + QTILE
    heads = q_ref.shape[1] // hd
    scale = hd ** (-0.5)

    @pl.when(t == 0)
    def _():
        window[:rows, :] = prior_ref[...]
        window[rows:, :] = own_ref[...]
        total[...] = jnp.zeros_like(total)

        def step(b, carry):
            n_own, n_prior = carry
            rank = b // images
            fresh = b % images == 0
            n_own = jnp.where(fresh, 0, n_own)
            n_prior = jnp.where(fresh, 0, n_prior)
            at = place_ref[b] - (c - 1) * per_shard
            is_prior = (at >= 0) & (at < per_shard)
            is_own = (at >= per_shard) & (at < 2 * per_shard)

            @pl.when(is_own)
            def _():
                window[rows16(at), :] = image_ref[rank, 0, rows16(n_own), :]

            @pl.when(is_prior)
            def _():
                window[rows16(at), :] = image_ref[rank, 1, rows16(n_prior), :]

            return n_own + is_own.astype(jnp.int32), n_prior + is_prior.astype(jnp.int32)

        lax.fori_loop(0, blocks, step, (jnp.int32(0), jnp.int32(0)))

    first = pl.multiple_of(t * QTILE, QTILE)
    keys = window[pl.ds(first, span), :hd]
    values = window[pl.ds(first, span), hd:]
    values_t = values.T
    key_pos = lax.broadcasted_iota(jnp.int32, (span, QTILE), 0) + first
    query_pos = lax.broadcasted_iota(jnp.int32, (span, QTILE), 1) + (first + rows)
    allowed = (key_pos <= query_pos) & (key_pos >= start_ref[...])
    bias = jnp.where(allowed, 0.0, -1e30)
    bias = jnp.concatenate([bias, bias], axis=1)

    def stack(ref, a, b):
        return jnp.concatenate([ref[:, h * hd : (h + 1) * hd] for h in range(a, b)], axis=0)

    for h in range(0, heads, 2):
        query = stack(q_ref, h, h + 2)
        grad = stack(g_ref, h, h + 2)
        scores = dot(keys, query, NT) * (scale * LOG2E) + bias
        top = jnp.max(scores, axis=0, keepdims=True)
        e = jnp.exp2(scores - top)
        p = e * (1.0 / jnp.sum(e, axis=0, keepdims=True))
        low = p.astype(jnp.bfloat16)
        context_t = dot(values_t, low, NN)
        grad_p = dot(values, grad, NT)
        grad_t = grad.astype(jnp.float32).T
        delta = jnp.sum(grad_t * context_t, axis=0, keepdims=True)
        ds = (p * (grad_p - delta)).astype(jnp.bfloat16)
        context = context_t.T.astype(jnp.bfloat16)
        out_ref[:, h * hd : (h + 1) * hd] = context[:QTILE]
        out_ref[:, (h + 1) * hd : (h + 2) * hd] = context[QTILE:]
        probs[:, h * QTILE : (h + 2) * QTILE] = low
        grads[:, h * QTILE : (h + 2) * QTILE] = ds
    total[pl.ds(first, span), :hd] += dot(grads[...], stack(q_ref, 0, heads), NN)
    total[pl.ds(first, span), hd:] += dot(probs[...], stack(g_ref, 0, heads), NN)

    @pl.when(t == pl.num_programs(0) - 1)
    def _():
        total[:, :hd] = total[:, :hd] * scale
        prior_grad_ref[...] = jnp.zeros_like(prior_grad_ref)

        def step(b, carry):
            n_own, n_prior = carry
            at = place_ref[b] - (c - 1) * per_shard
            is_prior = (at >= 0) & (at < per_shard)
            is_own = (at >= per_shard) & (at < 2 * per_shard)

            @pl.when(is_own)
            def _():
                own_grad_ref[rows16(n_own), :] = total[rows16(at), :]

            @pl.when(is_prior)
            def _():
                prior_grad_ref[rows16(n_prior), :] = total[rows16(at), :]

            return n_own + is_own.astype(jnp.int32), n_prior + is_prior.astype(jnp.int32)

        lax.fori_loop(0, blocks, step, (jnp.int32(0), jnp.int32(0)))


def attention(c, place, start, queries, d_out, own, prior, image, images, per_shard, image_rows):
    rows, width = own.shape
    cols = queries.shape[1]
    tiles = rows // QTILE
    span = rows + QTILE
    head_rows = cols // (width // 2) * QTILE
    whole = lambda a: pl.BlockSpec(a.shape, lambda t, *_: (0,) * a.ndim)
    tile = pl.BlockSpec((QTILE, cols), lambda t, *_: (t, 0))
    grad = jax.ShapeDtypeStruct((image_rows, width), jnp.float32)
    return pl.pallas_call(
        functools.partial(attention_body, per_shard, images),
        grid_spec=pltpu.PrefetchScalarGridSpec(
            num_scalar_prefetch=2,
            grid=(tiles,),
            in_specs=[
                pl.BlockSpec((1, QTILE), lambda t, *_: (0, t)),
                tile,
                tile,
                whole(own),
                whole(prior),
                whole(image),
            ],
            out_specs=[tile, whole(grad), whole(grad)],
            scratch_shapes=[
                pltpu.VMEM((2 * rows, width), jnp.bfloat16),
                pltpu.VMEM((span, head_rows), jnp.bfloat16),
                pltpu.VMEM((span, head_rows), jnp.bfloat16),
                pltpu.VMEM((2 * rows, width), jnp.float32),
            ],
        ),
        out_shape=[jax.ShapeDtypeStruct((rows, cols), jnp.bfloat16), grad, grad],
        compiler_params=params(),
    )(c, place, start, queries, d_out, own, prior, image)


def reorder_body(per_shard, images, c_ref, place_ref, g_ref, out_ref, mine_ref, count):
    shards = g_ref.shape[0]
    for s in range(shards):
        count[s] = 0
    c = c_ref[0]

    def step(b, carry):
        dest = place_ref[b] // per_shard
        slot = count[dest]
        count[dest] = slot + 1
        out_ref[rows16(b), :] = g_ref[dest, rows16(slot), :]
        return carry

    lax.fori_loop(0, place_ref.shape[0], step, 0)
    rows = mine_ref.shape[1]
    mine = out_ref[pl.ds(pl.multiple_of(c * rows, IMGTOK), rows), :]
    for m in range(mine_ref.shape[0]):
        mine_ref[m] = mine


def reorder(c, place, gathered, copies, per_shard, images):
    shards, rows, width = gathered.shape
    smem = pl.BlockSpec(memory_space=pltpu.SMEM)
    vmem = pl.BlockSpec(memory_space=pltpu.VMEM)
    return pl.pallas_call(
        functools.partial(reorder_body, per_shard, images),
        in_specs=[smem, smem, vmem],
        out_specs=[vmem, vmem],
        out_shape=[
            jax.ShapeDtypeStruct((shards * rows, width), gathered.dtype),
            jax.ShapeDtypeStruct((copies, rows, width), gathered.dtype),
        ],
        scratch_shapes=[pltpu.SMEM((shards,), jnp.int32)],
        compiler_params=params(),
    )(c, place, gathered)


def weight_body(s_ref, g_ref, out_ref):
    out_ref[...] = dot(s_ref[0], g_ref[...], TN)


def weight_term(states, grad):
    parts, rows, cols = states.shape
    width = grad.shape[1]
    return pl.pallas_call(
        weight_body,
        grid=(parts,),
        in_specs=[
            pl.BlockSpec((1, rows, cols), lambda k: (k, 0, 0)),
            pl.BlockSpec((rows, width), lambda k: (0, 0)),
        ],
        out_specs=pl.BlockSpec((cols, width), lambda k: (k, 0)),
        out_shape=jax.ShapeDtypeStruct((parts * cols, width), jnp.float32),
        compiler_params=params(),
    )(states, grad)


def image_body(d_ref, g_ref, near_ref, far_ref, out_ref):
    j = pl.program_id(0)
    heads, cols, _ = near_ref.shape
    half = out_ref.shape[1] // 2
    d = d_ref[0]
    for ref, side in ((near_ref, d), (far_ref, 1 - d)):
        total = dot(g_ref[0], ref[0], NT)
        for h in range(1, heads):
            total = total + dot(g_ref[h], ref[h], NT)
        at = pl.multiple_of(side * half + j * cols, cols)
        out_ref[:, pl.ds(at, cols)] = total.astype(out_ref.dtype)


def image_term(d, grad, near, far):
    heads, half, width = near.shape
    rows = grad.shape[1]
    tiles = 4
    side = pl.BlockSpec((heads, half // tiles, width), lambda j, d: (0, j, 0))
    return pl.pallas_call(
        image_body,
        grid_spec=pltpu.PrefetchScalarGridSpec(
            num_scalar_prefetch=1,
            grid=(tiles,),
            in_specs=[pl.BlockSpec(grad.shape, lambda j, d: (0, 0, 0)), side, side],
            out_specs=pl.BlockSpec((rows, 2 * half), lambda j, d: (0, 0)),
        ),
        out_shape=jax.ShapeDtypeStruct((rows, 2 * half), jnp.bfloat16),
        compiler_params=params(),
    )(d, grad, near, far)


def per_device(image_states, place_index, doc_ids, queries, text_kv, kv_weight, d_out):
    ranks = lax.axis_size("ctx")
    mps = lax.axis_size("mp")
    c = lax.axis_index("ctx")
    d = lax.axis_index("dp")
    rows = queries.shape[1]
    states = image_states[0]
    image_rows, feats = states.shape
    images = image_rows // IMGTOK
    per_shard = rows // IMGTOK
    capacity = IMGTOK * ((images + ranks - 1) // ranks)
    weights = kv_weight[0]
    width = weights.shape[1]
    c1 = jnp.reshape(c, (1,)).astype(jnp.int32)
    d1 = jnp.reshape(d, (1,)).astype(jnp.int32)
    place = place_index[0, ::IMGTOK] // IMGTOK

    halves = weights.reshape(mps, 2, feats // 2, width)
    mine = lax.dynamic_index_in_dim(halves, d, axis=1, keepdims=False)
    near = exchange(mine, "mp")
    far = swap(near, "dp")

    sub = feats * mps // ranks // mps
    per_mp = ranks // mps
    pieces = states.reshape(image_rows, per_mp, mps, sub).transpose(2, 0, 1, 3)
    pieces = exchange(pieces, "mp")
    pieces = pieces.transpose(0, 2, 1, 3).reshape(ranks, image_rows, sub)
    pieces = exchange(pieces, "ctx").reshape(ranks * image_rows, sub)
    all_states = lax.all_gather(pieces, "mp", axis=0)

    prior_text = shift(text_kv[0], "ctx", 1)
    docs = doc_ids[0]
    own_docs = lax.dynamic_slice_in_dim(docs, c * rows, rows)
    prior_docs = lax.dynamic_slice_in_dim(docs, jnp.maximum(c - 1, 0) * rows, rows)
    prior_docs = jnp.where(c > 0, prior_docs, -1)
    key_docs = jnp.concatenate([prior_docs, own_docs])
    start = jnp.sum((key_docs[:, None] < own_docs[None, :]).astype(jnp.int32), axis=0)[None]

    parts = exchange(project(d1, states, near, far), "mp")
    packed = pack(c1, place, parts, ranks, capacity, per_shard)
    image = exchange(packed, "ctx")
    attn_out, own_grad, prior_grad = attention(
        c1, place, start, queries[0], d_out[0], text_kv[0], prior_text, image,
        images, per_shard, image_rows,
    )
    grad = (own_grad + shift(prior_grad, "ctx", -1)).astype(jnp.bfloat16)
    gathered = exchange(jnp.broadcast_to(grad, (ranks,) + grad.shape), "ctx")
    by_rank, mine = reorder(c1, place, gathered, mps, per_shard, images)
    head_grad = exchange(mine, "mp")
    image_grad = image_term(d1, head_grad, near, far)
    term = weight_term(all_states, by_rank)
    weight_grad = term + swap(term, "dp")
    return (attn_out[None], image_grad[None], weight_grad[None])


def solution(mesh):
    in_specs = (
        P("dp", "ctx", "mp"),
        P("dp", None),
        P("dp", None),
        P("dp", "ctx", "mp"),
        P("dp", "ctx", "mp"),
        P("mp", None, None),
        P("dp", "ctx", "mp"),
    )
    out_specs = (P("dp", "ctx", "mp"), P("dp", "ctx", "mp"), P("mp", "ctx", None))
    return jax.shard_map(
        per_device, mesh=mesh, in_specs=in_specs, out_specs=out_specs, check_vma=False
    )
```

```python
import functools

import jax
import jax.numpy as jnp
from jax import lax
from jax.experimental import pallas as pl
from jax.experimental.pallas import tpu as pltpu
from jax.sharding import PartitionSpec as P

IMGTOK = 16
QTILE = 128
LOG2E = 1.4426950408889634
VMEM = 24 * 1024 * 1024

NN = (((1,), (0,)), ((), ()))
NT = (((1,), (1,)), ((), ()))
TN = (((0,), (0,)), ((), ()))


def dot(a, b, dims):
    return lax.dot_general(a, b, dims, preferred_element_type=jnp.float32)


def params():
    return pltpu.CompilerParams(vmem_limit_bytes=VMEM)


def cost(flops, moved):
    return pl.CostEstimate(flops=int(flops), bytes_accessed=int(moved), transcendentals=0)


def shift(block, axis, distance):
    devices = range(lax.axis_size(axis))
    route = [(i - distance, i) for i in devices if i - distance in devices]
    return lax.ppermute(block, axis, route)


def swap(block, axis):
    count = lax.axis_size(axis)
    return lax.ppermute(block, axis, [(i, count - 1 - i) for i in range(count)])


def exchange(blocks, axis):
    return lax.all_to_all(blocks, axis, split_axis=0, concat_axis=0, tiled=True)


def trade(block, axis, step):
    count = lax.axis_size(axis)
    return lax.ppermute(block, axis, [(i, i ^ step) for i in range(count)])


def rows16(start):
    return pl.ds(pl.multiple_of(start * IMGTOK, IMGTOK), IMGTOK)


def project_body(d_ref, s_ref, near_ref, far_ref, out_ref):
    half = near_ref.shape[0]
    d = d_ref[0]
    near = s_ref[:, pl.ds(pl.multiple_of(d * half, half), half)]
    far = s_ref[:, pl.ds(pl.multiple_of((1 - d) * half, half), half)]
    out_ref[...] = dot(near, near_ref[...], NN) + dot(far, far_ref[...], NN)


def project(d, states, near, far):
    half, width = near.shape
    rows = states.shape[0]
    vmem = pl.BlockSpec(memory_space=pltpu.VMEM)
    return pl.pallas_call(
        project_body,
        in_specs=[pl.BlockSpec(memory_space=pltpu.SMEM), vmem, vmem, vmem],
        out_specs=vmem,
        out_shape=jax.ShapeDtypeStruct((rows, width), jnp.float32),
        cost_estimate=cost(4 * rows * half * width, 4 * states.size),
        compiler_params=params(),
    )(d, states, near, far)


def pack_body(per_shard, c_ref, place_ref, *refs):
    *part_refs, out_ref, rounded, count = refs
    shards = out_ref.shape[0]
    total = part_refs[0][...]
    for ref in part_refs[1:]:
        total = total + ref[...]
    rounded[...] = total.astype(jnp.bfloat16)
    out_ref[...] = jnp.zeros_like(out_ref)
    for s in range(shards):
        count[s] = 0
    images = rounded.shape[0] // IMGTOK
    c = c_ref[0]

    def step(i, carry):
        dest = place_ref[c * images + i] // per_shard
        slot = count[dest]
        count[dest] = slot + 1
        block = rounded[rows16(i), :]
        out_ref[dest, 0, rows16(slot), :] = block

        @pl.when(dest + 1 < shards)
        def _():
            out_ref[dest + 1, 1, rows16(slot), :] = block

        return carry

    lax.fori_loop(0, images, step, 0)


def pack(c, place, parts, shards, capacity, per_shard):
    rows, width = parts[0].shape
    smem = pl.BlockSpec(memory_space=pltpu.SMEM)
    vmem = pl.BlockSpec(memory_space=pltpu.VMEM)
    return pl.pallas_call(
        functools.partial(pack_body, per_shard),
        in_specs=[smem, smem] + [vmem] * len(parts),
        out_specs=vmem,
        out_shape=jax.ShapeDtypeStruct((shards, 2, capacity, width), jnp.bfloat16),
        scratch_shapes=[
            pltpu.VMEM((rows, width), jnp.bfloat16),
            pltpu.SMEM((shards,), jnp.int32),
        ],
        cost_estimate=cost(0, parts[0].size * 4 * 6),
        compiler_params=params(),
    )(c, place, *parts)


def attention_body(
    per_shard,
    images,
    c_ref,
    place_ref,
    start_ref,
    q_ref,
    g_ref,
    own_ref,
    prior_ref,
    image_ref,
    out_ref,
    own_grad_ref,
    prior_grad_ref,
    window,
    probs,
    grads,
    total,
):
    t = pl.program_id(0)
    c = c_ref[0]
    rows = own_ref.shape[0]
    hd = own_ref.shape[1] // 2
    blocks = place_ref.shape[0]
    span = rows + QTILE
    heads = q_ref.shape[1] // hd
    scale = hd ** (-0.5)

    @pl.when(t == 0)
    def _():
        window[:rows, :] = prior_ref[...]
        window[rows:, :] = own_ref[...]
        total[...] = jnp.zeros_like(total)

        def step(b, carry):
            n_own, n_prior = carry
            rank = b // images
            fresh = b % images == 0
            n_own = jnp.where(fresh, 0, n_own)
            n_prior = jnp.where(fresh, 0, n_prior)
            at = place_ref[b] - (c - 1) * per_shard
            is_prior = (at >= 0) & (at < per_shard)
            is_own = (at >= per_shard) & (at < 2 * per_shard)

            @pl.when(is_own)
            def _():
                window[rows16(at), :] = image_ref[rank, 0, rows16(n_own), :]

            @pl.when(is_prior)
            def _():
                window[rows16(at), :] = image_ref[rank, 1, rows16(n_prior), :]

            return n_own + is_own.astype(jnp.int32), n_prior + is_prior.astype(jnp.int32)

        lax.fori_loop(0, blocks, step, (jnp.int32(0), jnp.int32(0)))

    first = pl.multiple_of(t * QTILE, QTILE)
    keys = window[pl.ds(first, span), :hd]
    values = window[pl.ds(first, span), hd:]
    values_t = values.T
    key_pos = lax.broadcasted_iota(jnp.int32, (span, QTILE), 0) + first
    query_pos = lax.broadcasted_iota(jnp.int32, (span, QTILE), 1) + (first + rows)
    allowed = (key_pos <= query_pos) & (key_pos >= start_ref[...])
    bias = jnp.where(allowed, 0.0, -1e30)
    bias = jnp.concatenate([bias, bias], axis=1)

    def stack(ref, a, b):
        return jnp.concatenate([ref[:, h * hd : (h + 1) * hd] for h in range(a, b)], axis=0)

    for h in range(0, heads, 2):
        query = stack(q_ref, h, h + 2)
        grad = stack(g_ref, h, h + 2)
        scores = dot(keys, query, NT) * (scale * LOG2E) + bias
        top = jnp.max(scores, axis=0, keepdims=True)
        e = jnp.exp2(scores - top)
        p = e * (1.0 / jnp.sum(e, axis=0, keepdims=True))
        low = p.astype(jnp.bfloat16)
        context_t = dot(values_t, low, NN)
        grad_p = dot(values, grad, NT)
        grad_t = grad.astype(jnp.float32).T
        delta = jnp.sum(grad_t * context_t, axis=0, keepdims=True)
        ds = (p * (grad_p - delta)).astype(jnp.bfloat16)
        context = context_t.T.astype(jnp.bfloat16)
        out_ref[:, h * hd : (h + 1) * hd] = context[:QTILE]
        out_ref[:, (h + 1) * hd : (h + 2) * hd] = context[QTILE:]
        probs[:, h * QTILE : (h + 2) * QTILE] = low
        grads[:, h * QTILE : (h + 2) * QTILE] = ds
    total[pl.ds(first, span), :hd] += dot(grads[...], stack(q_ref, 0, heads), NN)
    total[pl.ds(first, span), hd:] += dot(probs[...], stack(g_ref, 0, heads), NN)

    @pl.when(t == pl.num_programs(0) - 1)
    def _():
        total[:, :hd] = total[:, :hd] * scale
        prior_grad_ref[...] = jnp.zeros_like(prior_grad_ref)

        def step(b, carry):
            n_own, n_prior = carry
            at = place_ref[b] - (c - 1) * per_shard
            is_prior = (at >= 0) & (at < per_shard)
            is_own = (at >= per_shard) & (at < 2 * per_shard)

            @pl.when(is_own)
            def _():
                own_grad_ref[rows16(n_own), :] = total[rows16(at), :]

            @pl.when(is_prior)
            def _():
                prior_grad_ref[rows16(n_prior), :] = total[rows16(at), :]

            return n_own + is_own.astype(jnp.int32), n_prior + is_prior.astype(jnp.int32)

        lax.fori_loop(0, blocks, step, (jnp.int32(0), jnp.int32(0)))


def attention(c, place, start, queries, d_out, own, prior, image, images, per_shard, image_rows):
    rows, width = own.shape
    cols = queries.shape[1]
    tiles = rows // QTILE
    span = rows + QTILE
    head_rows = cols // (width // 2) * QTILE
    whole = lambda a: pl.BlockSpec(a.shape, lambda t, *_: (0,) * a.ndim)
    tile = pl.BlockSpec((QTILE, cols), lambda t, *_: (t, 0))
    grad = jax.ShapeDtypeStruct((image_rows, width), jnp.float32)
    return pl.pallas_call(
        functools.partial(attention_body, per_shard, images),
        grid_spec=pltpu.PrefetchScalarGridSpec(
            num_scalar_prefetch=2,
            grid=(tiles,),
            in_specs=[
                pl.BlockSpec((1, QTILE), lambda t, *_: (0, t)),
                tile,
                tile,
                whole(own),
                whole(prior),
                whole(image),
            ],
            out_specs=[tile, whole(grad), whole(grad)],
            scratch_shapes=[
                pltpu.VMEM((2 * rows, width), jnp.bfloat16),
                pltpu.VMEM((span, head_rows), jnp.bfloat16),
                pltpu.VMEM((span, head_rows), jnp.bfloat16),
                pltpu.VMEM((2 * rows, width), jnp.float32),
            ],
        ),
        out_shape=[jax.ShapeDtypeStruct((rows, cols), jnp.bfloat16), grad, grad],
        cost_estimate=cost(2 * 20 * cols * span * rows, 4 * queries.size * 2),
        compiler_params=params(),
    )(c, place, start, queries, d_out, own, prior, image)


def reorder_body(per_shard, images, c_ref, place_ref, g_ref, out_ref, mine_ref, count):
    shards = g_ref.shape[0]
    for s in range(shards):
        count[s] = 0
    c = c_ref[0]

    def step(b, carry):
        dest = place_ref[b] // per_shard
        slot = count[dest]
        count[dest] = slot + 1
        out_ref[rows16(b), :] = g_ref[dest, rows16(slot), :]
        return carry

    lax.fori_loop(0, place_ref.shape[0], step, 0)
    rows = mine_ref.shape[0]
    mine_ref[...] = out_ref[pl.ds(pl.multiple_of(c * rows, IMGTOK), rows), :]


def reorder(c, place, gathered, per_shard, images):
    shards, rows, width = gathered.shape
    smem = pl.BlockSpec(memory_space=pltpu.SMEM)
    vmem = pl.BlockSpec(memory_space=pltpu.VMEM)
    return pl.pallas_call(
        functools.partial(reorder_body, per_shard, images),
        in_specs=[smem, smem, vmem],
        out_specs=[vmem, vmem],
        out_shape=[
            jax.ShapeDtypeStruct((shards * rows, width), gathered.dtype),
            jax.ShapeDtypeStruct((rows, width), gathered.dtype),
        ],
        scratch_shapes=[pltpu.SMEM((shards,), jnp.int32)],
        cost_estimate=cost(0, gathered.size * 2 * 4),
        compiler_params=params(),
    )(c, place, gathered)


def weight_body(mixed, s_ref, g_ref, out_ref):
    k = pl.program_id(0)
    ranks, rows, _ = g_ref.shape
    if not mixed:
        out_ref[...] = dot(s_ref[0], g_ref[...].reshape(ranks * rows, -1), TN)
        return
    grad = jnp.concatenate([g_ref[k ^ s] for s in range(ranks)], axis=0)
    out_ref[...] = dot(s_ref[0], grad, TN)


def weight_term(states, grad, mixed):
    parts, rows, cols = states.shape
    width = grad.shape[2]
    return pl.pallas_call(
        functools.partial(weight_body, mixed),
        grid=(parts,),
        in_specs=[
            pl.BlockSpec((1, rows, cols), lambda k: (k, 0, 0)),
            pl.BlockSpec(grad.shape, lambda k: (0, 0, 0)),
        ],
        out_specs=pl.BlockSpec((cols, width), lambda k: (k, 0)),
        out_shape=jax.ShapeDtypeStruct((parts * cols, width), jnp.float32),
        cost_estimate=cost(2 * states.size * width, states.size * 4),
        compiler_params=params(),
    )(states, grad)


def image_body(d_ref, *refs):
    out_ref = refs[-1]
    heads = (len(refs) - 1) // 3
    grads, sides = refs[:heads], (refs[heads : 2 * heads], refs[2 * heads : -1])
    j = pl.program_id(0)
    cols = sides[0][0].shape[0]
    half = out_ref.shape[1] // 2
    d = d_ref[0]
    for refs_of, side in zip(sides, (d, 1 - d)):
        total = dot(grads[0][...], refs_of[0][...], NT)
        for h in range(1, heads):
            total = total + dot(grads[h][...], refs_of[h][...], NT)
        at = pl.multiple_of(side * half + j * cols, cols)
        out_ref[:, pl.ds(at, cols)] = total.astype(out_ref.dtype)


def image_term(d, grads, near, far):
    heads = len(near)
    half, width = near[0].shape
    rows = grads[0].shape[0]
    tiles = 4
    side = pl.BlockSpec((half // tiles, width), lambda j, d: (j, 0))
    grad = pl.BlockSpec((rows, width), lambda j, d: (0, 0))
    return pl.pallas_call(
        image_body,
        grid_spec=pltpu.PrefetchScalarGridSpec(
            num_scalar_prefetch=1,
            grid=(tiles,),
            in_specs=[grad] * heads + [side] * (2 * heads),
            out_specs=pl.BlockSpec((rows, 2 * half), lambda j, d: (0, 0)),
        ),
        out_shape=jax.ShapeDtypeStruct((rows, 2 * half), jnp.bfloat16),
        cost_estimate=cost(4 * heads * near[0].size * rows, 4 * heads * near[0].size * 2),
        compiler_params=params(),
    )(d, *grads, *near, *far)


def per_device(image_states, place_index, doc_ids, queries, text_kv, kv_weight, d_out):
    ranks = lax.axis_size("ctx")
    mps = lax.axis_size("mp")
    c = lax.axis_index("ctx")
    d = lax.axis_index("dp")
    rows = queries.shape[1]
    states = image_states[0]
    image_rows, feats = states.shape
    images = image_rows // IMGTOK
    per_shard = rows // IMGTOK
    capacity = IMGTOK * ((images + ranks - 1) // ranks)
    weights = kv_weight[0]
    width = weights.shape[1]
    c1 = jnp.reshape(c, (1,)).astype(jnp.int32)
    d1 = jnp.reshape(d, (1,)).astype(jnp.int32)
    place = place_index[0, ::IMGTOK] // IMGTOK

    m = lax.axis_index("mp")
    steps = range(mps)

    half = feats // 2
    near = [
        lax.dynamic_slice_in_dim(weights, (m ^ s) * feats + d * half, half) for s in steps
    ]
    near = [trade(near[s], "mp", s) if s else near[0] for s in steps]
    far = [swap(near[s], "dp") for s in steps]

    prior_text = shift(text_kv[0], "ctx", 1)
    docs = doc_ids[0]
    own_docs = lax.dynamic_slice_in_dim(docs, c * rows, rows)
    prior_docs = lax.dynamic_slice_in_dim(docs, jnp.maximum(c - 1, 0) * rows, rows)
    prior_docs = jnp.where(c > 0, prior_docs, -1)
    key_docs = jnp.concatenate([prior_docs, own_docs])
    start = jnp.sum((key_docs[:, None] < own_docs[None, :]).astype(jnp.int32), axis=0)[None]

    sub = feats // (ranks // mps) // mps
    mixed = ranks == mps
    *near, states_late, prior_text, start, place = lax.optimization_barrier(
        (*near, states, prior_text, start, place)
    )
    if mixed:
        pieces = []
        for s in steps:
            piece = lax.dynamic_slice_in_dim(states_late, (c ^ s) * sub, sub, axis=1)
            route = [
                (i * mps + j, j * mps + (i ^ s)) for i in range(ranks) for j in range(mps)
            ]
            pieces.append(lax.ppermute(piece, ("ctx", "mp"), route))
        pieces = jnp.concatenate(pieces, axis=0)
    else:
        pieces = states_late.reshape(image_rows, ranks // mps, mps, sub).transpose(2, 0, 1, 3)
        pieces = exchange(pieces, "mp")
        pieces = pieces.transpose(0, 2, 1, 3).reshape(ranks, image_rows, sub)
        pieces = exchange(pieces, "ctx").reshape(ranks * image_rows, sub)
    all_states = lax.all_gather(pieces, "mp", axis=0)

    parts = [project(d1, states, near[s], far[s]) for s in steps]
    parts = [trade(parts[s], "mp", s) if s else parts[0] for s in steps]
    packed = pack(c1, place, parts, ranks, capacity, per_shard)
    image = exchange(packed, "ctx")
    attn_out, own_grad, prior_grad = attention(
        c1, place, start, queries[0], d_out[0], text_kv[0], prior_text, image,
        images, per_shard, image_rows,
    )
    grad = (own_grad + shift(prior_grad, "ctx", -1)).astype(jnp.bfloat16)
    gathered = exchange(jnp.broadcast_to(grad, (ranks,) + grad.shape), "ctx")
    by_rank, mine = reorder(c1, place, gathered, per_shard, images)
    head_grad = [trade(mine, "mp", s) if s else mine for s in steps]
    term = weight_term(all_states, by_rank.reshape(ranks, image_rows, width), mixed)
    image_grad = image_term(d1, head_grad, near, far)
    weight_grad = term + swap(term, "dp")
    return (attn_out[None], image_grad[None], weight_grad[None])


def solution(mesh):
    in_specs = (
        P("dp", "ctx", "mp"),
        P("dp", None),
        P("dp", None),
        P("dp", "ctx", "mp"),
        P("dp", "ctx", "mp"),
        P("mp", None, None),
        P("dp", "ctx", "mp"),
    )
    out_specs = (P("dp", "ctx", "mp"), P("dp", "ctx", "mp"), P("mp", "ctx", None))
    return jax.shard_map(
        per_device, mesh=mesh, in_specs=in_specs, out_specs=out_specs, check_vma=False
    )
```

```python
import functools

import jax
import jax.numpy as jnp
from jax import lax
from jax.experimental import pallas as pl
from jax.experimental.pallas import tpu as pltpu
from jax.sharding import PartitionSpec as P

IMGTOK = 16
QTILE = 128
SPANS = (2, 3)
LOG2E = 1.4426950408889634
VMEM = 24 * 1024 * 1024

NN = (((1,), (0,)), ((), ()))
NT = (((1,), (1,)), ((), ()))
TN = (((0,), (0,)), ((), ()))


def dot(a, b, dims):
    return lax.dot_general(a, b, dims, preferred_element_type=jnp.float32)


def params():
    return pltpu.CompilerParams(vmem_limit_bytes=VMEM)


def cost(flops, moved):
    return pl.CostEstimate(flops=int(flops), bytes_accessed=int(moved), transcendentals=0)


def shift(block, axis, distance):
    devices = range(lax.axis_size(axis))
    route = [(i - distance, i) for i in devices if i - distance in devices]
    return lax.ppermute(block, axis, route)


def swap(block, axis):
    count = lax.axis_size(axis)
    return lax.ppermute(block, axis, [(i, count - 1 - i) for i in range(count)])


def exchange(blocks, axis):
    return lax.all_to_all(blocks, axis, split_axis=0, concat_axis=0, tiled=True)


def trade(block, axis, step):
    count = lax.axis_size(axis)
    return lax.ppermute(block, axis, [(i, i ^ step) for i in range(count)])


def rows16(start):
    return pl.ds(pl.multiple_of(start * IMGTOK, IMGTOK), IMGTOK)


def project_body(d_ref, m_ref, s_ref, own_near, near_ref, own_far, far_ref, out_ref):
    half = own_near.shape[0]
    d = d_ref[0]
    m = m_ref[0]
    near = s_ref[:, pl.ds(pl.multiple_of(d * half, half), half)]
    far = s_ref[:, pl.ds(pl.multiple_of((1 - d) * half, half), half)]
    for h in range(out_ref.shape[0]):
        near_w = near_ref[h - 1] if h else own_near[...]
        far_w = far_ref[h - 1] if h else own_far[...]
        out_ref[m ^ h] = dot(near, near_w, NN) + dot(far, far_w, NN)


def project(d, m, states, own_near, near, own_far, far):
    others, half, width = near.shape
    rows = states.shape[0]
    smem = pl.BlockSpec(memory_space=pltpu.SMEM)
    vmem = pl.BlockSpec(memory_space=pltpu.VMEM)
    return pl.pallas_call(
        project_body,
        in_specs=[smem, smem] + [vmem] * 5,
        out_specs=vmem,
        out_shape=jax.ShapeDtypeStruct((others + 1, rows, width), jnp.float32),
        cost_estimate=cost(4 * (others + 1) * rows * half * width, 8 * near.size),
        compiler_params=params(),
    )(d, m, states, own_near, near, own_far, far)


def pack_body(per_shard, c_ref, place_ref, part_ref, out_ref, rounded, count):
    shards = out_ref.shape[0]
    total = part_ref[0]
    for m in range(1, part_ref.shape[0]):
        total = total + part_ref[m]
    rounded[...] = total.astype(jnp.bfloat16)
    out_ref[...] = jnp.zeros_like(out_ref)
    for s in range(shards):
        count[s] = 0
    images = rounded.shape[0] // IMGTOK
    c = c_ref[0]

    def step(i, carry):
        dest = place_ref[c * images + i] // per_shard
        slot = count[dest]
        count[dest] = slot + 1
        block = rounded[rows16(i), :]
        out_ref[dest, 0, rows16(slot), :] = block

        @pl.when(dest + 1 < shards)
        def _():
            out_ref[dest + 1, 1, rows16(slot), :] = block

        return carry

    lax.fori_loop(0, images, step, 0)


def pack(c, place, parts, shards, capacity, per_shard):
    _, rows, width = parts.shape
    smem = pl.BlockSpec(memory_space=pltpu.SMEM)
    vmem = pl.BlockSpec(memory_space=pltpu.VMEM)
    return pl.pallas_call(
        functools.partial(pack_body, per_shard),
        in_specs=[smem, smem, vmem],
        out_specs=vmem,
        out_shape=jax.ShapeDtypeStruct((shards, 2, capacity, width), jnp.bfloat16),
        scratch_shapes=[
            pltpu.VMEM((rows, width), jnp.bfloat16),
            pltpu.SMEM((shards,), jnp.int32),
        ],
        cost_estimate=cost(0, parts.size * 6),
        compiler_params=params(),
    )(c, place, parts)


def attention_body(
    per_shard,
    images,
    c_ref,
    place_ref,
    first_ref,
    start_ref,
    q_ref,
    g_ref,
    own_ref,
    prior_ref,
    image_ref,
    out_ref,
    own_grad_ref,
    prior_grad_ref,
    window,
    probs,
    grads,
    total,
):
    t = pl.program_id(0)
    c = c_ref[0]
    rows = own_ref.shape[0]
    hd = own_ref.shape[1] // 2
    blocks = place_ref.shape[0]
    heads = q_ref.shape[1] // hd
    scale = hd ** (-0.5)

    @pl.when(t == 0)
    def _():
        window[:rows, :] = prior_ref[...]
        window[rows:, :] = own_ref[...]
        total[...] = jnp.zeros_like(total)

        def step(b, carry):
            n_own, n_prior = carry
            rank = b // images
            fresh = b % images == 0
            n_own = jnp.where(fresh, 0, n_own)
            n_prior = jnp.where(fresh, 0, n_prior)
            at = place_ref[b] - (c - 1) * per_shard
            is_prior = (at >= 0) & (at < per_shard)
            is_own = (at >= per_shard) & (at < 2 * per_shard)

            @pl.when(is_own)
            def _():
                window[rows16(at), :] = image_ref[rank, 0, rows16(n_own), :]

            @pl.when(is_prior)
            def _():
                window[rows16(at), :] = image_ref[rank, 1, rows16(n_prior), :]

            return n_own + is_own.astype(jnp.int32), n_prior + is_prior.astype(jnp.int32)

        lax.fori_loop(0, blocks, step, (jnp.int32(0), jnp.int32(0)))

    first = t * QTILE

    def stack(ref, a, b):
        return jnp.concatenate([ref[:, h * hd : (h + 1) * hd] for h in range(a, b)], axis=0)

    def tile(span):
        base = pl.multiple_of(first + (full - span), QTILE)
        keys = window[pl.ds(base, span), :hd]
        values = window[pl.ds(base, span), hd:]
        values_t = values.T
        key_pos = lax.broadcasted_iota(jnp.int32, (span, QTILE), 0) + base
        query_pos = lax.broadcasted_iota(jnp.int32, (span, QTILE), 1) + (first + rows)
        allowed = (key_pos <= query_pos) & (key_pos >= start_ref[...])
        bias = jnp.where(allowed, 0.0, -1e30)
        bias = jnp.concatenate([bias, bias], axis=1)

        def products(h):
            query = stack(q_ref, h, h + 2)
            grad = stack(g_ref, h, h + 2)
            return dot(keys, query, NT), dot(values, grad, NT)

        def softmax(h, scores):
            scores = scores * (scale * LOG2E) + bias
            top = jnp.max(scores, axis=0, keepdims=True)
            e = jnp.exp2(scores - top)
            p = e * (1.0 / jnp.sum(e, axis=0, keepdims=True))
            low = p.astype(jnp.bfloat16)
            probs[:span, h * QTILE : (h + 2) * QTILE] = low
            return p, dot(values_t, low, NN)

        def backward(h, p, grad_p, context_t):
            grad_t = stack(g_ref, h, h + 2).astype(jnp.float32).T
            delta = jnp.sum(grad_t * context_t, axis=0, keepdims=True)
            ds = (p * (grad_p - delta)).astype(jnp.bfloat16)
            context = context_t.T.astype(jnp.bfloat16)
            out_ref[:, h * hd : (h + 1) * hd] = context[:QTILE]
            out_ref[:, (h + 1) * hd : (h + 2) * hd] = context[QTILE:]
            grads[:span, h * QTILE : (h + 2) * QTILE] = ds

        pairs = heads // 2
        first_stage, second_stage = {}, {}
        for i in range(pairs + 2):
            if i < pairs:
                first_stage[i] = products(2 * i)
            if 1 <= i <= pairs:
                scores, grad_p = first_stage.pop(i - 1)
                second_stage[i - 1] = (grad_p, *softmax(2 * (i - 1), scores))
            if i >= 2:
                grad_p, p, context_t = second_stage.pop(i - 2)
                backward(2 * (i - 2), p, grad_p, context_t)
        total[pl.ds(base, span), :hd] += dot(grads[:span, :], stack(q_ref, 0, heads), NN)
        total[pl.ds(base, span), hd:] += dot(probs[:span, :], stack(g_ref, 0, heads), NN)

    full = rows + QTILE
    need = full - (first_ref[t] - first)
    below = 0
    for span in sorted({min(b * QTILE, full) for b in SPANS} | {full}):
        lower, below = below, span

        @pl.when((need > lower) & (need <= span))
        def _():
            tile(span)

    @pl.when(t == pl.num_programs(0) - 1)
    def _():
        total[:, :hd] = total[:, :hd] * scale
        prior_grad_ref[...] = jnp.zeros_like(prior_grad_ref)

        def step(b, carry):
            n_own, n_prior = carry
            at = place_ref[b] - (c - 1) * per_shard
            is_prior = (at >= 0) & (at < per_shard)
            is_own = (at >= per_shard) & (at < 2 * per_shard)

            @pl.when(is_own)
            def _():
                own_grad_ref[rows16(n_own), :] = total[rows16(at), :]

            @pl.when(is_prior)
            def _():
                prior_grad_ref[rows16(n_prior), :] = total[rows16(at), :]

            return n_own + is_own.astype(jnp.int32), n_prior + is_prior.astype(jnp.int32)

        lax.fori_loop(0, blocks, step, (jnp.int32(0), jnp.int32(0)))


def attention(c, place, start, queries, d_out, own, prior, image, images, per_shard, image_rows):
    rows, width = own.shape
    cols = queries.shape[1]
    tiles = rows // QTILE
    span = rows + QTILE
    head_rows = cols // (width // 2) * QTILE
    whole = lambda a: pl.BlockSpec(a.shape, lambda t, *_: (0,) * a.ndim)
    tile = pl.BlockSpec((QTILE, cols), lambda t, *_: (t, 0))
    grad = jax.ShapeDtypeStruct((image_rows, width), jnp.float32)
    return pl.pallas_call(
        functools.partial(attention_body, per_shard, images),
        grid_spec=pltpu.PrefetchScalarGridSpec(
            num_scalar_prefetch=3,
            grid=(tiles,),
            in_specs=[
                pl.BlockSpec((1, QTILE), lambda t, *_: (0, t)),
                tile,
                tile,
                whole(own),
                whole(prior),
                whole(image),
            ],
            out_specs=[tile, whole(grad), whole(grad)],
            scratch_shapes=[
                pltpu.VMEM((2 * rows, width), jnp.bfloat16),
                pltpu.VMEM((span, head_rows), jnp.bfloat16),
                pltpu.VMEM((span, head_rows), jnp.bfloat16),
                pltpu.VMEM((2 * rows, width), jnp.float32),
            ],
        ),
        out_shape=[jax.ShapeDtypeStruct((rows, cols), jnp.bfloat16), grad, grad],
        cost_estimate=cost(2 * 20 * cols * span * rows, 4 * queries.size * 2),
        compiler_params=params(),
    )(c, place, start[0, ::QTILE], start, queries, d_out, own, prior, image)


def reorder_body(per_shard, images, c_ref, place_ref, g_ref, out_ref, mine_ref, count):
    shards = g_ref.shape[0]
    for s in range(shards):
        count[s] = 0
    c = c_ref[0]

    def step(b, carry):
        dest = place_ref[b] // per_shard
        slot = count[dest]
        count[dest] = slot + 1
        out_ref[rows16(b), :] = g_ref[dest, rows16(slot), :]
        return carry

    lax.fori_loop(0, place_ref.shape[0], step, 0)
    rows = mine_ref.shape[0]
    mine_ref[...] = out_ref[pl.ds(pl.multiple_of(c * rows, IMGTOK), rows), :]


def reorder(c, place, gathered, per_shard, images):
    shards, rows, width = gathered.shape
    smem = pl.BlockSpec(memory_space=pltpu.SMEM)
    vmem = pl.BlockSpec(memory_space=pltpu.VMEM)
    return pl.pallas_call(
        functools.partial(reorder_body, per_shard, images),
        in_specs=[smem, smem, vmem],
        out_specs=[vmem, vmem],
        out_shape=[
            jax.ShapeDtypeStruct((shards * rows, width), gathered.dtype),
            jax.ShapeDtypeStruct((rows, width), gathered.dtype),
        ],
        scratch_shapes=[pltpu.SMEM((shards,), jnp.int32)],
        cost_estimate=cost(0, gathered.size * 2 * 4),
        compiler_params=params(),
    )(c, place, gathered)


def weight_body(mixed, c_ref, s_ref, g_ref, out_ref):
    ranks, rows, width = g_ref.shape
    c = c_ref[0]
    if mixed:
        grad = jnp.concatenate([g_ref[c ^ s] for s in range(ranks)], axis=0)
    else:
        grad = g_ref[...].reshape(ranks * rows, width)
    out_ref[...] = dot(s_ref[0], grad, TN)


def weight_term(c, states, grad, mixed):
    parts, rows, cols = states.shape
    width = grad.shape[2]
    return pl.pallas_call(
        functools.partial(weight_body, mixed),
        grid_spec=pltpu.PrefetchScalarGridSpec(
            num_scalar_prefetch=1,
            grid=(parts,),
            in_specs=[
                pl.BlockSpec((1, rows, cols), lambda k, c: (k, 0, 0)),
                pl.BlockSpec(grad.shape, lambda k, c: (0, 0, 0)),
            ],
            out_specs=pl.BlockSpec((cols, width), lambda k, c: (k, 0)),
        ),
        out_shape=jax.ShapeDtypeStruct((parts * cols, width), jnp.float32),
        cost_estimate=cost(2 * states.size * width, states.size * 4),
        compiler_params=params(),
    )(c, states, grad)


def image_body(d_ref, *refs):
    own_near, near_ref, own_far, far_ref, out_ref = refs[-5:]
    grads = refs[:-5]
    j = pl.program_id(0)
    cols = own_near.shape[0]
    half = out_ref.shape[1] // 2
    d = d_ref[0]
    for own, others, side in ((own_near, near_ref, d), (own_far, far_ref, 1 - d)):
        total = dot(grads[0][...], own[...], NT)
        for h in range(1, len(grads)):
            total = total + dot(grads[h][...], others[h - 1], NT)
        at = pl.multiple_of(side * half + j * cols, cols)
        out_ref[:, pl.ds(at, cols)] = total.astype(out_ref.dtype)


def image_term(d, grads, own_near, near, own_far, far):
    others, half, width = near.shape
    rows = grads[0].shape[0]
    tiles = 4
    own = pl.BlockSpec((half // tiles, width), lambda j, d: (j, 0))
    side = pl.BlockSpec((others, half // tiles, width), lambda j, d: (0, j, 0))
    grad = pl.BlockSpec((rows, width), lambda j, d: (0, 0))
    return pl.pallas_call(
        image_body,
        grid_spec=pltpu.PrefetchScalarGridSpec(
            num_scalar_prefetch=1,
            grid=(tiles,),
            in_specs=[grad] * len(grads) + [own, side] * 2,
            out_specs=pl.BlockSpec((rows, 2 * half), lambda j, d: (0, 0)),
        ),
        out_shape=jax.ShapeDtypeStruct((rows, 2 * half), jnp.bfloat16),
        cost_estimate=cost(4 * len(grads) * half * width * rows, 8 * near.size),
        compiler_params=params(),
    )(d, *grads, own_near, near, own_far, far)


def per_device(image_states, place_index, doc_ids, queries, text_kv, kv_weight, d_out):
    ranks = lax.axis_size("ctx")
    mps = lax.axis_size("mp")
    c = lax.axis_index("ctx")
    d = lax.axis_index("dp")
    rows = queries.shape[1]
    states = image_states[0]
    image_rows, feats = states.shape
    images = image_rows // IMGTOK
    per_shard = rows // IMGTOK
    capacity = IMGTOK * ((images + ranks - 1) // ranks)
    weights = kv_weight[0]
    width = weights.shape[1]
    c1 = jnp.reshape(c, (1,)).astype(jnp.int32)
    d1 = jnp.reshape(d, (1,)).astype(jnp.int32)
    place = place_index[0, ::IMGTOK] // IMGTOK

    m = lax.axis_index("mp")
    m1 = jnp.reshape(m, (1,)).astype(jnp.int32)
    steps = range(1, mps)

    half = feats // 2

    def slab(source, head, side):
        return lax.dynamic_slice_in_dim(source, head * feats + side * half, half)

    near = [trade(slab(weights, m ^ s, d), "mp", s) for s in steps]

    prior_text = shift(text_kv[0], "ctx", 1)
    docs = doc_ids[0]
    own_docs = lax.dynamic_slice_in_dim(docs, c * rows, rows)
    prior_docs = lax.dynamic_slice_in_dim(docs, jnp.maximum(c - 1, 0) * rows, rows)
    prior_docs = jnp.where(c > 0, prior_docs, -1)
    key_docs = jnp.concatenate([prior_docs, own_docs])
    start = jnp.sum((key_docs[:, None] < own_docs[None, :]).astype(jnp.int32), axis=0)[None]

    sub = feats // (ranks // mps) // mps
    mixed = ranks == mps
    pieces = states.reshape(image_rows, ranks // mps, mps, sub).transpose(2, 0, 1, 3)
    pieces = exchange(pieces, "mp")
    pieces = pieces.transpose(0, 2, 1, 3).reshape(ranks, image_rows, sub)
    *near, pieces, weights_late, prior_text, start, place = lax.optimization_barrier(
        (*near, pieces, weights, prior_text, start, place)
    )
    if mixed:
        moved = [lax.dynamic_index_in_dim(pieces, c ^ s, keepdims=False) for s in range(ranks)]
        moved = [trade(moved[s], "ctx", s) if s else moved[0] for s in range(ranks)]
    else:
        moved = [exchange(pieces, "ctx").reshape(ranks * image_rows, sub)]

    near = jnp.stack(near)
    far = swap(near, "dp")
    own_near = slab(weights_late, m, d)
    own_far = slab(weights_late, m, 1 - d)
    parts = exchange(project(d1, m1, states, own_near, near, own_far, far), "mp")
    packed = pack(c1, place, parts, ranks, capacity, per_shard)
    packed, *moved = lax.optimization_barrier((packed, *moved))
    all_states = lax.all_gather(jnp.concatenate(moved, axis=0), "mp", axis=0)
    image = exchange(packed, "ctx")
    attn_out, own_grad, prior_grad = attention(
        c1, place, start, queries[0], d_out[0], text_kv[0], prior_text, image,
        images, per_shard, image_rows,
    )
    grad = (own_grad + shift(prior_grad, "ctx", -1)).astype(jnp.bfloat16)
    gathered = exchange(jnp.broadcast_to(grad, (ranks,) + grad.shape), "ctx")
    by_rank, mine = reorder(c1, place, gathered, per_shard, images)
    head_grad = [mine] + [trade(mine, "mp", s) for s in steps]
    term = weight_term(c1, all_states, by_rank.reshape(ranks, image_rows, width), mixed)
    image_grad = image_term(d1, head_grad, own_near, near, own_far, far)
    weight_grad = term + swap(term, "dp")
    return (attn_out[None], image_grad[None], weight_grad[None])


def solution(mesh):
    in_specs = (
        P("dp", "ctx", "mp"),
        P("dp", None),
        P("dp", None),
        P("dp", "ctx", "mp"),
        P("dp", "ctx", "mp"),
        P("mp", None, None),
        P("dp", "ctx", "mp"),
    )
    out_specs = (P("dp", "ctx", "mp"), P("dp", "ctx", "mp"), P("mp", "ctx", None))
    return jax.shard_map(
        per_device, mesh=mesh, in_specs=in_specs, out_specs=out_specs, check_vma=False
    )
```

```python
import functools

import jax
import jax.numpy as jnp
from jax import lax
from jax.experimental import pallas as pl
from jax.experimental.pallas import tpu as pltpu
from jax.sharding import PartitionSpec as P

IMGTOK = 16
QTILE = 128
SPANS = (2, 3)
LOG2E = 1.4426950408889634
VMEM = 24 * 1024 * 1024

NN = (((1,), (0,)), ((), ()))
NT = (((1,), (1,)), ((), ()))
TN = (((0,), (0,)), ((), ()))


def dot(a, b, dims):
    return lax.dot_general(a, b, dims, preferred_element_type=jnp.float32)


def params():
    return pltpu.CompilerParams(vmem_limit_bytes=VMEM)


def cost(flops, moved):
    return pl.CostEstimate(flops=int(flops), bytes_accessed=int(moved), transcendentals=0)


def shift(block, axis, distance):
    devices = range(lax.axis_size(axis))
    route = [(i - distance, i) for i in devices if i - distance in devices]
    return lax.ppermute(block, axis, route)


def swap(block, axis):
    count = lax.axis_size(axis)
    return lax.ppermute(block, axis, [(i, count - 1 - i) for i in range(count)])


def exchange(blocks, axis):
    return lax.all_to_all(blocks, axis, split_axis=0, concat_axis=0, tiled=True)


def trade(block, axis, step):
    count = lax.axis_size(axis)
    return lax.ppermute(block, axis, [(i, i ^ step) for i in range(count)])


def rows16(start):
    return pl.ds(pl.multiple_of(start * IMGTOK, IMGTOK), IMGTOK)


def project_body(d_ref, s_ref, near_ref, far_ref, out_ref):
    half = near_ref.shape[0]
    d = d_ref[0]
    near = s_ref[:, pl.ds(pl.multiple_of(d * half, half), half)]
    far = s_ref[:, pl.ds(pl.multiple_of((1 - d) * half, half), half)]
    out_ref[...] = dot(near, near_ref[...], NN) + dot(far, far_ref[...], NN)


def project(d, states, near, far):
    half, width = near.shape
    rows = states.shape[0]
    vmem = pl.BlockSpec(memory_space=pltpu.VMEM)
    return pl.pallas_call(
        project_body,
        in_specs=[pl.BlockSpec(memory_space=pltpu.SMEM), vmem, vmem, vmem],
        out_specs=vmem,
        out_shape=jax.ShapeDtypeStruct((rows, width), jnp.float32),
        cost_estimate=cost(4 * rows * half * width, 4 * states.size),
        compiler_params=params(),
    )(d, states, near, far)


def pack_body(per_shard, terms, c_ref, place_ref, *refs):
    part_refs, out_refs = refs[:terms], refs[terms:-3]
    rounded, sorted_ref, count = refs[-3:]
    shards = sorted_ref.shape[0]
    total = part_refs[0][...]
    for ref in part_refs[1:]:
        total = total + ref[...]
    rounded[...] = total.astype(jnp.bfloat16)
    sorted_ref[...] = jnp.zeros_like(sorted_ref)
    for s in range(shards):
        count[s] = 0
    images = rounded.shape[0] // IMGTOK
    c = c_ref[0]

    def step(i, carry):
        dest = place_ref[c * images + i] // per_shard
        slot = count[dest]
        count[dest] = slot + 1
        block = rounded[rows16(i), :]
        sorted_ref[dest, 0, rows16(slot), :] = block

        @pl.when(dest + 1 < shards)
        def _():
            sorted_ref[dest + 1, 1, rows16(slot), :] = block

        return carry

    lax.fori_loop(0, images, step, 0)
    if len(out_refs) == 1:
        out_refs[0][...] = sorted_ref[...]
    else:
        for u, ref in enumerate(out_refs):
            ref[...] = sorted_ref[c ^ u]


def pack(c, place, parts, shards, capacity, per_shard, mixed):
    rows, width = parts[0].shape
    smem = pl.BlockSpec(memory_space=pltpu.SMEM)
    vmem = pl.BlockSpec(memory_space=pltpu.VMEM)
    shape = (2, capacity, width)
    if mixed:
        out = [jax.ShapeDtypeStruct(shape, jnp.bfloat16)] * shards
    else:
        out = [jax.ShapeDtypeStruct((shards,) + shape, jnp.bfloat16)]
    return pl.pallas_call(
        functools.partial(pack_body, per_shard, len(parts)),
        in_specs=[smem, smem] + [vmem] * len(parts),
        out_specs=[vmem] * len(out),
        out_shape=out,
        scratch_shapes=[
            pltpu.VMEM((rows, width), jnp.bfloat16),
            pltpu.VMEM((shards,) + shape, jnp.bfloat16),
            pltpu.SMEM((shards,), jnp.int32),
        ],
        cost_estimate=cost(0, parts[0].size * 4 * 6),
        compiler_params=params(),
    )(c, place, *parts)


def attention_body(
    per_shard,
    images,
    c_ref,
    place_ref,
    first_ref,
    start_ref,
    q_ref,
    g_ref,
    own_ref,
    prior_ref,
    *refs,
):
    image_refs = refs[:-8]
    out_ref, own_grad_ref, prior_grad_ref, window, probs, grads, total, image_ref = refs[-8:]
    t = pl.program_id(0)
    c = c_ref[0]
    rows = own_ref.shape[0]
    hd = own_ref.shape[1] // 2
    blocks = place_ref.shape[0]
    heads = q_ref.shape[1] // hd
    scale = hd ** (-0.5)

    @pl.when(t == 0)
    def _():
        window[:rows, :] = prior_ref[...]
        window[rows:, :] = own_ref[...]
        total[...] = jnp.zeros_like(total)
        if len(image_refs) == 1:
            image_ref[...] = image_refs[0][...]
        else:
            for u, ref in enumerate(image_refs):
                image_ref[c ^ u] = ref[...]

        def step(b, carry):
            n_own, n_prior = carry
            rank = b // images
            fresh = b % images == 0
            n_own = jnp.where(fresh, 0, n_own)
            n_prior = jnp.where(fresh, 0, n_prior)
            at = place_ref[b] - (c - 1) * per_shard
            is_prior = (at >= 0) & (at < per_shard)
            is_own = (at >= per_shard) & (at < 2 * per_shard)

            @pl.when(is_own)
            def _():
                window[rows16(at), :] = image_ref[rank, 0, rows16(n_own), :]

            @pl.when(is_prior)
            def _():
                window[rows16(at), :] = image_ref[rank, 1, rows16(n_prior), :]

            return n_own + is_own.astype(jnp.int32), n_prior + is_prior.astype(jnp.int32)

        lax.fori_loop(0, blocks, step, (jnp.int32(0), jnp.int32(0)))

    first = t * QTILE

    def stack(ref, a, b):
        return jnp.concatenate([ref[:, h * hd : (h + 1) * hd] for h in range(a, b)], axis=0)

    def tile(span):
        base = pl.multiple_of(first + (full - span), QTILE)
        keys = window[pl.ds(base, span), :hd]
        values = window[pl.ds(base, span), hd:]
        values_t = values.T
        key_pos = lax.broadcasted_iota(jnp.int32, (span, QTILE), 0) + base
        query_pos = lax.broadcasted_iota(jnp.int32, (span, QTILE), 1) + (first + rows)
        allowed = (key_pos <= query_pos) & (key_pos >= start_ref[...])
        bias = jnp.where(allowed, 0.0, -1e30)
        bias = jnp.concatenate([bias, bias], axis=1)

        def products(h):
            query = stack(q_ref, h, h + 2)
            grad = stack(g_ref, h, h + 2)
            return dot(keys, query, NT), dot(values, grad, NT)

        def softmax(h, scores):
            scores = scores * (scale * LOG2E) + bias
            top = jnp.max(scores, axis=0, keepdims=True)
            e = jnp.exp2(scores - top)
            p = e * (1.0 / jnp.sum(e, axis=0, keepdims=True))
            low = p.astype(jnp.bfloat16)
            probs[:span, h * QTILE : (h + 2) * QTILE] = low
            return p, dot(values_t, low, NN)

        def backward(h, p, grad_p, context_t):
            grad_t = stack(g_ref, h, h + 2).astype(jnp.float32).T
            delta = jnp.sum(grad_t * context_t, axis=0, keepdims=True)
            ds = (p * (grad_p - delta)).astype(jnp.bfloat16)
            context = context_t.T.astype(jnp.bfloat16)
            out_ref[:, h * hd : (h + 1) * hd] = context[:QTILE]
            out_ref[:, (h + 1) * hd : (h + 2) * hd] = context[QTILE:]
            grads[:span, h * QTILE : (h + 2) * QTILE] = ds

        pairs = heads // 2
        first_stage, second_stage = {}, {}
        for i in range(pairs + 2):
            if i < pairs:
                first_stage[i] = products(2 * i)
            if 1 <= i <= pairs:
                scores, grad_p = first_stage.pop(i - 1)
                second_stage[i - 1] = (grad_p, *softmax(2 * (i - 1), scores))
            if i >= 2:
                grad_p, p, context_t = second_stage.pop(i - 2)
                backward(2 * (i - 2), p, grad_p, context_t)
        total[pl.ds(base, span), :hd] += dot(grads[:span, :], stack(q_ref, 0, heads), NN)
        total[pl.ds(base, span), hd:] += dot(probs[:span, :], stack(g_ref, 0, heads), NN)

    full = rows + QTILE
    need = full - (first_ref[t] - first)
    below = 0
    for span in sorted({min(b * QTILE, full) for b in SPANS} | {full}):
        lower, below = below, span

        @pl.when((need > lower) & (need <= span))
        def _():
            tile(span)

    @pl.when(t == pl.num_programs(0) - 1)
    def _():
        total[:, :hd] = total[:, :hd] * scale
        prior_grad_ref[...] = jnp.zeros_like(prior_grad_ref)

        def step(b, carry):
            n_own, n_prior = carry
            at = place_ref[b] - (c - 1) * per_shard
            is_prior = (at >= 0) & (at < per_shard)
            is_own = (at >= per_shard) & (at < 2 * per_shard)

            @pl.when(is_own)
            def _():
                own_grad_ref[rows16(n_own), :] = total[rows16(at), :]

            @pl.when(is_prior)
            def _():
                prior_grad_ref[rows16(n_prior), :] = total[rows16(at), :].astype(jnp.bfloat16)

            return n_own + is_own.astype(jnp.int32), n_prior + is_prior.astype(jnp.int32)

        lax.fori_loop(0, blocks, step, (jnp.int32(0), jnp.int32(0)))


def attention(c, place, start, queries, d_out, own, prior, image, images, per_shard, image_rows):
    ranks = len(image) if len(image) > 1 else image[0].shape[0]
    rows, width = own.shape
    cols = queries.shape[1]
    tiles = rows // QTILE
    span = rows + QTILE
    head_rows = cols // (width // 2) * QTILE
    whole = lambda a: pl.BlockSpec(a.shape, lambda t, *_: (0,) * a.ndim)
    tile = pl.BlockSpec((QTILE, cols), lambda t, *_: (t, 0))
    grad = jax.ShapeDtypeStruct((image_rows, width), jnp.float32)
    prior_grad = jax.ShapeDtypeStruct((image_rows, width), jnp.bfloat16)
    return pl.pallas_call(
        functools.partial(attention_body, per_shard, images),
        grid_spec=pltpu.PrefetchScalarGridSpec(
            num_scalar_prefetch=3,
            grid=(tiles,),
            in_specs=[
                pl.BlockSpec((1, QTILE), lambda t, *_: (0, t)),
                tile,
                tile,
                whole(own),
                whole(prior),
                *map(whole, image),
            ],
            out_specs=[tile, whole(grad), whole(grad)],
            scratch_shapes=[
                pltpu.VMEM((2 * rows, width), jnp.bfloat16),
                pltpu.VMEM((span, head_rows), jnp.bfloat16),
                pltpu.VMEM((span, head_rows), jnp.bfloat16),
                pltpu.VMEM((2 * rows, width), jnp.float32),
                pltpu.VMEM((ranks,) + image[0].shape[-3:], jnp.bfloat16),
            ],
        ),
        out_shape=[jax.ShapeDtypeStruct((rows, cols), jnp.bfloat16), grad, prior_grad],
        cost_estimate=cost(2 * 20 * cols * span * rows, 4 * queries.size * 2),
        compiler_params=params(),
    )(c, place, start[0, ::QTILE], start, queries, d_out, own, prior, *image)


def reorder_body(per_shard, images, c_ref, place_ref, *refs):
    grad_refs = refs[:-4]
    out_ref, mine_ref, g_ref, count = refs[-4:]
    shards = g_ref.shape[0]
    if len(grad_refs) == 1:
        g_ref[...] = grad_refs[0][...]
    else:
        for u, ref in enumerate(grad_refs):
            g_ref[c_ref[0] ^ u] = ref[...]
    for s in range(shards):
        count[s] = 0
    c = c_ref[0]

    def step(b, carry):
        dest = place_ref[b] // per_shard
        slot = count[dest]
        count[dest] = slot + 1
        out_ref[rows16(b), :] = g_ref[dest, rows16(slot), :]
        return carry

    lax.fori_loop(0, place_ref.shape[0], step, 0)
    rows = mine_ref.shape[0]
    mine_ref[...] = out_ref[pl.ds(pl.multiple_of(c * rows, IMGTOK), rows), :]


def reorder(c, place, gathered, per_shard, images, shards):
    rows, width = gathered[0].shape[-2:]
    dtype = gathered[0].dtype
    smem = pl.BlockSpec(memory_space=pltpu.SMEM)
    vmem = pl.BlockSpec(memory_space=pltpu.VMEM)
    return pl.pallas_call(
        functools.partial(reorder_body, per_shard, images),
        in_specs=[smem, smem] + [vmem] * len(gathered),
        out_specs=[vmem, vmem],
        out_shape=[
            jax.ShapeDtypeStruct((shards * rows, width), dtype),
            jax.ShapeDtypeStruct((rows, width), dtype),
        ],
        scratch_shapes=[
            pltpu.VMEM((shards, rows, width), dtype),
            pltpu.SMEM((shards,), jnp.int32),
        ],
        cost_estimate=cost(0, shards * rows * width * 8),
        compiler_params=params(),
    )(c, place, *gathered)


def weight_body(mixed, c_ref, *refs):
    *state_refs, g_ref, out_ref = refs
    ranks, rows, width = g_ref.shape
    c = c_ref[0]
    total = None
    done = 0
    for ref in state_refs:
        count = ref.shape[1] // rows
        if mixed:
            grad = [g_ref[c ^ s] for s in range(done, done + count)]
            grad = jnp.concatenate(grad, axis=0)
        else:
            grad = g_ref[...].reshape(ranks * rows, width)
        done += count
        term = dot(ref[0], grad, TN)
        total = term if total is None else total + term
    out_ref[...] = total


def weight_term(c, states, grad, mixed):
    parts, _, cols = states[0].shape
    width = grad.shape[2]
    size = sum(a.size for a in states)
    return pl.pallas_call(
        functools.partial(weight_body, mixed),
        grid_spec=pltpu.PrefetchScalarGridSpec(
            num_scalar_prefetch=1,
            grid=(parts,),
            in_specs=[
                *[pl.BlockSpec((1,) + a.shape[1:], lambda k, c: (k, 0, 0)) for a in states],
                pl.BlockSpec(grad.shape, lambda k, c: (0, 0, 0)),
            ],
            out_specs=pl.BlockSpec((cols, width), lambda k, c: (k, 0)),
        ),
        out_shape=jax.ShapeDtypeStruct((parts * cols, width), jnp.float32),
        cost_estimate=cost(2 * size * width, size * 4),
        compiler_params=params(),
    )(c, *states, grad)


def image_body(d_ref, *refs):
    out_ref = refs[-1]
    heads = (len(refs) - 1) // 3
    grads, near, far = refs[:heads], refs[heads : 2 * heads], refs[2 * heads : -1]
    j = pl.program_id(0)
    cols = near[0].shape[0]
    half = out_ref.shape[1] // 2
    d = d_ref[0]
    for weights, side in ((near, d), (far, 1 - d)):
        total = dot(grads[0][...], weights[0][...], NT)
        for h in range(1, heads):
            total = total + dot(grads[h][...], weights[h][...], NT)
        at = pl.multiple_of(side * half + j * cols, cols)
        out_ref[:, pl.ds(at, cols)] = total.astype(out_ref.dtype)


def image_term(d, grads, near, far):
    heads = len(near)
    half, width = near[0].shape
    rows = grads[0].shape[0]
    tiles = 4
    side = pl.BlockSpec((half // tiles, width), lambda j, d: (j, 0))
    grad = pl.BlockSpec((rows, width), lambda j, d: (0, 0))
    return pl.pallas_call(
        image_body,
        grid_spec=pltpu.PrefetchScalarGridSpec(
            num_scalar_prefetch=1,
            grid=(tiles,),
            in_specs=[grad] * heads + [side] * (2 * heads),
            out_specs=pl.BlockSpec((rows, 2 * half), lambda j, d: (0, 0)),
        ),
        out_shape=jax.ShapeDtypeStruct((rows, 2 * half), jnp.bfloat16),
        cost_estimate=cost(4 * heads * half * width * rows, 4 * heads * half * width * 2),
        compiler_params=params(),
    )(d, *grads, *near, *far)


def per_device(image_states, place_index, doc_ids, queries, text_kv, kv_weight, d_out):
    ranks = lax.axis_size("ctx")
    mps = lax.axis_size("mp")
    c = lax.axis_index("ctx")
    d = lax.axis_index("dp")
    rows = queries.shape[1]
    states = image_states[0]
    image_rows, feats = states.shape
    images = image_rows // IMGTOK
    per_shard = rows // IMGTOK
    capacity = IMGTOK * ((images + ranks - 1) // ranks)
    weights = kv_weight[0]
    width = weights.shape[1]
    c1 = jnp.reshape(c, (1,)).astype(jnp.int32)
    d1 = jnp.reshape(d, (1,)).astype(jnp.int32)
    place = place_index[0, ::IMGTOK] // IMGTOK

    m = lax.axis_index("mp")
    steps = range(1, mps)
    mixed = ranks == mps

    half = feats // 2

    def slab(source, head, side):
        return lax.dynamic_slice_in_dim(source, head * feats + side * half, half)

    slabs = [slab(weights, m ^ s, d) for s in steps]
    *slabs, states_late = lax.optimization_barrier((*slabs, states))
    near = [trade(w, "mp", s) for w, s in zip(slabs, steps)]
    far = [swap(w, "dp") for w in near]

    prior_text = shift(text_kv[0], "ctx", 1)
    docs = doc_ids[0]
    own_docs = lax.dynamic_slice_in_dim(docs, c * rows, rows)
    prior_docs = lax.dynamic_slice_in_dim(docs, jnp.maximum(c - 1, 0) * rows, rows)
    prior_docs = jnp.where(c > 0, prior_docs, -1)
    key_docs = jnp.concatenate([prior_docs, own_docs])
    start = jnp.sum((key_docs[:, None] < own_docs[None, :]).astype(jnp.int32), axis=0)[None]

    sub = feats // (ranks // mps) // mps
    if mixed:
        source = states_late
        pieces = [lax.dynamic_slice_in_dim(source, m * sub, sub, axis=1)]
        for s in steps:
            piece = lax.dynamic_slice_in_dim(source, (m ^ s) * sub, sub, axis=1)
            pieces.append(trade(piece, "mp", s))
        *near, pieces = lax.optimization_barrier((*near, jnp.stack(pieces)))
        moved = [
            lax.dynamic_index_in_dim(pieces, m ^ c ^ s, keepdims=False) for s in range(ranks)
        ]
    else:
        pieces = states.reshape(image_rows, ranks // mps, mps, sub).transpose(2, 0, 1, 3)
        pieces = exchange(pieces, "mp")
        pieces = pieces.transpose(0, 2, 1, 3).reshape(ranks, image_rows, sub)
        moved = [exchange(pieces, "ctx").reshape(ranks * image_rows, sub)]

    weights_late, _ = lax.optimization_barrier((weights, near[-1]))
    near = [slab(weights_late, m, d)] + near
    far = [slab(weights_late, m, 1 - d)] + far
    parts = [project(d1, states, near[s], far[s]) for s in range(mps)]
    parts = [trade(parts[s], "mp", s) if s else parts[0] for s in range(mps)]
    packed = pack(c1, place, parts, ranks, capacity, per_shard, mixed)
    cut = ranks // 2
    if mixed:
        for s in range(1, cut):
            moved[s] = trade(moved[s], "ctx", s)
        moved[cut], _ = lax.optimization_barrier((moved[cut], packed[0]))
        moved[cut] = trade(moved[cut], "ctx", cut)
        image = [trade(packed[s], "ctx", s) if s else packed[0] for s in range(ranks)]
        for s in range(cut + 1, ranks):
            moved[s], *image = lax.optimization_barrier((moved[s], *image))
            moved[s] = trade(moved[s], "ctx", s)
        moved = [jnp.concatenate(moved[:cut], axis=0), jnp.concatenate(moved[cut:], axis=0)]
    else:
        image = [exchange(packed[0], "ctx")]
    moved[0], _ = lax.optimization_barrier((moved[0], packed[0]))
    all_states = [lax.all_gather(moved[0], "mp", axis=0)]
    attn_out, own_grad, prior_grad = attention(
        c1, place, start, queries[0], d_out[0], text_kv[0], prior_text, image,
        images, per_shard, image_rows,
    )
    if mixed:
        moved[1], prior_grad = lax.optimization_barrier((moved[1], prior_grad))
        all_states.append(lax.all_gather(moved[1], "mp", axis=0))
    grad = own_grad + shift(prior_grad, "ctx", -1).astype(jnp.float32)
    grad = grad.astype(jnp.bfloat16)
    if mixed:
        gathered = [trade(grad, "ctx", s) if s else grad for s in range(ranks)]
    else:
        gathered = [exchange(jnp.broadcast_to(grad, (ranks,) + grad.shape), "ctx")]
    by_rank, mine = reorder(c1, place, gathered, per_shard, images, ranks)
    head_grad = [mine] + [trade(mine, "mp", s) for s in steps]
    by_rank, *head_grad = lax.optimization_barrier((by_rank, *head_grad))
    image_grad = image_term(d1, head_grad, near, far)
    term = weight_term(c1, all_states, by_rank.reshape(ranks, image_rows, width), mixed)
    weight_grad = term + swap(term, "dp")
    return (attn_out[None], image_grad[None], weight_grad[None])


def solution(mesh):
    in_specs = (
        P("dp", "ctx", "mp"),
        P("dp", None),
        P("dp", None),
        P("dp", "ctx", "mp"),
        P("dp", "ctx", "mp"),
        P("mp", None, None),
        P("dp", "ctx", "mp"),
    )
    out_specs = (P("dp", "ctx", "mp"), P("dp", "ctx", "mp"), P("mp", "ctx", None))
    return jax.shard_map(
        per_device, mesh=mesh, in_specs=in_specs, out_specs=out_specs, check_vma=False
    )
```

```python
import functools

import jax
import jax.numpy as jnp
from jax import lax
from jax.experimental import pallas as pl
from jax.experimental.pallas import tpu as pltpu
from jax.sharding import PartitionSpec as P

IMGTOK = 16
QTILE = 128
SPANS = (2, 3)
LOG2E = 1.4426950408889634
VMEM = 24 * 1024 * 1024

NN = (((1,), (0,)), ((), ()))
NT = (((1,), (1,)), ((), ()))
TN = (((0,), (0,)), ((), ()))


def dot(a, b, dims):
    return lax.dot_general(a, b, dims, preferred_element_type=jnp.float32)


def params():
    return pltpu.CompilerParams(vmem_limit_bytes=VMEM)


def cost(flops, moved):
    return pl.CostEstimate(flops=int(flops), bytes_accessed=int(moved), transcendentals=0)


def shift(block, axis, distance):
    devices = range(lax.axis_size(axis))
    route = [(i - distance, i) for i in devices if i - distance in devices]
    return lax.ppermute(block, axis, route)


def swap(block, axis):
    count = lax.axis_size(axis)
    return lax.ppermute(block, axis, [(i, count - 1 - i) for i in range(count)])


def exchange(blocks, axis):
    return lax.all_to_all(blocks, axis, split_axis=0, concat_axis=0, tiled=True)


def trade(block, axis, step):
    count = lax.axis_size(axis)
    return lax.ppermute(block, axis, [(i, i ^ step) for i in range(count)])


def rows16(start):
    return pl.ds(pl.multiple_of(start * IMGTOK, IMGTOK), IMGTOK)


def project_body(m_ref, *refs):
    *pairs, out_ref = refs
    count = len(pairs) // 2
    total = dot(pairs[0][...], pairs[count][...], NN)
    for k in range(1, count):
        total = total + dot(pairs[k][...], pairs[count + k][...], NN)
    out_ref[...] = total


def project(m, blocks, weights):
    rows, feats = blocks[0].shape
    width = weights.shape[1]
    block = pl.BlockSpec((rows, feats), lambda i, m: (0, 0))
    chunk = lambda k: pl.BlockSpec((feats, width), lambda i, m: (m[0] ^ k, 0))
    return pl.pallas_call(
        project_body,
        grid_spec=pltpu.PrefetchScalarGridSpec(
            num_scalar_prefetch=1,
            grid=(1,),
            in_specs=[block] * len(blocks) + [chunk(k) for k in range(len(blocks))],
            out_specs=pl.BlockSpec((rows, width), lambda i, m: (0, 0)),
        ),
        out_shape=jax.ShapeDtypeStruct((rows, width), jnp.float32),
        cost_estimate=cost(2 * len(blocks) * rows * feats * width, 4 * len(blocks) * feats * width),
        compiler_params=params(),
    )(m, *blocks, *[weights] * len(blocks))


def pack_body(per_shard, m_ref, c_ref, place_ref, low_ref, high_ref, weight_ref, part_ref, *refs):
    out_refs = refs[:-3]
    rounded, sorted_ref, count = refs[-3:]
    shards = sorted_ref.shape[0]
    half = low_ref.shape[0]
    for at, ref in ((0, low_ref), (half, high_ref)):
        term = dot(ref[...], weight_ref[...], NN)
        rounded[at : at + half, :] = (part_ref[at : at + half, :] + term).astype(jnp.bfloat16)
    sorted_ref[...] = jnp.zeros_like(sorted_ref)
    for s in range(shards):
        count[s] = 0
    images = rounded.shape[0] // IMGTOK
    c = c_ref[0]

    def step(i, carry):
        dest = place_ref[c * images + i] // per_shard
        slot = count[dest]
        count[dest] = slot + 1
        block = rounded[rows16(i), :]
        sorted_ref[dest, 0, rows16(slot), :] = block

        @pl.when(dest + 1 < shards)
        def _():
            sorted_ref[dest + 1, 1, rows16(slot), :] = block

        return carry

    lax.fori_loop(0, images, step, 0)
    if len(out_refs) == 1:
        out_refs[0][...] = sorted_ref[...]
    else:
        for u, ref in enumerate(out_refs):
            ref[...] = sorted_ref[c ^ u]


def pack(m, c, place, low, high, weights, part, shards, capacity, per_shard, mixed):
    rows, width = part.shape
    feats = low.shape[1]
    whole = lambda a: pl.BlockSpec(a.shape, lambda i, *_: (0,) * len(a.shape))
    shape = (2, capacity, width)
    if mixed:
        out = [jax.ShapeDtypeStruct(shape, jnp.bfloat16)] * shards
    else:
        out = [jax.ShapeDtypeStruct((shards,) + shape, jnp.bfloat16)]
    return pl.pallas_call(
        functools.partial(pack_body, per_shard),
        grid_spec=pltpu.PrefetchScalarGridSpec(
            num_scalar_prefetch=3,
            grid=(1,),
            in_specs=[
                whole(low),
                whole(high),
                pl.BlockSpec((feats, width), lambda i, m, *_: (m[0] ^ 3, 0)),
                whole(part),
            ],
            out_specs=[whole(a) for a in out],
            scratch_shapes=[
                pltpu.VMEM((rows, width), jnp.bfloat16),
                pltpu.VMEM((shards,) + shape, jnp.bfloat16),
                pltpu.SMEM((shards,), jnp.int32),
            ],
        ),
        out_shape=out,
        cost_estimate=cost(2 * rows * feats * width, part.size * 16),
        compiler_params=params(),
    )(m, c, place, low, high, weights, part)


def slices_body(m_ref, c_ref, own_ref, x_ref, y_ref, low_ref, high_ref, kept_ref, *out_refs):
    m = m_ref[0]
    c = c_ref[0]
    sub = out_refs[0].shape[1]
    half = low_ref.shape[0]
    for u, ref in enumerate((kept_ref,) + out_refs):
        at = pl.ds(0, ref.shape[1]) if u == 0 else pl.ds(pl.multiple_of(m * sub, sub), sub)
        which = m ^ c ^ u
        for k, source in enumerate((own_ref, x_ref, y_ref)):

            @pl.when(which == k)
            def _():
                ref[...] = source[:, at]

        @pl.when(which == 3)
        def _():
            ref[:half, :] = low_ref[:, at]
            ref[half:, :] = high_ref[:, at]


def slices(m, c, blocks, sub):
    rows, feats = blocks[0].shape
    smem = pl.BlockSpec(memory_space=pltpu.SMEM)
    vmem = pl.BlockSpec(memory_space=pltpu.VMEM)
    dtype = blocks[0].dtype
    out = [jax.ShapeDtypeStruct((rows, feats), dtype)]
    out += [jax.ShapeDtypeStruct((rows, sub), dtype)] * 3
    return pl.pallas_call(
        slices_body,
        in_specs=[smem, smem] + [vmem] * len(blocks),
        out_specs=[vmem] * len(out),
        out_shape=out,
        cost_estimate=cost(0, rows * feats * 16),
        compiler_params=params(),
    )(m, c, *blocks)


def attention_body(
    per_shard,
    images,
    c_ref,
    place_ref,
    first_ref,
    start_ref,
    q_ref,
    g_ref,
    own_ref,
    prior_ref,
    *refs,
):
    image_refs = refs[:-8]
    out_ref, own_grad_ref, prior_grad_ref, window, probs, grads, total, image_ref = refs[-8:]
    t = pl.program_id(0)
    c = c_ref[0]
    rows = own_ref.shape[0]
    hd = own_ref.shape[1] // 2
    blocks = place_ref.shape[0]
    heads = q_ref.shape[1] // hd
    scale = hd ** (-0.5)

    @pl.when(t == 0)
    def _():
        window[:rows, :] = prior_ref[...]
        window[rows:, :] = own_ref[...]
        total[...] = jnp.zeros_like(total)
        if len(image_refs) == 1:
            image_ref[...] = image_refs[0][...]
        else:
            for u, ref in enumerate(image_refs):
                image_ref[c ^ u] = ref[...]

        def step(b, carry):
            n_own, n_prior = carry
            rank = b // images
            fresh = b % images == 0
            n_own = jnp.where(fresh, 0, n_own)
            n_prior = jnp.where(fresh, 0, n_prior)
            at = place_ref[b] - (c - 1) * per_shard
            is_prior = (at >= 0) & (at < per_shard)
            is_own = (at >= per_shard) & (at < 2 * per_shard)

            @pl.when(is_own)
            def _():
                window[rows16(at), :] = image_ref[rank, 0, rows16(n_own), :]

            @pl.when(is_prior)
            def _():
                window[rows16(at), :] = image_ref[rank, 1, rows16(n_prior), :]

            return n_own + is_own.astype(jnp.int32), n_prior + is_prior.astype(jnp.int32)

        lax.fori_loop(0, blocks, step, (jnp.int32(0), jnp.int32(0)))

    first = t * QTILE

    def stack(ref, a, b):
        return jnp.concatenate([ref[:, h * hd : (h + 1) * hd] for h in range(a, b)], axis=0)

    def tile(span):
        base = pl.multiple_of(first + (full - span), QTILE)
        keys = window[pl.ds(base, span), :hd]
        values = window[pl.ds(base, span), hd:]
        values_t = values.T
        key_pos = lax.broadcasted_iota(jnp.int32, (span, QTILE), 0) + base
        query_pos = lax.broadcasted_iota(jnp.int32, (span, QTILE), 1) + (first + rows)
        allowed = (key_pos <= query_pos) & (key_pos >= start_ref[...])
        bias = jnp.where(allowed, 0.0, -1e30)
        bias = jnp.concatenate([bias, bias], axis=1)

        def products(h):
            query = stack(q_ref, h, h + 2)
            grad = stack(g_ref, h, h + 2)
            return dot(keys, query, NT), dot(values, grad, NT)

        def softmax(h, scores):
            scores = scores * (scale * LOG2E) + bias
            top = jnp.max(scores, axis=0, keepdims=True)
            e = jnp.exp2(scores - top)
            p = e * (1.0 / jnp.sum(e, axis=0, keepdims=True))
            low = p.astype(jnp.bfloat16)
            probs[:span, h * QTILE : (h + 2) * QTILE] = low
            return p, dot(values_t, low, NN)

        def backward(h, p, grad_p, context_t):
            grad_t = stack(g_ref, h, h + 2).astype(jnp.float32).T
            delta = jnp.sum(grad_t * context_t, axis=0, keepdims=True)
            ds = (p * (grad_p - delta)).astype(jnp.bfloat16)
            context = context_t.T.astype(jnp.bfloat16)
            out_ref[:, h * hd : (h + 1) * hd] = context[:QTILE]
            out_ref[:, (h + 1) * hd : (h + 2) * hd] = context[QTILE:]
            grads[:span, h * QTILE : (h + 2) * QTILE] = ds

        pairs = heads // 2
        first_stage, second_stage = {}, {}
        for i in range(pairs + 2):
            if i < pairs:
                first_stage[i] = products(2 * i)
            if 1 <= i <= pairs:
                scores, grad_p = first_stage.pop(i - 1)
                second_stage[i - 1] = (grad_p, *softmax(2 * (i - 1), scores))
            if i >= 2:
                grad_p, p, context_t = second_stage.pop(i - 2)
                backward(2 * (i - 2), p, grad_p, context_t)
        total[pl.ds(base, span), :hd] += dot(grads[:span, :], stack(q_ref, 0, heads), NN)
        total[pl.ds(base, span), hd:] += dot(probs[:span, :], stack(g_ref, 0, heads), NN)

    full = rows + QTILE
    need = full - (first_ref[t] - first)
    below = 0
    for span in sorted({min(b * QTILE, full) for b in SPANS} | {full}):
        lower, below = below, span

        @pl.when((need > lower) & (need <= span))
        def _():
            tile(span)

    @pl.when(t == pl.num_programs(0) - 1)
    def _():
        total[:, :hd] = total[:, :hd] * scale
        prior_grad_ref[...] = jnp.zeros_like(prior_grad_ref)

        def step(b, carry):
            n_own, n_prior = carry
            at = place_ref[b] - (c - 1) * per_shard
            is_prior = (at >= 0) & (at < per_shard)
            is_own = (at >= per_shard) & (at < 2 * per_shard)

            @pl.when(is_own)
            def _():
                own_grad_ref[rows16(n_own), :] = total[rows16(at), :]

            @pl.when(is_prior)
            def _():
                prior_grad_ref[rows16(n_prior), :] = total[rows16(at), :].astype(jnp.bfloat16)

            return n_own + is_own.astype(jnp.int32), n_prior + is_prior.astype(jnp.int32)

        lax.fori_loop(0, blocks, step, (jnp.int32(0), jnp.int32(0)))


def attention(c, place, start, queries, d_out, own, prior, image, images, per_shard, image_rows):
    ranks = len(image) if len(image) > 1 else image[0].shape[0]
    rows, width = own.shape
    cols = queries.shape[1]
    tiles = rows // QTILE
    span = rows + QTILE
    head_rows = cols // (width // 2) * QTILE
    whole = lambda a: pl.BlockSpec(a.shape, lambda t, *_: (0,) * a.ndim)
    tile = pl.BlockSpec((QTILE, cols), lambda t, *_: (t, 0))
    grad = jax.ShapeDtypeStruct((image_rows, width), jnp.float32)
    prior_grad = jax.ShapeDtypeStruct((image_rows, width), jnp.bfloat16)
    return pl.pallas_call(
        functools.partial(attention_body, per_shard, images),
        grid_spec=pltpu.PrefetchScalarGridSpec(
            num_scalar_prefetch=3,
            grid=(tiles,),
            in_specs=[
                pl.BlockSpec((1, QTILE), lambda t, *_: (0, t)),
                tile,
                tile,
                whole(own),
                whole(prior),
                *map(whole, image),
            ],
            out_specs=[tile, whole(grad), whole(grad)],
            scratch_shapes=[
                pltpu.VMEM((2 * rows, width), jnp.bfloat16),
                pltpu.VMEM((span, head_rows), jnp.bfloat16),
                pltpu.VMEM((span, head_rows), jnp.bfloat16),
                pltpu.VMEM((2 * rows, width), jnp.float32),
                pltpu.VMEM((ranks,) + image[0].shape[-3:], jnp.bfloat16),
            ],
        ),
        out_shape=[jax.ShapeDtypeStruct((rows, cols), jnp.bfloat16), grad, prior_grad],
        cost_estimate=cost(2 * 20 * cols * span * rows, 4 * queries.size * 2),
        compiler_params=params(),
    )(c, place, start[0, ::QTILE], start, queries, d_out, own, prior, *image)


def reorder_body(per_shard, images, c_ref, place_ref, *refs):
    grad_refs = refs[:-4]
    out_ref, mine_ref, g_ref, count = refs[-4:]
    shards = g_ref.shape[0]
    if len(grad_refs) == 1:
        g_ref[...] = grad_refs[0][...]
    else:
        for u, ref in enumerate(grad_refs):
            g_ref[c_ref[0] ^ u] = ref[...]
    for s in range(shards):
        count[s] = 0
    c = c_ref[0]

    def step(b, carry):
        dest = place_ref[b] // per_shard
        slot = count[dest]
        count[dest] = slot + 1
        out_ref[rows16(b), :] = g_ref[dest, rows16(slot), :]
        return carry

    lax.fori_loop(0, place_ref.shape[0], step, 0)
    rows = mine_ref.shape[0]
    mine_ref[...] = out_ref[pl.ds(pl.multiple_of(c * rows, IMGTOK), rows), :]


def reorder(c, place, gathered, per_shard, images, shards):
    rows, width = gathered[0].shape[-2:]
    dtype = gathered[0].dtype
    smem = pl.BlockSpec(memory_space=pltpu.SMEM)
    vmem = pl.BlockSpec(memory_space=pltpu.VMEM)
    return pl.pallas_call(
        functools.partial(reorder_body, per_shard, images),
        in_specs=[smem, smem] + [vmem] * len(gathered),
        out_specs=[vmem, vmem],
        out_shape=[
            jax.ShapeDtypeStruct((shards * rows, width), dtype),
            jax.ShapeDtypeStruct((rows, width), dtype),
        ],
        scratch_shapes=[
            pltpu.VMEM((shards, rows, width), dtype),
            pltpu.SMEM((shards,), jnp.int32),
        ],
        cost_estimate=cost(0, shards * rows * width * 8),
        compiler_params=params(),
    )(c, place, *gathered)


def weight_body(mixed, c_ref, *refs):
    *state_refs, g_ref, out_ref = refs
    ranks, rows, width = g_ref.shape
    c = c_ref[0]
    if mixed:
        total = dot(state_refs[0][...], g_ref[c], TN)
        grad = jnp.concatenate([g_ref[c ^ s] for s in range(1, ranks)], axis=0)
        out_ref[...] = total + dot(state_refs[1][0], grad, TN)
    else:
        grad = g_ref[...].reshape(ranks * rows, width)
        out_ref[...] = dot(state_refs[0][0], grad, TN)


def weight_term(c, kept, states, grad):
    parts, count, cols = states.shape
    _, rows, width = grad.shape
    specs = [pl.BlockSpec((1, count, cols), lambda k, c: (k, 0, 0))]
    arrays = [states]
    if kept is not None:
        specs.insert(0, pl.BlockSpec((rows, cols), lambda k, c: (0, k)))
        arrays.insert(0, kept)
    return pl.pallas_call(
        functools.partial(weight_body, kept is not None),
        grid_spec=pltpu.PrefetchScalarGridSpec(
            num_scalar_prefetch=1,
            grid=(parts,),
            in_specs=specs + [pl.BlockSpec(grad.shape, lambda k, c: (0, 0, 0))],
            out_specs=pl.BlockSpec((cols, width), lambda k, c: (k, 0)),
        ),
        out_shape=jax.ShapeDtypeStruct((parts * cols, width), jnp.float32),
        cost_estimate=cost(2 * states.size * width, states.size * 4),
        compiler_params=params(),
    )(c, *arrays, grad)


def image_body(d_ref, *refs):
    out_ref = refs[-1]
    heads = (len(refs) - 1) // 3
    grads, near, far = refs[:heads], refs[heads : 2 * heads], refs[2 * heads : -1]
    j = pl.program_id(0)
    cols = near[0].shape[0]
    half = out_ref.shape[1] // 2
    d = d_ref[0]
    for weights, side in ((near, d), (far, 1 - d)):
        total = dot(grads[0][...], weights[0][...], NT)
        for h in range(1, heads):
            total = total + dot(grads[h][...], weights[h][...], NT)
        at = pl.multiple_of(side * half + j * cols, cols)
        out_ref[:, pl.ds(at, cols)] = total.astype(out_ref.dtype)


def image_term(d, grads, near, far):
    heads = len(near)
    half, width = near[0].shape
    rows = grads[0].shape[0]
    tiles = 4
    side = pl.BlockSpec((half // tiles, width), lambda j, d: (j, 0))
    grad = pl.BlockSpec((rows, width), lambda j, d: (0, 0))
    return pl.pallas_call(
        image_body,
        grid_spec=pltpu.PrefetchScalarGridSpec(
            num_scalar_prefetch=1,
            grid=(tiles,),
            in_specs=[grad] * heads + [side] * (2 * heads),
            out_specs=pl.BlockSpec((rows, 2 * half), lambda j, d: (0, 0)),
        ),
        out_shape=jax.ShapeDtypeStruct((rows, 2 * half), jnp.bfloat16),
        cost_estimate=cost(4 * heads * half * width * rows, 4 * heads * half * width * 2),
        compiler_params=params(),
    )(d, *grads, *near, *far)


def per_device(image_states, place_index, doc_ids, queries, text_kv, kv_weight, d_out):
    ranks = lax.axis_size("ctx")
    mps = lax.axis_size("mp")
    c = lax.axis_index("ctx")
    d = lax.axis_index("dp")
    rows = queries.shape[1]
    states = image_states[0]
    image_rows, feats = states.shape
    images = image_rows // IMGTOK
    per_shard = rows // IMGTOK
    capacity = IMGTOK * ((images + ranks - 1) // ranks)
    weights = kv_weight[0]
    width = weights.shape[1]
    c1 = jnp.reshape(c, (1,)).astype(jnp.int32)
    d1 = jnp.reshape(d, (1,)).astype(jnp.int32)
    place = place_index[0, ::IMGTOK] // IMGTOK

    m = lax.axis_index("mp")
    m1 = jnp.reshape(m, (1,)).astype(jnp.int32)
    steps = range(1, mps)
    mixed = ranks == mps

    x = trade(states, "mp", 1)
    y = trade(states, "mp", 2)
    low = trade(x[: image_rows // 2], "mp", 2)
    high = trade(y[image_rows // 2 :], "mp", 1)
    part = project(m1, [states, x, y], weights)

    prior_text = shift(text_kv[0], "ctx", 1)
    docs = doc_ids[0]
    own_docs = lax.dynamic_slice_in_dim(docs, c * rows, rows)
    prior_docs = lax.dynamic_slice_in_dim(docs, jnp.maximum(c - 1, 0) * rows, rows)
    prior_docs = jnp.where(c > 0, prior_docs, -1)
    key_docs = jnp.concatenate([prior_docs, own_docs])
    start = jnp.sum((key_docs[:, None] < own_docs[None, :]).astype(jnp.int32), axis=0)[None]
    low, high, prior_text, start, place = lax.optimization_barrier(
        (low, high, prior_text, start, place)
    )
    packed = pack(
        m1, c1, place, low, high, weights, part, ranks, capacity, per_shard, mixed
    )

    if mixed:
        kept, *moved = slices(m1, c1, [states, x, y, low, high], feats // mps)
        moved[1], moved[2], _ = lax.optimization_barrier((moved[1], moved[2], packed[0]))
        far_slices = [trade(moved[1], "ctx", 2), trade(moved[2], "ctx", 3)]
        image = [trade(packed[s], "ctx", s) if s else packed[0] for s in range(ranks)]
        moved[0], weights_late, *image = lax.optimization_barrier((moved[0], weights, *image))
        moved = [trade(moved[0], "ctx", 1)] + far_slices
    else:
        kept = None
        image = [exchange(packed[0], "ctx")]
        whole = lax.all_gather(states, "mp", axis=1, tiled=True)
        moved = whole.reshape(image_rows, ranks, mps, -1)
        moved = lax.dynamic_index_in_dim(moved, m, axis=2, keepdims=False).transpose(1, 0, 2)
        moved = [exchange(moved, "ctx").reshape(ranks * image_rows, -1)]
        weights_late, *image = lax.optimization_barrier((weights, *image))

    half = feats // 2

    def slab(head, side):
        return lax.dynamic_slice_in_dim(weights_late, head * feats + side * half, half)

    near = [trade(slab(m ^ s, d), "mp", s) for s in steps]

    attn_out, own_grad, prior_grad = attention(
        c1, place, start, queries[0], d_out[0], text_kv[0], prior_text, image,
        images, per_shard, image_rows,
    )
    prior_grad, near[0], near[-1], *moved = lax.optimization_barrier(
        (prior_grad, near[0], near[-1], *moved)
    )
    all_states = lax.all_gather(jnp.concatenate(moved, axis=0), "mp", axis=0)
    grad = own_grad + shift(prior_grad, "ctx", -1).astype(jnp.float32)
    grad = grad.astype(jnp.bfloat16)
    if mixed:
        gathered = [trade(grad, "ctx", s) if s else grad for s in range(ranks)]
    else:
        gathered = [exchange(jnp.broadcast_to(grad, (ranks,) + grad.shape), "ctx")]
    count = len(gathered)
    both = lax.optimization_barrier((*gathered, *near))
    gathered, near = both[:count], list(both[count:])
    far = [slab(m, 1 - d)] + [swap(w, "dp") for w in near]
    near = [slab(m, d)] + near
    by_rank, mine = reorder(c1, place, gathered, per_shard, images, ranks)
    head_grad = [mine] + [trade(mine, "mp", s) for s in steps]
    by_rank, *both = lax.optimization_barrier((by_rank, *head_grad, *far))
    head_grad, far = both[:mps], both[mps:]
    image_grad = image_term(d1, head_grad, near, far)
    term = weight_term(c1, kept, all_states, by_rank.reshape(ranks, image_rows, width))
    weight_grad = term + swap(term, "dp")
    return (attn_out[None], image_grad[None], weight_grad[None])


def solution(mesh):
    in_specs = (
        P("dp", "ctx", "mp"),
        P("dp", None),
        P("dp", None),
        P("dp", "ctx", "mp"),
        P("dp", "ctx", "mp"),
        P("mp", None, None),
        P("dp", "ctx", "mp"),
    )
    out_specs = (P("dp", "ctx", "mp"), P("dp", "ctx", "mp"), P("mp", "ctx", None))
    return jax.shard_map(
        per_device, mesh=mesh, in_specs=in_specs, out_specs=out_specs, check_vma=False
    )
```

```python
import functools

import jax
import jax.numpy as jnp
from jax import lax
from jax.experimental import pallas as pl
from jax.experimental.pallas import tpu as pltpu
from jax.sharding import PartitionSpec as P

IMGTOK = 16
QTILE = 128
SPANS = (2, 3)
LOG2E = 1.4426950408889634
VMEM = 24 * 1024 * 1024

NN = (((1,), (0,)), ((), ()))
NT = (((1,), (1,)), ((), ()))
TN = (((0,), (0,)), ((), ()))


def dot(a, b, dims):
    return lax.dot_general(a, b, dims, preferred_element_type=jnp.float32)


def params():
    return pltpu.CompilerParams(vmem_limit_bytes=VMEM)


def cost(flops, moved):
    return pl.CostEstimate(flops=int(flops), bytes_accessed=int(moved), transcendentals=0)


def shift(block, axis, distance):
    devices = range(lax.axis_size(axis))
    route = [(i - distance, i) for i in devices if i - distance in devices]
    return lax.ppermute(block, axis, route)


def swap(block, axis):
    count = lax.axis_size(axis)
    return lax.ppermute(block, axis, [(i, count - 1 - i) for i in range(count)])


def exchange(blocks, axis):
    return lax.all_to_all(blocks, axis, split_axis=0, concat_axis=0, tiled=True)


def trade(block, axis, step):
    count = lax.axis_size(axis)
    return lax.ppermute(block, axis, [(i, i ^ step) for i in range(count)])


def rows16(start):
    return pl.ds(pl.multiple_of(start * IMGTOK, IMGTOK), IMGTOK)


def project_body(m_ref, *refs):
    *pairs, out_ref = refs
    count = len(pairs) // 2
    total = dot(pairs[0][...], pairs[count][...], NN)
    for k in range(1, count):
        total = total + dot(pairs[k][...], pairs[count + k][...], NN)
    out_ref[...] = total


def project(m, blocks, weights):
    rows, feats = blocks[0].shape
    width = weights.shape[1]
    block = pl.BlockSpec((rows, feats), lambda i, m: (0, 0))
    chunk = lambda k: pl.BlockSpec((feats, width), lambda i, m: (m[0] ^ k, 0))
    return pl.pallas_call(
        project_body,
        grid_spec=pltpu.PrefetchScalarGridSpec(
            num_scalar_prefetch=1,
            grid=(1,),
            in_specs=[block] * len(blocks) + [chunk(k) for k in range(len(blocks))],
            out_specs=pl.BlockSpec((rows, width), lambda i, m: (0, 0)),
        ),
        out_shape=jax.ShapeDtypeStruct((rows, width), jnp.float32),
        cost_estimate=cost(2 * len(blocks) * rows * feats * width, 4 * len(blocks) * feats * width),
        compiler_params=params(),
    )(m, *blocks, *[weights] * len(blocks))


def pack_body(per_shard, m_ref, c_ref, place_ref, low_ref, high_ref, weight_ref, part_ref, *refs):
    out_refs = refs[:-3]
    rounded, sorted_ref, count = refs[-3:]
    shards = sorted_ref.shape[0]
    half = low_ref.shape[0]
    for at, ref in ((0, low_ref), (half, high_ref)):
        term = dot(ref[...], weight_ref[...], NN)
        rounded[at : at + half, :] = (part_ref[at : at + half, :] + term).astype(jnp.bfloat16)
    sorted_ref[...] = jnp.zeros_like(sorted_ref)
    for s in range(shards):
        count[s] = 0
    images = rounded.shape[0] // IMGTOK
    c = c_ref[0]

    def step(i, carry):
        dest = place_ref[c * images + i] // per_shard
        slot = count[dest]
        count[dest] = slot + 1
        block = rounded[rows16(i), :]
        sorted_ref[dest, 0, rows16(slot), :] = block

        @pl.when(dest + 1 < shards)
        def _():
            sorted_ref[dest + 1, 1, rows16(slot), :] = block

        return carry

    lax.fori_loop(0, images, step, 0)
    if len(out_refs) == 1:
        out_refs[0][...] = sorted_ref[...]
    else:
        for u, ref in enumerate(out_refs):
            ref[...] = sorted_ref[c ^ u]


def pack(m, c, place, low, high, weights, part, shards, capacity, per_shard, mixed):
    rows, width = part.shape
    feats = low.shape[1]
    whole = lambda a: pl.BlockSpec(a.shape, lambda i, *_: (0,) * len(a.shape))
    shape = (2, capacity, width)
    if mixed:
        out = [jax.ShapeDtypeStruct(shape, jnp.bfloat16)] * shards
    else:
        out = [jax.ShapeDtypeStruct((shards,) + shape, jnp.bfloat16)]
    return pl.pallas_call(
        functools.partial(pack_body, per_shard),
        grid_spec=pltpu.PrefetchScalarGridSpec(
            num_scalar_prefetch=3,
            grid=(1,),
            in_specs=[
                whole(low),
                whole(high),
                pl.BlockSpec((feats, width), lambda i, m, *_: (m[0] ^ 3, 0)),
                whole(part),
            ],
            out_specs=[whole(a) for a in out],
            scratch_shapes=[
                pltpu.VMEM((rows, width), jnp.bfloat16),
                pltpu.VMEM((shards,) + shape, jnp.bfloat16),
                pltpu.SMEM((shards,), jnp.int32),
            ],
        ),
        out_shape=out,
        cost_estimate=cost(2 * rows * feats * width, part.size * 16),
        compiler_params=params(),
    )(m, c, place, low, high, weights, part)


def slices_body(m_ref, c_ref, own_ref, x_ref, y_ref, low_ref, high_ref, kept_ref, *out_refs):
    m = m_ref[0]
    c = c_ref[0]
    sub = out_refs[0].shape[1]
    half = low_ref.shape[0]
    for u, ref in enumerate((kept_ref,) + out_refs):
        at = pl.ds(0, ref.shape[1]) if u == 0 else pl.ds(pl.multiple_of(m * sub, sub), sub)
        which = m ^ c ^ u
        for k, source in enumerate((own_ref, x_ref, y_ref)):

            @pl.when(which == k)
            def _():
                ref[...] = source[:, at]

        @pl.when(which == 3)
        def _():
            ref[:half, :] = low_ref[:, at]
            ref[half:, :] = high_ref[:, at]


def slices(m, c, blocks, sub):
    rows, feats = blocks[0].shape
    smem = pl.BlockSpec(memory_space=pltpu.SMEM)
    vmem = pl.BlockSpec(memory_space=pltpu.VMEM)
    dtype = blocks[0].dtype
    out = [jax.ShapeDtypeStruct((rows, feats), dtype)]
    out += [jax.ShapeDtypeStruct((rows, sub), dtype)] * 3
    return pl.pallas_call(
        slices_body,
        in_specs=[smem, smem] + [vmem] * len(blocks),
        out_specs=[vmem] * len(out),
        out_shape=out,
        cost_estimate=cost(0, rows * feats * 16),
        compiler_params=params(),
    )(m, c, *blocks)


def attention_body(
    per_shard,
    images,
    c_ref,
    place_ref,
    first_ref,
    start_ref,
    q_ref,
    g_ref,
    own_ref,
    prior_ref,
    *refs,
):
    image_refs = refs[:-8]
    out_ref, own_grad_ref, prior_grad_ref, window, probs, grads, total, image_ref = refs[-8:]
    t = pl.program_id(0)
    c = c_ref[0]
    rows = own_ref.shape[0]
    hd = own_ref.shape[1] // 2
    blocks = place_ref.shape[0]
    heads = q_ref.shape[1] // hd
    scale = hd ** (-0.5)

    @pl.when(t == 0)
    def _():
        window[:rows, :] = prior_ref[...]
        window[rows:, :] = own_ref[...]
        total[...] = jnp.zeros_like(total)
        if len(image_refs) == 1:
            image_ref[...] = image_refs[0][...]
        else:
            for u, ref in enumerate(image_refs):
                image_ref[c ^ u] = ref[...]

        def step(b, carry):
            n_own, n_prior = carry
            rank = b // images
            fresh = b % images == 0
            n_own = jnp.where(fresh, 0, n_own)
            n_prior = jnp.where(fresh, 0, n_prior)
            at = place_ref[b] - (c - 1) * per_shard
            is_prior = (at >= 0) & (at < per_shard)
            is_own = (at >= per_shard) & (at < 2 * per_shard)

            @pl.when(is_own)
            def _():
                window[rows16(at), :] = image_ref[rank, 0, rows16(n_own), :]

            @pl.when(is_prior)
            def _():
                window[rows16(at), :] = image_ref[rank, 1, rows16(n_prior), :]

            return n_own + is_own.astype(jnp.int32), n_prior + is_prior.astype(jnp.int32)

        lax.fori_loop(0, blocks, step, (jnp.int32(0), jnp.int32(0)))

    first = t * QTILE

    def stack(ref, a, b):
        return jnp.concatenate([ref[:, h * hd : (h + 1) * hd] for h in range(a, b)], axis=0)

    def tile(span):
        base = pl.multiple_of(first + (full - span), QTILE)
        keys = window[pl.ds(base, span), :hd]
        values = window[pl.ds(base, span), hd:]
        values_t = values.T
        key_pos = lax.broadcasted_iota(jnp.int32, (span, QTILE), 0) + base
        query_pos = lax.broadcasted_iota(jnp.int32, (span, QTILE), 1) + (first + rows)
        allowed = (key_pos <= query_pos) & (key_pos >= start_ref[...])
        bias = jnp.where(allowed, 0.0, -1e30)
        bias = jnp.concatenate([bias, bias], axis=1)

        def products(h):
            query = stack(q_ref, h, h + 2)
            grad = stack(g_ref, h, h + 2)
            return dot(keys, query, NT), dot(values, grad, NT)

        def softmax(h, scores):
            scores = scores * (scale * LOG2E) + bias
            top = jnp.max(scores, axis=0, keepdims=True)
            e = jnp.exp2(scores - top)
            p = e * (1.0 / jnp.sum(e, axis=0, keepdims=True))
            low = p.astype(jnp.bfloat16)
            probs[:span, h * QTILE : (h + 2) * QTILE] = low
            return p, dot(values_t, low, NN)

        def backward(h, p, grad_p, context_t):
            grad_t = stack(g_ref, h, h + 2).astype(jnp.float32).T
            delta = jnp.sum(grad_t * context_t, axis=0, keepdims=True)
            ds = (p * (grad_p - delta)).astype(jnp.bfloat16)
            context = context_t.T.astype(jnp.bfloat16)
            out_ref[:, h * hd : (h + 1) * hd] = context[:QTILE]
            out_ref[:, (h + 1) * hd : (h + 2) * hd] = context[QTILE:]
            grads[:span, h * QTILE : (h + 2) * QTILE] = ds

        pairs = heads // 2
        first_stage, second_stage = {}, {}
        for i in range(pairs + 2):
            if i < pairs:
                first_stage[i] = products(2 * i)
            if 1 <= i <= pairs:
                scores, grad_p = first_stage.pop(i - 1)
                second_stage[i - 1] = (grad_p, *softmax(2 * (i - 1), scores))
            if i >= 2:
                grad_p, p, context_t = second_stage.pop(i - 2)
                backward(2 * (i - 2), p, grad_p, context_t)
        total[pl.ds(base, span), :hd] += dot(grads[:span, :], stack(q_ref, 0, heads), NN)
        total[pl.ds(base, span), hd:] += dot(probs[:span, :], stack(g_ref, 0, heads), NN)

    full = rows + QTILE
    need = full - (first_ref[t] - first)
    below = 0
    for span in sorted({min(b * QTILE, full) for b in SPANS} | {full}):
        lower, below = below, span

        @pl.when((need > lower) & (need <= span))
        def _():
            tile(span)

    @pl.when(t == pl.num_programs(0) - 1)
    def _():
        total[:, :hd] = total[:, :hd] * scale
        prior_grad_ref[...] = jnp.zeros_like(prior_grad_ref)

        def step(b, carry):
            n_own, n_prior = carry
            at = place_ref[b] - (c - 1) * per_shard
            is_prior = (at >= 0) & (at < per_shard)
            is_own = (at >= per_shard) & (at < 2 * per_shard)

            @pl.when(is_own)
            def _():
                own_grad_ref[rows16(n_own), :] = total[rows16(at), :]

            @pl.when(is_prior)
            def _():
                prior_grad_ref[rows16(n_prior), :] = total[rows16(at), :].astype(jnp.bfloat16)

            return n_own + is_own.astype(jnp.int32), n_prior + is_prior.astype(jnp.int32)

        lax.fori_loop(0, blocks, step, (jnp.int32(0), jnp.int32(0)))


def attention(c, place, start, queries, d_out, own, prior, image, images, per_shard, image_rows):
    ranks = len(image) if len(image) > 1 else image[0].shape[0]
    rows, width = own.shape
    cols = queries.shape[1]
    tiles = rows // QTILE
    span = rows + QTILE
    head_rows = cols // (width // 2) * QTILE
    whole = lambda a: pl.BlockSpec(a.shape, lambda t, *_: (0,) * a.ndim)
    tile = pl.BlockSpec((QTILE, cols), lambda t, *_: (t, 0))
    grad = jax.ShapeDtypeStruct((image_rows, width), jnp.float32)
    prior_grad = jax.ShapeDtypeStruct((image_rows, width), jnp.bfloat16)
    return pl.pallas_call(
        functools.partial(attention_body, per_shard, images),
        grid_spec=pltpu.PrefetchScalarGridSpec(
            num_scalar_prefetch=3,
            grid=(tiles,),
            in_specs=[
                pl.BlockSpec((1, QTILE), lambda t, *_: (0, t)),
                tile,
                tile,
                whole(own),
                whole(prior),
                *map(whole, image),
            ],
            out_specs=[tile, whole(grad), whole(grad)],
            scratch_shapes=[
                pltpu.VMEM((2 * rows, width), jnp.bfloat16),
                pltpu.VMEM((span, head_rows), jnp.bfloat16),
                pltpu.VMEM((span, head_rows), jnp.bfloat16),
                pltpu.VMEM((2 * rows, width), jnp.float32),
                pltpu.VMEM((ranks,) + image[0].shape[-3:], jnp.bfloat16),
            ],
        ),
        out_shape=[jax.ShapeDtypeStruct((rows, cols), jnp.bfloat16), grad, prior_grad],
        cost_estimate=cost(2 * 20 * cols * span * rows, 4 * queries.size * 2),
        compiler_params=params(),
    )(c, place, start[0, ::QTILE], start, queries, d_out, own, prior, *image)


def reorder_body(per_shard, images, c_ref, place_ref, *refs):
    grad_refs = refs[:-4]
    out_ref, mine_ref, g_ref, count = refs[-4:]
    shards = g_ref.shape[0]
    if len(grad_refs) == 1:
        g_ref[...] = grad_refs[0][...]
    else:
        for u, ref in enumerate(grad_refs):
            g_ref[c_ref[0] ^ u] = ref[...]
    for s in range(shards):
        count[s] = 0
    c = c_ref[0]

    def step(b, carry):
        dest = place_ref[b] // per_shard
        slot = count[dest]
        count[dest] = slot + 1
        out_ref[rows16(b), :] = g_ref[dest, rows16(slot), :]
        return carry

    lax.fori_loop(0, place_ref.shape[0], step, 0)
    rows = mine_ref.shape[0]
    mine_ref[...] = out_ref[pl.ds(pl.multiple_of(c * rows, IMGTOK), rows), :]


def reorder(c, place, gathered, per_shard, images, shards):
    rows, width = gathered[0].shape[-2:]
    dtype = gathered[0].dtype
    smem = pl.BlockSpec(memory_space=pltpu.SMEM)
    vmem = pl.BlockSpec(memory_space=pltpu.VMEM)
    return pl.pallas_call(
        functools.partial(reorder_body, per_shard, images),
        in_specs=[smem, smem] + [vmem] * len(gathered),
        out_specs=[vmem, vmem],
        out_shape=[
            jax.ShapeDtypeStruct((shards * rows, width), dtype),
            jax.ShapeDtypeStruct((rows, width), dtype),
        ],
        scratch_shapes=[
            pltpu.VMEM((shards, rows, width), dtype),
            pltpu.SMEM((shards,), jnp.int32),
        ],
        cost_estimate=cost(0, shards * rows * width * 8),
        compiler_params=params(),
    )(c, place, *gathered)


def weight_body(s_ref, g_ref, out_ref):
    out_ref[...] = dot(s_ref[0], g_ref[...], TN)


def weight_term(states, grad):
    parts, rows, cols = states.shape
    width = grad.shape[1]
    return pl.pallas_call(
        weight_body,
        grid=(parts,),
        in_specs=[
            pl.BlockSpec((1, rows, cols), lambda k: (k, 0, 0)),
            pl.BlockSpec(grad.shape, lambda k: (0, 0)),
        ],
        out_specs=pl.BlockSpec((cols, width), lambda k: (k, 0)),
        out_shape=jax.ShapeDtypeStruct((parts * cols, width), jnp.float32),
        cost_estimate=cost(2 * states.size * width, states.size * 4),
        compiler_params=params(),
    )(states, grad)


def slice_body(first, groups, m_ref, c_ref, kept_ref, g_ref, *refs):
    out_ref = refs[-1]
    ranks, rows, width = g_ref.shape
    m = m_ref[0]
    c = c_ref[0]
    grad = jnp.concatenate([g_ref[c ^ u] for u in range(1, ranks)], axis=0)
    cols = refs[0].shape[1]
    state_refs = list(refs[:-1])
    for k, count in enumerate(groups):
        at = pl.multiple_of((m ^ (first + k)) * cols, cols)
        total = dot(kept_ref[:, pl.ds(at, cols)], g_ref[c], TN)
        done = 0
        for ref in state_refs[:count]:
            total = total + dot(ref[...], grad[done : done + ref.shape[0]], TN)
            done += ref.shape[0]
        state_refs = state_refs[count:]
        out_ref[k] = total


def slice_terms(first, groups, m, c, kept, grad, states):
    cols = states[0].shape[1]
    width = grad.shape[2]
    smem = pl.BlockSpec(memory_space=pltpu.SMEM)
    vmem = pl.BlockSpec(memory_space=pltpu.VMEM)
    rows = grad.shape[0] * grad.shape[1]
    return pl.pallas_call(
        functools.partial(slice_body, first, groups),
        in_specs=[smem, smem] + [vmem] * (2 + len(states)),
        out_specs=vmem,
        out_shape=jax.ShapeDtypeStruct((len(groups), cols, width), jnp.float32),
        cost_estimate=cost(2 * rows * cols * width * len(groups), rows * cols * len(groups) * 4),
        compiler_params=params(),
    )(m, c, kept, grad, *states)


def settle_body(m_ref, *refs):
    out_ref = refs[-1]
    m = m_ref[0]
    half = (len(refs) - 1) // 2
    k = 0
    for own, other in zip(refs[:half], refs[half:-1]):
        for i in range(own.shape[0]):
            cols = own.shape[1]
            at = pl.ds(pl.multiple_of((m ^ k) * cols, cols), cols)
            out_ref[at, :] = own[i] + other[i]
            k += 1


def settle(m, own, other):
    count = sum(a.shape[0] for a in own)
    _, cols, width = own[0].shape
    vmem = pl.BlockSpec(memory_space=pltpu.VMEM)
    return pl.pallas_call(
        settle_body,
        in_specs=[pl.BlockSpec(memory_space=pltpu.SMEM)] + [vmem] * (2 * len(own)),
        out_specs=vmem,
        out_shape=jax.ShapeDtypeStruct((count * cols, width), jnp.float32),
        cost_estimate=cost(0, count * cols * width * 12),
        compiler_params=params(),
    )(m, *own, *other)


def image_body(d_ref, *refs):
    out_ref = refs[-1]
    heads = (len(refs) - 1) // 3
    grads, near, far = refs[:heads], refs[heads : 2 * heads], refs[2 * heads : -1]
    j = pl.program_id(0)
    cols = near[0].shape[0]
    half = out_ref.shape[1] // 2
    d = d_ref[0]
    for weights, side in ((near, d), (far, 1 - d)):
        total = dot(grads[0][...], weights[0][...], NT)
        for h in range(1, heads):
            total = total + dot(grads[h][...], weights[h][...], NT)
        at = pl.multiple_of(side * half + j * cols, cols)
        out_ref[:, pl.ds(at, cols)] = total.astype(out_ref.dtype)


def image_term(d, grads, near, far):
    heads = len(near)
    half, width = near[0].shape
    rows = grads[0].shape[0]
    tiles = 4
    side = pl.BlockSpec((half // tiles, width), lambda j, d: (j, 0))
    grad = pl.BlockSpec((rows, width), lambda j, d: (0, 0))
    return pl.pallas_call(
        image_body,
        grid_spec=pltpu.PrefetchScalarGridSpec(
            num_scalar_prefetch=1,
            grid=(tiles,),
            in_specs=[grad] * heads + [side] * (2 * heads),
            out_specs=pl.BlockSpec((rows, 2 * half), lambda j, d: (0, 0)),
        ),
        out_shape=jax.ShapeDtypeStruct((rows, 2 * half), jnp.bfloat16),
        cost_estimate=cost(4 * heads * half * width * rows, 4 * heads * half * width * 2),
        compiler_params=params(),
    )(d, *grads, *near, *far)


def per_device(image_states, place_index, doc_ids, queries, text_kv, kv_weight, d_out):
    ranks = lax.axis_size("ctx")
    mps = lax.axis_size("mp")
    c = lax.axis_index("ctx")
    d = lax.axis_index("dp")
    rows = queries.shape[1]
    states = image_states[0]
    image_rows, feats = states.shape
    images = image_rows // IMGTOK
    per_shard = rows // IMGTOK
    capacity = IMGTOK * ((images + ranks - 1) // ranks)
    weights = kv_weight[0]
    width = weights.shape[1]
    c1 = jnp.reshape(c, (1,)).astype(jnp.int32)
    d1 = jnp.reshape(d, (1,)).astype(jnp.int32)
    place = place_index[0, ::IMGTOK] // IMGTOK

    m = lax.axis_index("mp")
    m1 = jnp.reshape(m, (1,)).astype(jnp.int32)
    steps = range(1, mps)
    mixed = ranks == mps

    x = trade(states, "mp", 1)
    y = trade(states, "mp", 2)
    low = trade(x[: image_rows // 2], "mp", 2)
    high = trade(y[image_rows // 2 :], "mp", 1)
    part = project(m1, [states, x, y], weights)

    prior_text = shift(text_kv[0], "ctx", 1)
    docs = doc_ids[0]
    own_docs = lax.dynamic_slice_in_dim(docs, c * rows, rows)
    prior_docs = lax.dynamic_slice_in_dim(docs, jnp.maximum(c - 1, 0) * rows, rows)
    prior_docs = jnp.where(c > 0, prior_docs, -1)
    key_docs = jnp.concatenate([prior_docs, own_docs])
    start = jnp.sum((key_docs[:, None] < own_docs[None, :]).astype(jnp.int32), axis=0)[None]
    low, high, prior_text, start, place = lax.optimization_barrier(
        (low, high, prior_text, start, place)
    )
    packed = pack(
        m1, c1, place, low, high, weights, part, ranks, capacity, per_shard, mixed
    )

    half = feats // 2

    def slab(head, side):
        return lax.dynamic_slice_in_dim(weights_late, head * feats + side * half, half)

    weights_late, _, _ = lax.optimization_barrier((weights, x, y))
    slabs = [slab(m ^ s, d) for s in steps]
    own_slabs = [slab(m, d), slab(m, 1 - d)]
    *both, _ = lax.optimization_barrier((*slabs, *own_slabs, packed[0]))
    slabs, own_slabs = both[: len(slabs)], both[len(slabs) :]
    near = [None] * len(slabs)
    near[0] = trade(slabs[0], "mp", 1)
    near[2] = trade(slabs[2], "mp", 3)

    if mixed:
        kept, *moved = slices(m1, c1, [states, x, y, low, high], feats // mps)
        image = [trade(packed[s], "ctx", s) if s else packed[0] for s in range(ranks)]
        both = lax.optimization_barrier((*moved, *image))
        moved, image = both[: len(moved)], both[len(moved) :]
        moved = [trade(moved[s - 1], "ctx", s) for s in range(1, ranks)]
    else:
        image = [exchange(packed[0], "ctx")]
        whole = lax.all_gather(states, "mp", axis=1, tiled=True)
        moved = whole.reshape(image_rows, ranks, mps, -1)
        moved = lax.dynamic_index_in_dim(moved, m, axis=2, keepdims=False).transpose(1, 0, 2)
        moved = [exchange(moved, "ctx").reshape(ranks * image_rows, -1)]

    attn_out, own_grad, prior_grad = attention(
        c1, place, start, queries[0], d_out[0], text_kv[0], prior_text, image,
        images, per_shard, image_rows,
    )
    early = ranks // 2 if mixed else 1
    prior_grad, slabs[1], near[0], near[2], *both = lax.optimization_barrier(
        (prior_grad, slabs[1], near[0], near[2], *moved[:early])
    )
    moved = both + list(moved[early:])
    near[1] = trade(slabs[1], "mp", 2)
    far = [own_slabs[1], swap(near[0], "dp"), None, swap(near[2], "dp")]
    grad = own_grad + shift(prior_grad, "ctx", -1).astype(jnp.float32)
    grad = grad.astype(jnp.bfloat16)
    grad, far[1], far[3], *moved = lax.optimization_barrier((grad, far[1], far[3], *moved))
    if mixed:
        gathered = [trade(grad, "ctx", s) if s else grad for s in range(ranks)]
        base = jnp.concatenate(moved, axis=0)
        cut = base.shape[0] // 2
        base_x = trade(base, "mp", 1)
        base_y = trade(base, "mp", 2)
        base_low = trade(base_x[:cut], "mp", 2)
        base_high = trade(base_y[cut:], "mp", 1)
    else:
        gathered = [exchange(jnp.broadcast_to(grad, (ranks,) + grad.shape), "ctx")]
        all_states = lax.all_gather(moved[0], "mp", axis=0)
    near[1], *gathered = lax.optimization_barrier((near[1], *gathered))
    by_rank, mine = reorder(c1, place, gathered, per_shard, images, ranks)
    head_grad = [mine] + [trade(mine, "mp", s) for s in steps]
    by_rank, *head_grad = lax.optimization_barrier((by_rank, *head_grad))
    far[2] = swap(near[1], "dp")
    near = [own_slabs[0]] + near
    image_grad = image_term(d1, head_grad, near, far)
    if mixed:
        by_rank = by_rank.reshape(ranks, image_rows, width)
        terms = [
            slice_terms(0, (1, 1, 1), m1, c1, kept, by_rank, [base, base_x, base_y]),
            slice_terms(3, (2,), m1, c1, kept, by_rank, [base_low, base_high]),
        ]
        weight_grad = settle(m1, terms, [swap(a, "dp") for a in terms])
    else:
        term = weight_term(all_states, by_rank)
        weight_grad = term + swap(term, "dp")
    return (attn_out[None], image_grad[None], weight_grad[None])


def solution(mesh):
    in_specs = (
        P("dp", "ctx", "mp"),
        P("dp", None),
        P("dp", None),
        P("dp", "ctx", "mp"),
        P("dp", "ctx", "mp"),
        P("mp", None, None),
        P("dp", "ctx", "mp"),
    )
    out_specs = (P("dp", "ctx", "mp"), P("dp", "ctx", "mp"), P("mp", "ctx", None))
    return jax.shard_map(
        per_device, mesh=mesh, in_specs=in_specs, out_specs=out_specs, check_vma=False
    )
```

```python
import functools

import jax
import jax.numpy as jnp
from jax import lax
from jax.experimental import pallas as pl
from jax.experimental.pallas import tpu as pltpu
from jax.sharding import PartitionSpec as P

IMGTOK = 16
QTILE = 128
SPANS = (2, 3)
LOG2E = 1.4426950408889634
VMEM = 24 * 1024 * 1024

NN = (((1,), (0,)), ((), ()))
NT = (((1,), (1,)), ((), ()))
TN = (((0,), (0,)), ((), ()))


def dot(a, b, dims):
    return lax.dot_general(a, b, dims, preferred_element_type=jnp.float32)


def params():
    return pltpu.CompilerParams(vmem_limit_bytes=VMEM)


def cost(flops, moved):
    return pl.CostEstimate(flops=int(flops), bytes_accessed=int(moved), transcendentals=0)


def shift(block, axis, distance):
    devices = range(lax.axis_size(axis))
    route = [(i - distance, i) for i in devices if i - distance in devices]
    return lax.ppermute(block, axis, route)


def swap(block, axis):
    count = lax.axis_size(axis)
    return lax.ppermute(block, axis, [(i, count - 1 - i) for i in range(count)])


def exchange(blocks, axis):
    return lax.all_to_all(blocks, axis, split_axis=0, concat_axis=0, tiled=True)


def trade(block, axis, step):
    count = lax.axis_size(axis)
    return lax.ppermute(block, axis, [(i, i ^ step) for i in range(count)])


def rows16(start):
    return pl.ds(pl.multiple_of(start * IMGTOK, IMGTOK), IMGTOK)


def project_body(m_ref, *refs):
    *pairs, out_ref = refs
    count = len(pairs) // 2
    total = dot(pairs[0][...], pairs[count][...], NN)
    for k in range(1, count):
        total = total + dot(pairs[k][...], pairs[count + k][...], NN)
    out_ref[...] = total


def project(m, blocks, weights):
    rows, feats = blocks[0].shape
    width = weights.shape[1]
    block = pl.BlockSpec((rows, feats), lambda i, m: (0, 0))
    chunk = lambda k: pl.BlockSpec((feats, width), lambda i, m: (m[0] ^ k, 0))
    return pl.pallas_call(
        project_body,
        grid_spec=pltpu.PrefetchScalarGridSpec(
            num_scalar_prefetch=1,
            grid=(1,),
            in_specs=[block] * len(blocks) + [chunk(k) for k in range(len(blocks))],
            out_specs=pl.BlockSpec((rows, width), lambda i, m: (0, 0)),
        ),
        out_shape=jax.ShapeDtypeStruct((rows, width), jnp.float32),
        cost_estimate=cost(2 * len(blocks) * rows * feats * width, 4 * len(blocks) * feats * width),
        compiler_params=params(),
    )(m, *blocks, *[weights] * len(blocks))


def pack_body(per_shard, m_ref, c_ref, place_ref, low_ref, high_ref, weight_ref, part_ref, *refs):
    out_refs = refs[:-3]
    rounded, sorted_ref, count = refs[-3:]
    shards = sorted_ref.shape[0]
    half = low_ref.shape[0]
    for at, ref in ((0, low_ref), (half, high_ref)):
        term = dot(ref[...], weight_ref[...], NN)
        rounded[at : at + half, :] = (part_ref[at : at + half, :] + term).astype(jnp.bfloat16)
    sorted_ref[...] = jnp.zeros_like(sorted_ref)
    for s in range(shards):
        count[s] = 0
    images = rounded.shape[0] // IMGTOK
    c = c_ref[0]

    def step(i, carry):
        dest = place_ref[c * images + i] // per_shard
        slot = count[dest]
        count[dest] = slot + 1
        block = rounded[rows16(i), :]
        sorted_ref[dest, 0, rows16(slot), :] = block

        @pl.when(dest + 1 < shards)
        def _():
            sorted_ref[dest + 1, 1, rows16(slot), :] = block

        return carry

    lax.fori_loop(0, images, step, 0)
    if len(out_refs) == 1:
        out_refs[0][...] = sorted_ref[...]
    else:
        for u, ref in enumerate(out_refs):
            ref[...] = sorted_ref[c ^ u]


def pack(m, c, place, low, high, weights, part, shards, capacity, per_shard, mixed):
    rows, width = part.shape
    feats = low.shape[1]
    whole = lambda a: pl.BlockSpec(a.shape, lambda i, *_: (0,) * len(a.shape))
    shape = (2, capacity, width)
    if mixed:
        out = [jax.ShapeDtypeStruct(shape, jnp.bfloat16)] * shards
    else:
        out = [jax.ShapeDtypeStruct((shards,) + shape, jnp.bfloat16)]
    return pl.pallas_call(
        functools.partial(pack_body, per_shard),
        grid_spec=pltpu.PrefetchScalarGridSpec(
            num_scalar_prefetch=3,
            grid=(1,),
            in_specs=[
                whole(low),
                whole(high),
                pl.BlockSpec((feats, width), lambda i, m, *_: (m[0] ^ 3, 0)),
                whole(part),
            ],
            out_specs=[whole(a) for a in out],
            scratch_shapes=[
                pltpu.VMEM((rows, width), jnp.bfloat16),
                pltpu.VMEM((shards,) + shape, jnp.bfloat16),
                pltpu.SMEM((shards,), jnp.int32),
            ],
        ),
        out_shape=out,
        cost_estimate=cost(2 * rows * feats * width, part.size * 16),
        compiler_params=params(),
    )(m, c, place, low, high, weights, part)


def slices_body(m_ref, c_ref, own_ref, x_ref, y_ref, low_ref, high_ref, kept_ref, *out_refs):
    m = m_ref[0]
    c = c_ref[0]
    sub = out_refs[0].shape[1]
    half = low_ref.shape[0]
    for u, ref in enumerate((kept_ref,) + out_refs):
        at = pl.ds(0, ref.shape[1]) if u == 0 else pl.ds(pl.multiple_of(m * sub, sub), sub)
        which = m ^ c ^ u
        for k, source in enumerate((own_ref, x_ref, y_ref)):

            @pl.when(which == k)
            def _():
                ref[...] = source[:, at]

        @pl.when(which == 3)
        def _():
            ref[:half, :] = low_ref[:, at]
            ref[half:, :] = high_ref[:, at]


def slices(m, c, blocks, sub):
    rows, feats = blocks[0].shape
    smem = pl.BlockSpec(memory_space=pltpu.SMEM)
    vmem = pl.BlockSpec(memory_space=pltpu.VMEM)
    dtype = blocks[0].dtype
    out = [jax.ShapeDtypeStruct((rows, feats), dtype)]
    out += [jax.ShapeDtypeStruct((rows, sub), dtype)] * 3
    return pl.pallas_call(
        slices_body,
        in_specs=[smem, smem] + [vmem] * len(blocks),
        out_specs=[vmem] * len(out),
        out_shape=out,
        cost_estimate=cost(0, rows * feats * 16),
        compiler_params=params(),
    )(m, c, *blocks)


def attention_body(
    per_shard,
    images,
    c_ref,
    place_ref,
    first_ref,
    start_ref,
    q_ref,
    g_ref,
    own_ref,
    prior_ref,
    *refs,
):
    image_refs = refs[:-8]
    out_ref, own_grad_ref, prior_grad_ref, window, probs, grads, total, image_ref = refs[-8:]
    t = pl.program_id(0)
    c = c_ref[0]
    rows = own_ref.shape[0]
    hd = own_ref.shape[1] // 2
    blocks = place_ref.shape[0]
    heads = q_ref.shape[1] // hd
    scale = hd ** (-0.5)

    @pl.when(t == 0)
    def _():
        window[:rows, :] = prior_ref[...]
        window[rows:, :] = own_ref[...]
        total[...] = jnp.zeros_like(total)
        if len(image_refs) == 1:
            image_ref[...] = image_refs[0][...]
        else:
            for u, ref in enumerate(image_refs):
                image_ref[c ^ u] = ref[...]

        def step(b, carry):
            n_own, n_prior = carry
            rank = b // images
            fresh = b % images == 0
            n_own = jnp.where(fresh, 0, n_own)
            n_prior = jnp.where(fresh, 0, n_prior)
            at = place_ref[b] - (c - 1) * per_shard
            is_prior = (at >= 0) & (at < per_shard)
            is_own = (at >= per_shard) & (at < 2 * per_shard)

            @pl.when(is_own)
            def _():
                window[rows16(at), :] = image_ref[rank, 0, rows16(n_own), :]

            @pl.when(is_prior)
            def _():
                window[rows16(at), :] = image_ref[rank, 1, rows16(n_prior), :]

            return n_own + is_own.astype(jnp.int32), n_prior + is_prior.astype(jnp.int32)

        lax.fori_loop(0, blocks, step, (jnp.int32(0), jnp.int32(0)))

    first = t * QTILE

    def stack(ref, a, b):
        return jnp.concatenate([ref[:, h * hd : (h + 1) * hd] for h in range(a, b)], axis=0)

    def tile(span):
        base = pl.multiple_of(first + (full - span), QTILE)
        keys = window[pl.ds(base, span), :hd]
        values = window[pl.ds(base, span), hd:]
        values_t = values.T
        key_pos = lax.broadcasted_iota(jnp.int32, (span, QTILE), 0) + base
        query_pos = lax.broadcasted_iota(jnp.int32, (span, QTILE), 1) + (first + rows)
        allowed = (key_pos <= query_pos) & (key_pos >= start_ref[...])
        bias = jnp.where(allowed, 0.0, -1e30)
        bias = jnp.concatenate([bias, bias], axis=1)

        def products(h):
            query = stack(q_ref, h, h + 2)
            grad = stack(g_ref, h, h + 2)
            return dot(keys, query, NT), dot(values, grad, NT)

        def softmax(h, scores):
            scores = scores * (scale * LOG2E) + bias
            top = jnp.max(scores, axis=0, keepdims=True)
            e = jnp.exp2(scores - top)
            p = e * (1.0 / jnp.sum(e, axis=0, keepdims=True))
            low = p.astype(jnp.bfloat16)
            probs[:span, h * QTILE : (h + 2) * QTILE] = low
            return p, dot(values_t, low, NN)

        def backward(h, p, grad_p, context_t):
            grad_t = stack(g_ref, h, h + 2).astype(jnp.float32).T
            delta = jnp.sum(grad_t * context_t, axis=0, keepdims=True)
            ds = (p * (grad_p - delta)).astype(jnp.bfloat16)
            context = context_t.T.astype(jnp.bfloat16)
            out_ref[:, h * hd : (h + 1) * hd] = context[:QTILE]
            out_ref[:, (h + 1) * hd : (h + 2) * hd] = context[QTILE:]
            grads[:span, h * QTILE : (h + 2) * QTILE] = ds

        pairs = heads // 2
        first_stage, second_stage = {}, {}
        for i in range(pairs + 2):
            if i < pairs:
                first_stage[i] = products(2 * i)
            if 1 <= i <= pairs:
                scores, grad_p = first_stage.pop(i - 1)
                second_stage[i - 1] = (grad_p, *softmax(2 * (i - 1), scores))
            if i >= 2:
                grad_p, p, context_t = second_stage.pop(i - 2)
                backward(2 * (i - 2), p, grad_p, context_t)
        total[pl.ds(base, span), :hd] += dot(grads[:span, :], stack(q_ref, 0, heads), NN)
        total[pl.ds(base, span), hd:] += dot(probs[:span, :], stack(g_ref, 0, heads), NN)

    full = rows + QTILE
    need = full - (first_ref[t] - first)
    below = 0
    for span in sorted({min(b * QTILE, full) for b in SPANS} | {full}):
        lower, below = below, span

        @pl.when((need > lower) & (need <= span))
        def _():
            tile(span)

    @pl.when(t == pl.num_programs(0) - 1)
    def _():
        total[:, :hd] = total[:, :hd] * scale
        prior_grad_ref[...] = jnp.zeros_like(prior_grad_ref)

        def step(b, carry):
            n_own, n_prior = carry
            at = place_ref[b] - (c - 1) * per_shard
            is_prior = (at >= 0) & (at < per_shard)
            is_own = (at >= per_shard) & (at < 2 * per_shard)

            @pl.when(is_own)
            def _():
                own_grad_ref[rows16(n_own), :] = total[rows16(at), :]

            @pl.when(is_prior)
            def _():
                prior_grad_ref[rows16(n_prior), :] = total[rows16(at), :].astype(jnp.bfloat16)

            return n_own + is_own.astype(jnp.int32), n_prior + is_prior.astype(jnp.int32)

        lax.fori_loop(0, blocks, step, (jnp.int32(0), jnp.int32(0)))


def attention(c, place, start, queries, d_out, own, prior, image, images, per_shard, image_rows):
    ranks = len(image) if len(image) > 1 else image[0].shape[0]
    rows, width = own.shape
    cols = queries.shape[1]
    tiles = rows // QTILE
    span = rows + QTILE
    head_rows = cols // (width // 2) * QTILE
    whole = lambda a: pl.BlockSpec(a.shape, lambda t, *_: (0,) * a.ndim)
    tile = pl.BlockSpec((QTILE, cols), lambda t, *_: (t, 0))
    grad = jax.ShapeDtypeStruct((image_rows, width), jnp.float32)
    prior_grad = jax.ShapeDtypeStruct((image_rows, width), jnp.bfloat16)
    return pl.pallas_call(
        functools.partial(attention_body, per_shard, images),
        grid_spec=pltpu.PrefetchScalarGridSpec(
            num_scalar_prefetch=3,
            grid=(tiles,),
            in_specs=[
                pl.BlockSpec((1, QTILE), lambda t, *_: (0, t)),
                tile,
                tile,
                whole(own),
                whole(prior),
                *map(whole, image),
            ],
            out_specs=[tile, whole(grad), whole(grad)],
            scratch_shapes=[
                pltpu.VMEM((2 * rows, width), jnp.bfloat16),
                pltpu.VMEM((span, head_rows), jnp.bfloat16),
                pltpu.VMEM((span, head_rows), jnp.bfloat16),
                pltpu.VMEM((2 * rows, width), jnp.float32),
                pltpu.VMEM((ranks,) + image[0].shape[-3:], jnp.bfloat16),
            ],
        ),
        out_shape=[jax.ShapeDtypeStruct((rows, cols), jnp.bfloat16), grad, prior_grad],
        cost_estimate=cost(2 * 20 * cols * span * rows, 4 * queries.size * 2),
        compiler_params=params(),
    )(c, place, start[0, ::QTILE], start, queries, d_out, own, prior, *image)


def reorder_body(per_shard, images, c_ref, place_ref, *refs):
    grad_refs = refs[:-4]
    out_ref, mine_ref, g_ref, count = refs[-4:]
    shards = g_ref.shape[0]
    if len(grad_refs) == 1:
        g_ref[...] = grad_refs[0][...]
    else:
        for u, ref in enumerate(grad_refs):
            g_ref[c_ref[0] ^ u] = ref[...]
    for s in range(shards):
        count[s] = 0
    c = c_ref[0]

    def step(b, carry):
        dest = place_ref[b] // per_shard
        slot = count[dest]
        count[dest] = slot + 1
        out_ref[rows16(b), :] = g_ref[dest, rows16(slot), :]
        return carry

    lax.fori_loop(0, place_ref.shape[0], step, 0)
    rows = mine_ref.shape[0]
    mine_ref[...] = out_ref[pl.ds(pl.multiple_of(c * rows, IMGTOK), rows), :]


def reorder(c, place, gathered, per_shard, images, shards):
    rows, width = gathered[0].shape[-2:]
    dtype = gathered[0].dtype
    smem = pl.BlockSpec(memory_space=pltpu.SMEM)
    vmem = pl.BlockSpec(memory_space=pltpu.VMEM)
    return pl.pallas_call(
        functools.partial(reorder_body, per_shard, images),
        in_specs=[smem, smem] + [vmem] * len(gathered),
        out_specs=[vmem, vmem],
        out_shape=[
            jax.ShapeDtypeStruct((shards * rows, width), dtype),
            jax.ShapeDtypeStruct((rows, width), dtype),
        ],
        scratch_shapes=[
            pltpu.VMEM((shards, rows, width), dtype),
            pltpu.SMEM((shards,), jnp.int32),
        ],
        cost_estimate=cost(0, shards * rows * width * 8),
        compiler_params=params(),
    )(c, place, *gathered)


def weight_body(s_ref, g_ref, out_ref):
    out_ref[...] = dot(s_ref[0], g_ref[...], TN)


def weight_term(states, grad):
    parts, rows, cols = states.shape
    width = grad.shape[1]
    return pl.pallas_call(
        weight_body,
        grid=(parts,),
        in_specs=[
            pl.BlockSpec((1, rows, cols), lambda k: (k, 0, 0)),
            pl.BlockSpec(grad.shape, lambda k: (0, 0)),
        ],
        out_specs=pl.BlockSpec((cols, width), lambda k: (k, 0)),
        out_shape=jax.ShapeDtypeStruct((parts * cols, width), jnp.float32),
        cost_estimate=cost(2 * states.size * width, states.size * 4),
        compiler_params=params(),
    )(states, grad)


def slice_body(first, groups, m_ref, c_ref, kept_ref, g_ref, *refs):
    out_ref = refs[-1]
    ranks, rows, width = g_ref.shape
    m = m_ref[0]
    c = c_ref[0]
    grad = jnp.concatenate([g_ref[c ^ u] for u in range(1, ranks)], axis=0)
    cols = refs[0].shape[1]
    state_refs = list(refs[:-1])
    for k, count in enumerate(groups):
        at = pl.multiple_of((m ^ (first + k)) * cols, cols)
        total = dot(kept_ref[:, pl.ds(at, cols)], g_ref[c], TN)
        done = 0
        for ref in state_refs[:count]:
            total = total + dot(ref[...], grad[done : done + ref.shape[0]], TN)
            done += ref.shape[0]
        state_refs = state_refs[count:]
        out_ref[k] = total


def slice_terms(first, groups, m, c, kept, grad, states):
    cols = states[0].shape[1]
    width = grad.shape[2]
    smem = pl.BlockSpec(memory_space=pltpu.SMEM)
    vmem = pl.BlockSpec(memory_space=pltpu.VMEM)
    rows = grad.shape[0] * grad.shape[1]
    return pl.pallas_call(
        functools.partial(slice_body, first, groups),
        in_specs=[smem, smem] + [vmem] * (2 + len(states)),
        out_specs=vmem,
        out_shape=jax.ShapeDtypeStruct((len(groups), cols, width), jnp.float32),
        cost_estimate=cost(2 * rows * cols * width * len(groups), rows * cols * len(groups) * 4),
        compiler_params=params(),
    )(m, c, kept, grad, *states)


def settle_body(m_ref, *refs):
    out_ref = refs[-1]
    m = m_ref[0]
    half = (len(refs) - 1) // 2
    k = 0
    for own, other in zip(refs[:half], refs[half:-1]):
        for i in range(own.shape[0]):
            cols = own.shape[1]
            at = pl.ds(pl.multiple_of((m ^ k) * cols, cols), cols)
            out_ref[at, :] = own[i] + other[i]
            k += 1


def settle(m, own, other):
    count = sum(a.shape[0] for a in own)
    _, cols, width = own[0].shape
    vmem = pl.BlockSpec(memory_space=pltpu.VMEM)
    return pl.pallas_call(
        settle_body,
        in_specs=[pl.BlockSpec(memory_space=pltpu.SMEM)] + [vmem] * (2 * len(own)),
        out_specs=vmem,
        out_shape=jax.ShapeDtypeStruct((count * cols, width), jnp.float32),
        cost_estimate=cost(0, count * cols * width * 12),
        compiler_params=params(),
    )(m, *own, *other)


def image_body(d_ref, *refs):
    out_ref = refs[-1]
    heads = (len(refs) - 1) // 3
    grads, near, far = refs[:heads], refs[heads : 2 * heads], refs[2 * heads : -1]
    j = pl.program_id(0)
    cols = near[0].shape[0]
    half = out_ref.shape[1] // 2
    d = d_ref[0]
    for weights, side in ((near, d), (far, 1 - d)):
        total = dot(grads[0][...], weights[0][...], NT)
        for h in range(1, heads):
            total = total + dot(grads[h][...], weights[h][...], NT)
        at = pl.multiple_of(side * half + j * cols, cols)
        out_ref[:, pl.ds(at, cols)] = total.astype(out_ref.dtype)


def image_term(d, grads, near, far):
    heads = len(near)
    half, width = near[0].shape
    rows = grads[0].shape[0]
    tiles = 4
    side = pl.BlockSpec((half // tiles, width), lambda j, d: (j, 0))
    grad = pl.BlockSpec((rows, width), lambda j, d: (0, 0))
    return pl.pallas_call(
        image_body,
        grid_spec=pltpu.PrefetchScalarGridSpec(
            num_scalar_prefetch=1,
            grid=(tiles,),
            in_specs=[grad] * heads + [side] * (2 * heads),
            out_specs=pl.BlockSpec((rows, 2 * half), lambda j, d: (0, 0)),
        ),
        out_shape=jax.ShapeDtypeStruct((rows, 2 * half), jnp.bfloat16),
        cost_estimate=cost(4 * heads * half * width * rows, 4 * heads * half * width * 2),
        compiler_params=params(),
    )(d, *grads, *near, *far)


def per_device(image_states, place_index, doc_ids, queries, text_kv, kv_weight, d_out):
    ranks = lax.axis_size("ctx")
    mps = lax.axis_size("mp")
    c = lax.axis_index("ctx")
    d = lax.axis_index("dp")
    rows = queries.shape[1]
    states = image_states[0]
    image_rows, feats = states.shape
    images = image_rows // IMGTOK
    per_shard = rows // IMGTOK
    capacity = IMGTOK * ((images + ranks - 1) // ranks)
    weights = kv_weight[0]
    width = weights.shape[1]
    c1 = jnp.reshape(c, (1,)).astype(jnp.int32)
    d1 = jnp.reshape(d, (1,)).astype(jnp.int32)
    place = place_index[0, ::IMGTOK] // IMGTOK

    m = lax.axis_index("mp")
    m1 = jnp.reshape(m, (1,)).astype(jnp.int32)
    steps = range(1, mps)
    mixed = ranks == mps

    x = trade(states, "mp", 1)
    y = trade(states, "mp", 2)
    low = trade(x[: image_rows // 2], "mp", 2)
    high = trade(y[image_rows // 2 :], "mp", 1)
    part = project(m1, [states, x, y], weights)

    prior_text = shift(text_kv[0], "ctx", 1)
    docs = doc_ids[0]
    own_docs = lax.dynamic_slice_in_dim(docs, c * rows, rows)
    prior_docs = lax.dynamic_slice_in_dim(docs, jnp.maximum(c - 1, 0) * rows, rows)
    prior_docs = jnp.where(c > 0, prior_docs, -1)
    key_docs = jnp.concatenate([prior_docs, own_docs])
    start = jnp.sum((key_docs[:, None] < own_docs[None, :]).astype(jnp.int32), axis=0)[None]
    low, high, prior_text, start, place = lax.optimization_barrier(
        (low, high, prior_text, start, place)
    )
    packed = pack(
        m1, c1, place, low, high, weights, part, ranks, capacity, per_shard, mixed
    )

    half = feats // 2

    def slab(head, side):
        return lax.dynamic_slice_in_dim(weights_late, head * feats + side * half, half)

    weights_late, _, _ = lax.optimization_barrier((weights, x, y))
    slabs = [slab(m ^ s, d) for s in steps]
    own_slabs = [slab(m, d), slab(m, 1 - d)]
    *both, _ = lax.optimization_barrier((*slabs, *own_slabs, packed[0]))
    slabs, own_slabs = both[: len(slabs)], both[len(slabs) :]
    last = trade(slabs[2], "mp", 3)

    if mixed:
        kept, *moved = slices(m1, c1, [states, x, y, low, high], feats // mps)
        moved[2], _ = lax.optimization_barrier((moved[2], packed[0]))
        moved[2] = trade(moved[2], "ctx", 3)
        image = [trade(packed[s], "ctx", s) if s else packed[0] for s in range(ranks)]
        moved[0], moved[1], slabs[0], slabs[1], *image = lax.optimization_barrier(
            (moved[0], moved[1], slabs[0], slabs[1], *image)
        )
        moved = [trade(moved[0], "ctx", 1), trade(moved[1], "ctx", 2), moved[2]]
    else:
        image = [exchange(packed[0], "ctx")]
        whole = lax.all_gather(states, "mp", axis=1, tiled=True)
        moved = whole.reshape(image_rows, ranks, mps, -1)
        moved = lax.dynamic_index_in_dim(moved, m, axis=2, keepdims=False).transpose(1, 0, 2)
        moved = [exchange(moved, "ctx").reshape(ranks * image_rows, -1)]
    near = [trade(slabs[0], "mp", 1), trade(slabs[1], "mp", 2), last]

    attn_out, own_grad, prior_grad = attention(
        c1, place, start, queries[0], d_out[0], text_kv[0], prior_text, image,
        images, per_shard, image_rows,
    )
    prior_grad, *both = lax.optimization_barrier((prior_grad, *near, *moved))
    near, moved = both[: len(near)], both[len(near) :]
    far = [own_slabs[1]] + [swap(w, "dp") for w in near]
    grad = own_grad + shift(prior_grad, "ctx", -1).astype(jnp.float32)
    grad = grad.astype(jnp.bfloat16)
    if mixed:
        gathered = [trade(grad, "ctx", s) if s else grad for s in range(ranks)]
        base = jnp.concatenate(moved, axis=0)
        cut = base.shape[0] // 2
        base_x = trade(base, "mp", 1)
        base_y = trade(base, "mp", 2)
    else:
        gathered = [exchange(jnp.broadcast_to(grad, (ranks,) + grad.shape), "ctx")]
        all_states = lax.all_gather(moved[0], "mp", axis=0)
        base_x = base_y = all_states
    base_x, base_y, *both = lax.optimization_barrier((base_x, base_y, *far, *gathered))
    far, gathered = both[: len(far)], both[len(far) :]
    by_rank, mine = reorder(c1, place, gathered, per_shard, images, ranks)
    head_grad = [mine] + [trade(mine, "mp", s) for s in steps]
    if mixed:
        base_low = trade(base_x[:cut], "mp", 2)
        base_high = trade(base_y[cut:], "mp", 1)
        by_rank, base_low, base_high, *head_grad = lax.optimization_barrier(
            (by_rank, base_low, base_high, *head_grad)
        )
    near = [own_slabs[0]] + list(near)
    image_grad = image_term(d1, head_grad, near, far)
    if mixed:
        by_rank = by_rank.reshape(ranks, image_rows, width)
        terms = [
            slice_terms(0, (1, 1, 1), m1, c1, kept, by_rank, [base, base_x, base_y]),
            slice_terms(3, (2,), m1, c1, kept, by_rank, [base_low, base_high]),
        ]
        weight_grad = settle(m1, terms, [swap(a, "dp") for a in terms])
    else:
        term = weight_term(all_states, by_rank)
        weight_grad = term + swap(term, "dp")
    return (attn_out[None], image_grad[None], weight_grad[None])


def solution(mesh):
    in_specs = (
        P("dp", "ctx", "mp"),
        P("dp", None),
        P("dp", None),
        P("dp", "ctx", "mp"),
        P("dp", "ctx", "mp"),
        P("mp", None, None),
        P("dp", "ctx", "mp"),
    )
    out_specs = (P("dp", "ctx", "mp"), P("dp", "ctx", "mp"), P("mp", "ctx", None))
    return jax.shard_map(
        per_device, mesh=mesh, in_specs=in_specs, out_specs=out_specs, check_vma=False
    )
```

```python
import functools

import jax
import jax.numpy as jnp
from jax import lax
from jax.experimental import pallas as pl
from jax.experimental.pallas import tpu as pltpu
from jax.sharding import PartitionSpec as P

IMGTOK = 16
QTILE = 128
SPANS = (2, 3)
LOG2E = 1.4426950408889634
VMEM = 24 * 1024 * 1024

NN = (((1,), (0,)), ((), ()))
NT = (((1,), (1,)), ((), ()))
TN = (((0,), (0,)), ((), ()))


def dot(a, b, dims):
    return lax.dot_general(a, b, dims, preferred_element_type=jnp.float32)


def params():
    return pltpu.CompilerParams(vmem_limit_bytes=VMEM)


def cost(flops, moved):
    return pl.CostEstimate(flops=int(flops), bytes_accessed=int(moved), transcendentals=0)


def shift(block, axis, distance):
    devices = range(lax.axis_size(axis))
    route = [(i - distance, i) for i in devices if i - distance in devices]
    return lax.ppermute(block, axis, route)


def swap(block, axis):
    count = lax.axis_size(axis)
    return lax.ppermute(block, axis, [(i, count - 1 - i) for i in range(count)])


def exchange(blocks, axis):
    return lax.all_to_all(blocks, axis, split_axis=0, concat_axis=0, tiled=True)


def trade(block, axis, step):
    count = lax.axis_size(axis)
    return lax.ppermute(block, axis, [(i, i ^ step) for i in range(count)])


def rows16(start):
    return pl.ds(pl.multiple_of(start * IMGTOK, IMGTOK), IMGTOK)


def project_body(m_ref, d_ref, own_ref, x_ref, y_ref, weight_ref, out_ref, *slab_refs):
    m = m_ref[0]
    d = d_ref[0]
    feats = own_ref.shape[1]
    half = slab_refs[0].shape[0]

    def rows(k, at, count):
        return pl.ds(pl.multiple_of((m ^ k) * feats + at, half), count)

    total = dot(own_ref[...], weight_ref[rows(0, 0, feats), :], NN)
    for k, ref in ((1, x_ref), (2, y_ref)):
        total = total + dot(ref[...], weight_ref[rows(k, 0, feats), :], NN)
    out_ref[...] = total
    for k, side, ref in zip((1, 2, 3, 0, 0), (d, d, d, d, 1 - d), slab_refs):
        ref[...] = weight_ref[rows(k, side * half, half), :]


def project(m, d, blocks, weights):
    rows, feats = blocks[0].shape
    width = weights.shape[1]
    smem = pl.BlockSpec(memory_space=pltpu.SMEM)
    vmem = pl.BlockSpec(memory_space=pltpu.VMEM)
    slab = jax.ShapeDtypeStruct((feats // 2, width), weights.dtype)
    return pl.pallas_call(
        project_body,
        in_specs=[smem, smem] + [vmem] * 4,
        out_specs=[vmem] * 6,
        out_shape=[jax.ShapeDtypeStruct((rows, width), jnp.float32)] + [slab] * 5,
        cost_estimate=cost(6 * rows * feats * width, 4 * weights.size),
        compiler_params=params(),
    )(m, d, *blocks, weights)


def pack_body(per_shard, m_ref, c_ref, place_ref, low_ref, high_ref, weight_ref, part_ref, *refs):
    out_refs = refs[:-3]
    rounded, sorted_ref, count = refs[-3:]
    shards = sorted_ref.shape[0]
    half = low_ref.shape[0]
    for at, ref in ((0, low_ref), (half, high_ref)):
        term = dot(ref[...], weight_ref[...], NN)
        rounded[at : at + half, :] = (part_ref[at : at + half, :] + term).astype(jnp.bfloat16)
    sorted_ref[...] = jnp.zeros_like(sorted_ref)
    for s in range(shards):
        count[s] = 0
    images = rounded.shape[0] // IMGTOK
    c = c_ref[0]

    def step(i, carry):
        dest = place_ref[c * images + i] // per_shard
        slot = count[dest]
        count[dest] = slot + 1
        block = rounded[rows16(i), :]
        sorted_ref[dest, 0, rows16(slot), :] = block

        @pl.when(dest + 1 < shards)
        def _():
            sorted_ref[dest + 1, 1, rows16(slot), :] = block

        return carry

    lax.fori_loop(0, images, step, 0)
    if len(out_refs) == 1:
        out_refs[0][...] = sorted_ref[...]
    else:
        for u, ref in enumerate(out_refs):
            ref[...] = sorted_ref[c ^ u]


def pack(m, c, place, low, high, weights, part, shards, capacity, per_shard, mixed):
    rows, width = part.shape
    feats = low.shape[1]
    whole = lambda a: pl.BlockSpec(a.shape, lambda i, *_: (0,) * len(a.shape))
    shape = (2, capacity, width)
    if mixed:
        out = [jax.ShapeDtypeStruct(shape, jnp.bfloat16)] * shards
    else:
        out = [jax.ShapeDtypeStruct((shards,) + shape, jnp.bfloat16)]
    return pl.pallas_call(
        functools.partial(pack_body, per_shard),
        grid_spec=pltpu.PrefetchScalarGridSpec(
            num_scalar_prefetch=3,
            grid=(1,),
            in_specs=[
                whole(low),
                whole(high),
                pl.BlockSpec((feats, width), lambda i, m, *_: (m[0] ^ 3, 0)),
                whole(part),
            ],
            out_specs=[whole(a) for a in out],
            scratch_shapes=[
                pltpu.VMEM((rows, width), jnp.bfloat16),
                pltpu.VMEM((shards,) + shape, jnp.bfloat16),
                pltpu.SMEM((shards,), jnp.int32),
            ],
        ),
        out_shape=out,
        cost_estimate=cost(2 * rows * feats * width, part.size * 16),
        compiler_params=params(),
    )(m, c, place, low, high, weights, part)


def slices_body(m_ref, c_ref, own_ref, x_ref, y_ref, low_ref, high_ref, kept_ref, *out_refs):
    m = m_ref[0]
    c = c_ref[0]
    sub = out_refs[0].shape[1]
    half = low_ref.shape[0]
    for u, ref in enumerate((kept_ref,) + out_refs):
        at = pl.ds(0, ref.shape[1]) if u == 0 else pl.ds(pl.multiple_of(m * sub, sub), sub)
        which = m ^ c ^ u
        for k, source in enumerate((own_ref, x_ref, y_ref)):

            @pl.when(which == k)
            def _():
                ref[...] = source[:, at]

        @pl.when(which == 3)
        def _():
            ref[:half, :] = low_ref[:, at]
            ref[half:, :] = high_ref[:, at]


def slices(m, c, blocks, sub):
    rows, feats = blocks[0].shape
    smem = pl.BlockSpec(memory_space=pltpu.SMEM)
    vmem = pl.BlockSpec(memory_space=pltpu.VMEM)
    dtype = blocks[0].dtype
    out = [jax.ShapeDtypeStruct((rows, feats), dtype)]
    out += [jax.ShapeDtypeStruct((rows, sub), dtype)] * 3
    return pl.pallas_call(
        slices_body,
        in_specs=[smem, smem] + [vmem] * len(blocks),
        out_specs=[vmem] * len(out),
        out_shape=out,
        cost_estimate=cost(0, rows * feats * 16),
        compiler_params=params(),
    )(m, c, *blocks)


def attention_body(
    per_shard,
    images,
    c_ref,
    place_ref,
    first_ref,
    start_ref,
    q_ref,
    g_ref,
    own_ref,
    prior_ref,
    *refs,
):
    image_refs = refs[:-8]
    out_ref, own_grad_ref, prior_grad_ref, window, probs, grads, total, image_ref = refs[-8:]
    t = pl.program_id(0)
    c = c_ref[0]
    rows = own_ref.shape[0]
    hd = own_ref.shape[1] // 2
    blocks = place_ref.shape[0]
    heads = q_ref.shape[1] // hd
    scale = hd ** (-0.5)

    @pl.when(t == 0)
    def _():
        window[:rows, :] = prior_ref[...]
        window[rows:, :] = own_ref[...]
        total[...] = jnp.zeros_like(total)
        if len(image_refs) == 1:
            image_ref[...] = image_refs[0][...]
        else:
            for u, ref in enumerate(image_refs):
                image_ref[c ^ u] = ref[...]

        def step(b, carry):
            n_own, n_prior = carry
            rank = b // images
            fresh = b % images == 0
            n_own = jnp.where(fresh, 0, n_own)
            n_prior = jnp.where(fresh, 0, n_prior)
            at = place_ref[b] - (c - 1) * per_shard
            is_prior = (at >= 0) & (at < per_shard)
            is_own = (at >= per_shard) & (at < 2 * per_shard)

            @pl.when(is_own)
            def _():
                window[rows16(at), :] = image_ref[rank, 0, rows16(n_own), :]

            @pl.when(is_prior)
            def _():
                window[rows16(at), :] = image_ref[rank, 1, rows16(n_prior), :]

            return n_own + is_own.astype(jnp.int32), n_prior + is_prior.astype(jnp.int32)

        lax.fori_loop(0, blocks, step, (jnp.int32(0), jnp.int32(0)))

    first = t * QTILE

    def stack(ref, a, b):
        return jnp.concatenate([ref[:, h * hd : (h + 1) * hd] for h in range(a, b)], axis=0)

    def tile(span):
        base = pl.multiple_of(first + (full - span), QTILE)
        keys = window[pl.ds(base, span), :hd]
        values = window[pl.ds(base, span), hd:]
        values_t = values.T
        key_pos = lax.broadcasted_iota(jnp.int32, (span, QTILE), 0) + base
        query_pos = lax.broadcasted_iota(jnp.int32, (span, QTILE), 1) + (first + rows)
        allowed = (key_pos <= query_pos) & (key_pos >= start_ref[...])
        bias = jnp.where(allowed, 0.0, -1e30)
        bias = jnp.concatenate([bias, bias], axis=1)

        def products(h):
            query = stack(q_ref, h, h + 2)
            grad = stack(g_ref, h, h + 2)
            return dot(keys, query, NT), dot(values, grad, NT)

        def softmax(h, scores):
            scores = scores * (scale * LOG2E) + bias
            top = jnp.max(scores, axis=0, keepdims=True)
            e = jnp.exp2(scores - top)
            p = e * (1.0 / jnp.sum(e, axis=0, keepdims=True))
            low = p.astype(jnp.bfloat16)
            probs[:span, h * QTILE : (h + 2) * QTILE] = low
            return p, dot(values_t, low, NN)

        def backward(h, p, grad_p, context_t):
            grad_t = stack(g_ref, h, h + 2).astype(jnp.float32).T
            delta = jnp.sum(grad_t * context_t, axis=0, keepdims=True)
            ds = (p * (grad_p - delta)).astype(jnp.bfloat16)
            context = context_t.T.astype(jnp.bfloat16)
            out_ref[:, h * hd : (h + 1) * hd] = context[:QTILE]
            out_ref[:, (h + 1) * hd : (h + 2) * hd] = context[QTILE:]
            grads[:span, h * QTILE : (h + 2) * QTILE] = ds

        pairs = heads // 2
        first_stage, second_stage = {}, {}
        for i in range(pairs + 2):
            if i < pairs:
                first_stage[i] = products(2 * i)
            if 1 <= i <= pairs:
                scores, grad_p = first_stage.pop(i - 1)
                second_stage[i - 1] = (grad_p, *softmax(2 * (i - 1), scores))
            if i >= 2:
                grad_p, p, context_t = second_stage.pop(i - 2)
                backward(2 * (i - 2), p, grad_p, context_t)
        total[pl.ds(base, span), :hd] += dot(grads[:span, :], stack(q_ref, 0, heads), NN)
        total[pl.ds(base, span), hd:] += dot(probs[:span, :], stack(g_ref, 0, heads), NN)

    full = rows + QTILE
    need = full - (first_ref[t] - first)
    below = 0
    for span in sorted({min(b * QTILE, full) for b in SPANS} | {full}):
        lower, below = below, span

        @pl.when((need > lower) & (need <= span))
        def _():
            tile(span)

    @pl.when(t == pl.num_programs(0) - 1)
    def _():
        total[:, :hd] = total[:, :hd] * scale
        prior_grad_ref[...] = jnp.zeros_like(prior_grad_ref)

        def step(b, carry):
            n_own, n_prior = carry
            at = place_ref[b] - (c - 1) * per_shard
            is_prior = (at >= 0) & (at < per_shard)
            is_own = (at >= per_shard) & (at < 2 * per_shard)

            @pl.when(is_own)
            def _():
                own_grad_ref[rows16(n_own), :] = total[rows16(at), :]

            @pl.when(is_prior)
            def _():
                prior_grad_ref[rows16(n_prior), :] = total[rows16(at), :].astype(jnp.bfloat16)

            return n_own + is_own.astype(jnp.int32), n_prior + is_prior.astype(jnp.int32)

        lax.fori_loop(0, blocks, step, (jnp.int32(0), jnp.int32(0)))


def attention(c, place, start, queries, d_out, own, prior, image, images, per_shard, image_rows):
    ranks = len(image) if len(image) > 1 else image[0].shape[0]
    rows, width = own.shape
    cols = queries.shape[1]
    tiles = rows // QTILE
    span = rows + QTILE
    head_rows = cols // (width // 2) * QTILE
    whole = lambda a: pl.BlockSpec(a.shape, lambda t, *_: (0,) * a.ndim)
    tile = pl.BlockSpec((QTILE, cols), lambda t, *_: (t, 0))
    grad = jax.ShapeDtypeStruct((image_rows, width), jnp.float32)
    prior_grad = jax.ShapeDtypeStruct((image_rows, width), jnp.bfloat16)
    return pl.pallas_call(
        functools.partial(attention_body, per_shard, images),
        grid_spec=pltpu.PrefetchScalarGridSpec(
            num_scalar_prefetch=3,
            grid=(tiles,),
            in_specs=[
                pl.BlockSpec((1, QTILE), lambda t, *_: (0, t)),
                tile,
                tile,
                whole(own),
                whole(prior),
                *map(whole, image),
            ],
            out_specs=[tile, whole(grad), whole(grad)],
            scratch_shapes=[
                pltpu.VMEM((2 * rows, width), jnp.bfloat16),
                pltpu.VMEM((span, head_rows), jnp.bfloat16),
                pltpu.VMEM((span, head_rows), jnp.bfloat16),
                pltpu.VMEM((2 * rows, width), jnp.float32),
                pltpu.VMEM((ranks,) + image[0].shape[-3:], jnp.bfloat16),
            ],
        ),
        out_shape=[jax.ShapeDtypeStruct((rows, cols), jnp.bfloat16), grad, prior_grad],
        cost_estimate=cost(4 * 20 * cols * span * rows, 4 * queries.size * 2),
        compiler_params=params(),
    )(c, place, start[0, ::QTILE], start, queries, d_out, own, prior, *image)


def reorder_body(per_shard, images, c_ref, place_ref, *refs):
    grad_refs = refs[:-4]
    out_ref, mine_ref, g_ref, count = refs[-4:]
    shards = g_ref.shape[0]
    if len(grad_refs) == 1:
        g_ref[...] = grad_refs[0][...]
    else:
        for u, ref in enumerate(grad_refs):
            g_ref[c_ref[0] ^ u] = ref[...]
    for s in range(shards):
        count[s] = 0
    c = c_ref[0]

    def step(b, carry):
        dest = place_ref[b] // per_shard
        slot = count[dest]
        count[dest] = slot + 1
        out_ref[rows16(b), :] = g_ref[dest, rows16(slot), :]
        return carry

    lax.fori_loop(0, place_ref.shape[0], step, 0)
    rows = mine_ref.shape[0]
    mine_ref[...] = out_ref[pl.ds(pl.multiple_of(c * rows, IMGTOK), rows), :]


def reorder(c, place, gathered, per_shard, images, shards):
    rows, width = gathered[0].shape[-2:]
    dtype = gathered[0].dtype
    smem = pl.BlockSpec(memory_space=pltpu.SMEM)
    vmem = pl.BlockSpec(memory_space=pltpu.VMEM)
    return pl.pallas_call(
        functools.partial(reorder_body, per_shard, images),
        in_specs=[smem, smem] + [vmem] * len(gathered),
        out_specs=[vmem, vmem],
        out_shape=[
            jax.ShapeDtypeStruct((shards * rows, width), dtype),
            jax.ShapeDtypeStruct((rows, width), dtype),
        ],
        scratch_shapes=[
            pltpu.VMEM((shards, rows, width), dtype),
            pltpu.SMEM((shards,), jnp.int32),
        ],
        cost_estimate=cost(0, shards * rows * width * 8),
        compiler_params=params(),
    )(c, place, *gathered)


def weight_body(s_ref, g_ref, out_ref):
    out_ref[...] = dot(s_ref[0], g_ref[...], TN)


def weight_term(states, grad):
    parts, rows, cols = states.shape
    width = grad.shape[1]
    return pl.pallas_call(
        weight_body,
        grid=(parts,),
        in_specs=[
            pl.BlockSpec((1, rows, cols), lambda k: (k, 0, 0)),
            pl.BlockSpec(grad.shape, lambda k: (0, 0)),
        ],
        out_specs=pl.BlockSpec((cols, width), lambda k: (k, 0)),
        out_shape=jax.ShapeDtypeStruct((parts * cols, width), jnp.float32),
        cost_estimate=cost(2 * states.size * width, states.size * 4),
        compiler_params=params(),
    )(states, grad)


def slice_body(first, groups, m_ref, c_ref, kept_ref, g_ref, *refs):
    out_ref = refs[-1]
    ranks, rows, width = g_ref.shape
    m = m_ref[0]
    c = c_ref[0]
    grad = jnp.concatenate([g_ref[c ^ u] for u in range(1, ranks)], axis=0)
    cols = refs[0].shape[1]
    state_refs = list(refs[:-1])
    for k, count in enumerate(groups):
        at = pl.multiple_of((m ^ (first + k)) * cols, cols)
        total = dot(kept_ref[:, pl.ds(at, cols)], g_ref[c], TN)
        done = 0
        for ref in state_refs[:count]:
            total = total + dot(ref[...], grad[done : done + ref.shape[0]], TN)
            done += ref.shape[0]
        state_refs = state_refs[count:]
        out_ref[k] = total


def slice_terms(first, groups, m, c, kept, grad, states):
    cols = states[0].shape[1]
    width = grad.shape[2]
    smem = pl.BlockSpec(memory_space=pltpu.SMEM)
    vmem = pl.BlockSpec(memory_space=pltpu.VMEM)
    rows = grad.shape[0] * grad.shape[1]
    return pl.pallas_call(
        functools.partial(slice_body, first, groups),
        in_specs=[smem, smem] + [vmem] * (2 + len(states)),
        out_specs=vmem,
        out_shape=jax.ShapeDtypeStruct((len(groups), cols, width), jnp.float32),
        cost_estimate=cost(2 * rows * cols * width * len(groups), rows * cols * len(groups) * 4),
        compiler_params=params(),
    )(m, c, kept, grad, *states)


def settle_body(m_ref, *refs):
    out_ref = refs[-1]
    m = m_ref[0]
    half = (len(refs) - 1) // 2
    k = 0
    for own, other in zip(refs[:half], refs[half:-1]):
        for i in range(own.shape[0]):
            cols = own.shape[1]
            at = pl.ds(pl.multiple_of((m ^ k) * cols, cols), cols)
            out_ref[at, :] = own[i] + other[i]
            k += 1


def settle(m, own, other):
    count = sum(a.shape[0] for a in own)
    _, cols, width = own[0].shape
    vmem = pl.BlockSpec(memory_space=pltpu.VMEM)
    return pl.pallas_call(
        settle_body,
        in_specs=[pl.BlockSpec(memory_space=pltpu.SMEM)] + [vmem] * (2 * len(own)),
        out_specs=vmem,
        out_shape=jax.ShapeDtypeStruct((count * cols, width), jnp.float32),
        cost_estimate=cost(0, count * cols * width * 12),
        compiler_params=params(),
    )(m, *own, *other)


def image_body(d_ref, *refs):
    out_ref = refs[-1]
    heads = (len(refs) - 1) // 3
    grads, near, far = refs[:heads], refs[heads : 2 * heads], refs[2 * heads : -1]
    j = pl.program_id(0)
    cols = near[0].shape[0]
    half = out_ref.shape[1] // 2
    d = d_ref[0]
    for weights, side in ((near, d), (far, 1 - d)):
        total = dot(grads[0][...], weights[0][...], NT)
        for h in range(1, heads):
            total = total + dot(grads[h][...], weights[h][...], NT)
        at = pl.multiple_of(side * half + j * cols, cols)
        out_ref[:, pl.ds(at, cols)] = total.astype(out_ref.dtype)


def image_term(d, grads, near, far):
    heads = len(near)
    half, width = near[0].shape
    rows = grads[0].shape[0]
    tiles = 4
    side = pl.BlockSpec((half // tiles, width), lambda j, d: (j, 0))
    grad = pl.BlockSpec((rows, width), lambda j, d: (0, 0))
    return pl.pallas_call(
        image_body,
        grid_spec=pltpu.PrefetchScalarGridSpec(
            num_scalar_prefetch=1,
            grid=(tiles,),
            in_specs=[grad] * heads + [side] * (2 * heads),
            out_specs=pl.BlockSpec((rows, 2 * half), lambda j, d: (0, 0)),
        ),
        out_shape=jax.ShapeDtypeStruct((rows, 2 * half), jnp.bfloat16),
        cost_estimate=cost(4 * heads * half * width * rows, 4 * heads * half * width * 2),
        compiler_params=params(),
    )(d, *grads, *near, *far)


def per_device(image_states, place_index, doc_ids, queries, text_kv, kv_weight, d_out):
    ranks = lax.axis_size("ctx")
    mps = lax.axis_size("mp")
    c = lax.axis_index("ctx")
    d = lax.axis_index("dp")
    rows = queries.shape[1]
    states = image_states[0]
    image_rows, feats = states.shape
    images = image_rows // IMGTOK
    per_shard = rows // IMGTOK
    capacity = IMGTOK * ((images + ranks - 1) // ranks)
    weights = kv_weight[0]
    width = weights.shape[1]
    c1 = jnp.reshape(c, (1,)).astype(jnp.int32)
    d1 = jnp.reshape(d, (1,)).astype(jnp.int32)
    place = place_index[0, ::IMGTOK] // IMGTOK

    m = lax.axis_index("mp")
    m1 = jnp.reshape(m, (1,)).astype(jnp.int32)
    steps = range(1, mps)
    mixed = ranks == mps

    x = trade(states, "mp", 1)
    y = trade(states, "mp", 2)
    low = trade(x[: image_rows // 2], "mp", 2)
    high = trade(y[image_rows // 2 :], "mp", 1)
    part, *slabs = project(m1, d1, [states, x, y], weights)

    prior_text = shift(text_kv[0], "ctx", 1)
    docs = doc_ids[0]
    own_docs = lax.dynamic_slice_in_dim(docs, c * rows, rows)
    prior_docs = lax.dynamic_slice_in_dim(docs, jnp.maximum(c - 1, 0) * rows, rows)
    prior_docs = jnp.where(c > 0, prior_docs, -1)
    key_docs = jnp.concatenate([prior_docs, own_docs])
    start = jnp.sum((key_docs[:, None] < own_docs[None, :]).astype(jnp.int32), axis=0)[None]
    low, high, prior_text, start, place = lax.optimization_barrier(
        (low, high, prior_text, start, place)
    )
    packed = pack(
        m1, c1, place, low, high, weights, part, ranks, capacity, per_shard, mixed
    )

    *slabs, _ = lax.optimization_barrier((*slabs, packed[0]))
    slabs, own_slabs = slabs[:3], slabs[3:]
    last = trade(slabs[2], "mp", 3)

    if mixed:
        c2, _ = lax.optimization_barrier((c1, packed[0]))
        kept, *moved = slices(m1, c2, [states, x, y, low, high], feats // mps)
        moved[2] = trade(moved[2], "ctx", 3)
        image = [trade(packed[s], "ctx", s) if s else packed[0] for s in range(ranks)]
        moved[0], moved[1], slabs[0], slabs[1], *image = lax.optimization_barrier(
            (moved[0], moved[1], slabs[0], slabs[1], *image)
        )
        moved = [trade(moved[0], "ctx", 1), trade(moved[1], "ctx", 2), moved[2]]
    else:
        image = [exchange(packed[0], "ctx")]
        whole = lax.all_gather(states, "mp", axis=1, tiled=True)
        moved = whole.reshape(image_rows, ranks, mps, -1)
        moved = lax.dynamic_index_in_dim(moved, m, axis=2, keepdims=False).transpose(1, 0, 2)
        moved = [exchange(moved, "ctx").reshape(ranks * image_rows, -1)]
    near = [trade(slabs[0], "mp", 1), trade(slabs[1], "mp", 2), last]

    attn_out, own_grad, prior_grad = attention(
        c1, place, start, queries[0], d_out[0], text_kv[0], prior_text, image,
        images, per_shard, image_rows,
    )
    prior_grad, *both = lax.optimization_barrier((prior_grad, *near, *moved))
    near, moved = both[: len(near)], both[len(near) :]
    far = [own_slabs[1]] + [swap(w, "dp") for w in near]
    grad = own_grad + shift(prior_grad, "ctx", -1).astype(jnp.float32)
    grad = grad.astype(jnp.bfloat16)
    grad, far[1], far[2] = lax.optimization_barrier((grad, far[1], far[2]))
    if mixed:
        gathered = [trade(grad, "ctx", s) if s else grad for s in range(ranks)]
        base = jnp.concatenate(moved, axis=0)
        cut = base.shape[0] // 2
        base_x = trade(base, "mp", 1)
        base_y = trade(base, "mp", 2)
    else:
        gathered = [exchange(jnp.broadcast_to(grad, (ranks,) + grad.shape), "ctx")]
        all_states = lax.all_gather(moved[0], "mp", axis=0)
        base_x = base_y = all_states
    base_x, base_y, *both = lax.optimization_barrier((base_x, base_y, *far, *gathered))
    far, gathered = both[: len(far)], both[len(far) :]
    by_rank, mine = reorder(c1, place, gathered, per_shard, images, ranks)
    head_grad = [mine] + [trade(mine, "mp", s) for s in steps]
    if mixed:
        base_low = trade(base_x[:cut], "mp", 2)
        base_high = trade(base_y[cut:], "mp", 1)
        by_rank, base_low, base_high, *head_grad = lax.optimization_barrier(
            (by_rank, base_low, base_high, *head_grad)
        )
    near = [own_slabs[0]] + list(near)
    image_grad = image_term(d1, head_grad, near, far)
    if mixed:
        by_rank = by_rank.reshape(ranks, image_rows, width)
        terms = [
            slice_terms(0, (1, 1, 1), m1, c1, kept, by_rank, [base, base_x, base_y]),
            slice_terms(3, (2,), m1, c1, kept, by_rank, [base_low, base_high]),
        ]
        weight_grad = settle(m1, terms, [swap(a, "dp") for a in terms])
    else:
        term = weight_term(all_states, by_rank)
        weight_grad = term + swap(term, "dp")
    return (attn_out[None], image_grad[None], weight_grad[None])


def solution(mesh):
    in_specs = (
        P("dp", "ctx", "mp"),
        P("dp", None),
        P("dp", None),
        P("dp", "ctx", "mp"),
        P("dp", "ctx", "mp"),
        P("mp", None, None),
        P("dp", "ctx", "mp"),
    )
    out_specs = (P("dp", "ctx", "mp"), P("dp", "ctx", "mp"), P("mp", "ctx", None))
    return jax.shard_map(
        per_device, mesh=mesh, in_specs=in_specs, out_specs=out_specs, check_vma=False
    )
```

```python
import functools

import jax
import jax.numpy as jnp
from jax import lax
from jax.experimental import pallas as pl
from jax.experimental.pallas import tpu as pltpu
from jax.sharding import PartitionSpec as P

IMGTOK = 16
QTILE = 128
SPANS = (2, 3)
LOG2E = 1.4426950408889634
VMEM = 24 * 1024 * 1024

NN = (((1,), (0,)), ((), ()))
NT = (((1,), (1,)), ((), ()))
TN = (((0,), (0,)), ((), ()))


def dot(a, b, dims):
    return lax.dot_general(a, b, dims, preferred_element_type=jnp.float32)


def params():
    return pltpu.CompilerParams(vmem_limit_bytes=VMEM)


def cost(flops, moved):
    return pl.CostEstimate(flops=int(flops), bytes_accessed=int(moved), transcendentals=0)


def shift(block, axis, distance):
    devices = range(lax.axis_size(axis))
    route = [(i - distance, i) for i in devices if i - distance in devices]
    return lax.ppermute(block, axis, route)


def swap(block, axis):
    count = lax.axis_size(axis)
    return lax.ppermute(block, axis, [(i, count - 1 - i) for i in range(count)])


def exchange(blocks, axis):
    return lax.all_to_all(blocks, axis, split_axis=0, concat_axis=0, tiled=True)


def trade(block, axis, step):
    count = lax.axis_size(axis)
    return lax.ppermute(block, axis, [(i, i ^ step) for i in range(count)])


def rows16(start):
    return pl.ds(pl.multiple_of(start * IMGTOK, IMGTOK), IMGTOK)


def project_body(m_ref, d_ref, own_ref, x_ref, y_ref, weight_ref, out_ref, *slab_refs):
    m = m_ref[0]
    d = d_ref[0]
    feats = own_ref.shape[1]
    half = slab_refs[0].shape[0]

    def rows(k, at, count):
        return pl.ds(pl.multiple_of((m ^ k) * feats + at, half), count)

    total = dot(own_ref[...], weight_ref[rows(0, 0, feats), :], NN)
    for k, ref in ((1, x_ref), (2, y_ref)):
        total = total + dot(ref[...], weight_ref[rows(k, 0, feats), :], NN)
    out_ref[...] = total
    for k, side, ref in zip((1, 2, 3, 0, 0), (d, d, d, d, 1 - d), slab_refs):
        ref[...] = weight_ref[rows(k, side * half, half), :]


def project(m, d, blocks, weights):
    rows, feats = blocks[0].shape
    width = weights.shape[1]
    smem = pl.BlockSpec(memory_space=pltpu.SMEM)
    vmem = pl.BlockSpec(memory_space=pltpu.VMEM)
    slab = jax.ShapeDtypeStruct((feats // 2, width), weights.dtype)
    return pl.pallas_call(
        project_body,
        in_specs=[smem, smem] + [vmem] * 4,
        out_specs=[vmem] * 6,
        out_shape=[jax.ShapeDtypeStruct((rows, width), jnp.float32)] + [slab] * 5,
        cost_estimate=cost(6 * rows * feats * width, 4 * weights.size),
        compiler_params=params(),
    )(m, d, *blocks, weights)


def pack_body(per_shard, m_ref, c_ref, place_ref, low_ref, high_ref, weight_ref, part_ref, *refs):
    out_refs = refs[:-3]
    rounded, sorted_ref, count = refs[-3:]
    shards = sorted_ref.shape[0]
    half = low_ref.shape[0]
    for at, ref in ((0, low_ref), (half, high_ref)):
        term = dot(ref[...], weight_ref[...], NN)
        rounded[at : at + half, :] = (part_ref[at : at + half, :] + term).astype(jnp.bfloat16)
    sorted_ref[...] = jnp.zeros_like(sorted_ref)
    for s in range(shards):
        count[s] = 0
    images = rounded.shape[0] // IMGTOK
    c = c_ref[0]

    def step(i, carry):
        dest = place_ref[c * images + i] // per_shard
        slot = count[dest]
        count[dest] = slot + 1
        block = rounded[rows16(i), :]
        sorted_ref[dest, 0, rows16(slot), :] = block

        @pl.when(dest + 1 < shards)
        def _():
            sorted_ref[dest + 1, 1, rows16(slot), :] = block

        return carry

    lax.fori_loop(0, images, step, 0)
    if len(out_refs) == 1:
        out_refs[0][...] = sorted_ref[...]
    else:
        for u, ref in enumerate(out_refs):
            ref[...] = sorted_ref[c ^ u]


def pack(m, c, place, low, high, weights, part, shards, capacity, per_shard, mixed):
    rows, width = part.shape
    feats = low.shape[1]
    whole = lambda a: pl.BlockSpec(a.shape, lambda i, *_: (0,) * len(a.shape))
    shape = (2, capacity, width)
    if mixed:
        out = [jax.ShapeDtypeStruct(shape, jnp.bfloat16)] * shards
    else:
        out = [jax.ShapeDtypeStruct((shards,) + shape, jnp.bfloat16)]
    return pl.pallas_call(
        functools.partial(pack_body, per_shard),
        grid_spec=pltpu.PrefetchScalarGridSpec(
            num_scalar_prefetch=3,
            grid=(1,),
            in_specs=[
                whole(low),
                whole(high),
                pl.BlockSpec((feats, width), lambda i, m, *_: (m[0] ^ 3, 0)),
                whole(part),
            ],
            out_specs=[whole(a) for a in out],
            scratch_shapes=[
                pltpu.VMEM((rows, width), jnp.bfloat16),
                pltpu.VMEM((shards,) + shape, jnp.bfloat16),
                pltpu.SMEM((shards,), jnp.int32),
            ],
        ),
        out_shape=out,
        cost_estimate=cost(2 * rows * feats * width, part.size * 16),
        compiler_params=params(),
    )(m, c, place, low, high, weights, part)


def slices_body(m_ref, c_ref, own_ref, x_ref, y_ref, low_ref, high_ref, kept_ref, *out_refs):
    m = m_ref[0]
    c = c_ref[0]
    sub = out_refs[0].shape[1]
    half = low_ref.shape[0]
    for u, ref in enumerate((kept_ref,) + out_refs):
        at = pl.ds(0, ref.shape[1]) if u == 0 else pl.ds(pl.multiple_of(m * sub, sub), sub)
        which = m ^ c ^ u
        for k, source in enumerate((own_ref, x_ref, y_ref)):

            @pl.when(which == k)
            def _():
                ref[...] = source[:, at]

        @pl.when(which == 3)
        def _():
            ref[:half, :] = low_ref[:, at]
            ref[half:, :] = high_ref[:, at]


def slices(m, c, blocks, sub):
    rows, feats = blocks[0].shape
    smem = pl.BlockSpec(memory_space=pltpu.SMEM)
    vmem = pl.BlockSpec(memory_space=pltpu.VMEM)
    dtype = blocks[0].dtype
    out = [jax.ShapeDtypeStruct((rows, feats), dtype)]
    out += [jax.ShapeDtypeStruct((rows, sub), dtype)] * 3
    return pl.pallas_call(
        slices_body,
        in_specs=[smem, smem] + [vmem] * len(blocks),
        out_specs=[vmem] * len(out),
        out_shape=out,
        cost_estimate=cost(0, rows * feats * 16),
        compiler_params=params(),
    )(m, c, *blocks)


def attention_body(
    per_shard,
    images,
    c_ref,
    place_ref,
    start_ref,
    q_ref,
    g_ref,
    own_ref,
    prior_ref,
    *refs,
):
    image_refs = refs[:-8]
    out_ref, own_grad_ref, prior_grad_ref, window, probs, grads, total, image_ref = refs[-8:]
    t = pl.program_id(0)
    c = c_ref[0]
    rows = own_ref.shape[0]
    hd = own_ref.shape[1] // 2
    blocks = place_ref.shape[0]
    heads = q_ref.shape[1] // hd
    scale = hd ** (-0.5)

    @pl.when(t == 0)
    def _():
        window[:rows, :] = prior_ref[...]
        window[rows:, :] = own_ref[...]
        total[...] = jnp.zeros_like(total)
        if len(image_refs) == 1:
            image_ref[...] = image_refs[0][...]
        else:
            for u, ref in enumerate(image_refs):
                image_ref[c ^ u] = ref[...]

        def step(b, carry):
            n_own, n_prior = carry
            rank = b // images
            fresh = b % images == 0
            n_own = jnp.where(fresh, 0, n_own)
            n_prior = jnp.where(fresh, 0, n_prior)
            at = place_ref[b] - (c - 1) * per_shard
            is_prior = (at >= 0) & (at < per_shard)
            is_own = (at >= per_shard) & (at < 2 * per_shard)

            @pl.when(is_own)
            def _():
                window[rows16(at), :] = image_ref[rank, 0, rows16(n_own), :]

            @pl.when(is_prior)
            def _():
                window[rows16(at), :] = image_ref[rank, 1, rows16(n_prior), :]

            return n_own + is_own.astype(jnp.int32), n_prior + is_prior.astype(jnp.int32)

        lax.fori_loop(0, blocks, step, (jnp.int32(0), jnp.int32(0)))

    first = t * QTILE

    def stack(ref, a, b):
        return jnp.concatenate([ref[:, h * hd : (h + 1) * hd] for h in range(a, b)], axis=0)

    def tile(span):
        base = pl.multiple_of(first + (full - span), QTILE)
        keys = window[pl.ds(base, span), :hd]
        values = window[pl.ds(base, span), hd:]
        values_t = values.T
        key_pos = lax.broadcasted_iota(jnp.int32, (span, QTILE), 0) + base
        query_pos = lax.broadcasted_iota(jnp.int32, (span, QTILE), 1) + (first + rows)
        allowed = (key_pos <= query_pos) & (key_pos >= start_ref[...])
        bias = jnp.where(allowed, 0.0, -1e30)
        bias = jnp.concatenate([bias, bias], axis=1)

        def products(h):
            query = stack(q_ref, h, h + 2)
            grad = stack(g_ref, h, h + 2)
            return dot(keys, query, NT), dot(values, grad, NT)

        def softmax(h, scores):
            scores = scores * (scale * LOG2E) + bias
            top = jnp.max(scores, axis=0, keepdims=True)
            e = jnp.exp2(scores - top)
            p = e * (1.0 / jnp.sum(e, axis=0, keepdims=True))
            low = p.astype(jnp.bfloat16)
            probs[:span, h * QTILE : (h + 2) * QTILE] = low
            return p, dot(values_t, low, NN)

        def backward(h, p, grad_p, context_t):
            grad_t = stack(g_ref, h, h + 2).astype(jnp.float32).T
            delta = jnp.sum(grad_t * context_t, axis=0, keepdims=True)
            ds = (p * (grad_p - delta)).astype(jnp.bfloat16)
            context = context_t.T.astype(jnp.bfloat16)
            out_ref[:, h * hd : (h + 1) * hd] = context[:QTILE]
            out_ref[:, (h + 1) * hd : (h + 2) * hd] = context[QTILE:]
            grads[:span, h * QTILE : (h + 2) * QTILE] = ds

        pairs = heads // 2
        first_stage, second_stage = {}, {}
        for i in range(pairs + 2):
            if i < pairs:
                first_stage[i] = products(2 * i)
            if 1 <= i <= pairs:
                scores, grad_p = first_stage.pop(i - 1)
                second_stage[i - 1] = (grad_p, *softmax(2 * (i - 1), scores))
            if i >= 2:
                grad_p, p, context_t = second_stage.pop(i - 2)
                backward(2 * (i - 2), p, grad_p, context_t)
        total[pl.ds(base, span), :hd] += dot(grads[:span, :], stack(q_ref, 0, heads), NN)
        total[pl.ds(base, span), hd:] += dot(probs[:span, :], stack(g_ref, 0, heads), NN)

    full = rows + QTILE
    need = full - (jnp.min(start_ref[...]) - first)
    below = 0
    for span in sorted({min(b * QTILE, full) for b in SPANS} | {full}):
        lower, below = below, span

        @pl.when((need > lower) & (need <= span))
        def _():
            tile(span)

    @pl.when(t == pl.num_programs(0) - 1)
    def _():
        total[:, :hd] = total[:, :hd] * scale
        prior_grad_ref[...] = jnp.zeros_like(prior_grad_ref)

        def step(b, carry):
            n_own, n_prior = carry
            at = place_ref[b] - (c - 1) * per_shard
            is_prior = (at >= 0) & (at < per_shard)
            is_own = (at >= per_shard) & (at < 2 * per_shard)

            @pl.when(is_own)
            def _():
                own_grad_ref[rows16(n_own), :] = total[rows16(at), :]

            @pl.when(is_prior)
            def _():
                prior_grad_ref[rows16(n_prior), :] = total[rows16(at), :].astype(jnp.bfloat16)

            return n_own + is_own.astype(jnp.int32), n_prior + is_prior.astype(jnp.int32)

        lax.fori_loop(0, blocks, step, (jnp.int32(0), jnp.int32(0)))


def attention(c, place, start, queries, d_out, own, prior, image, images, per_shard, image_rows):
    ranks = len(image) if len(image) > 1 else image[0].shape[0]
    rows, width = own.shape
    cols = queries.shape[1]
    tiles = rows // QTILE
    span = rows + QTILE
    head_rows = cols // (width // 2) * QTILE
    whole = lambda a: pl.BlockSpec(a.shape, lambda t, *_: (0,) * a.ndim)
    tile = pl.BlockSpec((QTILE, cols), lambda t, *_: (t, 0))
    grad = jax.ShapeDtypeStruct((image_rows, width), jnp.float32)
    prior_grad = jax.ShapeDtypeStruct((image_rows, width), jnp.bfloat16)
    return pl.pallas_call(
        functools.partial(attention_body, per_shard, images),
        grid_spec=pltpu.PrefetchScalarGridSpec(
            num_scalar_prefetch=2,
            grid=(tiles,),
            in_specs=[
                pl.BlockSpec((1, QTILE), lambda t, *_: (0, t)),
                tile,
                tile,
                whole(own),
                whole(prior),
                *map(whole, image),
            ],
            out_specs=[tile, whole(grad), whole(grad)],
            scratch_shapes=[
                pltpu.VMEM((2 * rows, width), jnp.bfloat16),
                pltpu.VMEM((span, head_rows), jnp.bfloat16),
                pltpu.VMEM((span, head_rows), jnp.bfloat16),
                pltpu.VMEM((2 * rows, width), jnp.float32),
                pltpu.VMEM((ranks,) + image[0].shape[-3:], jnp.bfloat16),
            ],
        ),
        out_shape=[jax.ShapeDtypeStruct((rows, cols), jnp.bfloat16), grad, prior_grad],
        cost_estimate=cost(2 * 20 * cols * span * rows, 4 * queries.size * 2),
        compiler_params=params(),
    )(c, place, start, queries, d_out, own, prior, *image)


def reorder_body(per_shard, images, c_ref, place_ref, *refs):
    grad_refs = refs[:-4]
    out_ref, mine_ref, g_ref, count = refs[-4:]
    shards = g_ref.shape[0]
    if len(grad_refs) == 1:
        g_ref[...] = grad_refs[0][...]
    else:
        for u, ref in enumerate(grad_refs):
            g_ref[c_ref[0] ^ u] = ref[...]
    for s in range(shards):
        count[s] = 0
    c = c_ref[0]

    def step(b, carry):
        dest = place_ref[b] // per_shard
        slot = count[dest]
        count[dest] = slot + 1
        out_ref[rows16(b), :] = g_ref[dest, rows16(slot), :]
        return carry

    lax.fori_loop(0, place_ref.shape[0], step, 0)
    rows = mine_ref.shape[0]
    mine_ref[...] = out_ref[pl.ds(pl.multiple_of(c * rows, IMGTOK), rows), :]


def reorder(c, place, gathered, per_shard, images, shards):
    rows, width = gathered[0].shape[-2:]
    dtype = gathered[0].dtype
    smem = pl.BlockSpec(memory_space=pltpu.SMEM)
    vmem = pl.BlockSpec(memory_space=pltpu.VMEM)
    return pl.pallas_call(
        functools.partial(reorder_body, per_shard, images),
        in_specs=[smem, smem] + [vmem] * len(gathered),
        out_specs=[vmem, vmem],
        out_shape=[
            jax.ShapeDtypeStruct((shards * rows, width), dtype),
            jax.ShapeDtypeStruct((rows, width), dtype),
        ],
        scratch_shapes=[
            pltpu.VMEM((shards, rows, width), dtype),
            pltpu.SMEM((shards,), jnp.int32),
        ],
        cost_estimate=cost(0, shards * rows * width * 8),
        compiler_params=params(),
    )(c, place, *gathered)


def weight_body(s_ref, g_ref, out_ref):
    out_ref[...] = dot(s_ref[0], g_ref[...], TN)


def weight_term(states, grad):
    parts, rows, cols = states.shape
    width = grad.shape[1]
    return pl.pallas_call(
        weight_body,
        grid=(parts,),
        in_specs=[
            pl.BlockSpec((1, rows, cols), lambda k: (k, 0, 0)),
            pl.BlockSpec(grad.shape, lambda k: (0, 0)),
        ],
        out_specs=pl.BlockSpec((cols, width), lambda k: (k, 0)),
        out_shape=jax.ShapeDtypeStruct((parts * cols, width), jnp.float32),
        cost_estimate=cost(2 * states.size * width, states.size * 4),
        compiler_params=params(),
    )(states, grad)


def slice_body(first, groups, m_ref, c_ref, kept_ref, g_ref, *refs):
    out_ref = refs[-1]
    ranks, rows, width = g_ref.shape
    m = m_ref[0]
    c = c_ref[0]
    grad = jnp.concatenate([g_ref[c ^ u] for u in range(1, ranks)], axis=0)
    cols = refs[0].shape[1]
    state_refs = list(refs[:-1])
    for k, count in enumerate(groups):
        at = pl.multiple_of((m ^ (first + k)) * cols, cols)
        total = dot(kept_ref[:, pl.ds(at, cols)], g_ref[c], TN)
        done = 0
        for ref in state_refs[:count]:
            total = total + dot(ref[...], grad[done : done + ref.shape[0]], TN)
            done += ref.shape[0]
        state_refs = state_refs[count:]
        out_ref[k] = total


def slice_terms(first, groups, m, c, kept, grad, states):
    cols = states[0].shape[1]
    width = grad.shape[2]
    smem = pl.BlockSpec(memory_space=pltpu.SMEM)
    vmem = pl.BlockSpec(memory_space=pltpu.VMEM)
    rows = grad.shape[0] * grad.shape[1]
    return pl.pallas_call(
        functools.partial(slice_body, first, groups),
        in_specs=[smem, smem] + [vmem] * (2 + len(states)),
        out_specs=vmem,
        out_shape=jax.ShapeDtypeStruct((len(groups), cols, width), jnp.float32),
        cost_estimate=cost(2 * rows * cols * width * len(groups), rows * cols * len(groups) * 4),
        compiler_params=params(),
    )(m, c, kept, grad, *states)


def settle_body(m_ref, *refs):
    out_ref = refs[-1]
    m = m_ref[0]
    half = (len(refs) - 1) // 2
    k = 0
    for own, other in zip(refs[:half], refs[half:-1]):
        for i in range(own.shape[0]):
            cols = own.shape[1]
            at = pl.ds(pl.multiple_of((m ^ k) * cols, cols), cols)
            out_ref[at, :] = own[i] + other[i]
            k += 1


def settle(m, own, other):
    count = sum(a.shape[0] for a in own)
    _, cols, width = own[0].shape
    vmem = pl.BlockSpec(memory_space=pltpu.VMEM)
    return pl.pallas_call(
        settle_body,
        in_specs=[pl.BlockSpec(memory_space=pltpu.SMEM)] + [vmem] * (2 * len(own)),
        out_specs=vmem,
        out_shape=jax.ShapeDtypeStruct((count * cols, width), jnp.float32),
        cost_estimate=cost(0, count * cols * width * 12),
        compiler_params=params(),
    )(m, *own, *other)


def image_body(d_ref, *refs):
    out_ref = refs[-1]
    heads = (len(refs) - 1) // 3
    grads, near, far = refs[:heads], refs[heads : 2 * heads], refs[2 * heads : -1]
    j = pl.program_id(0)
    cols = near[0].shape[0]
    half = out_ref.shape[1] // 2
    d = d_ref[0]
    for weights, side in ((near, d), (far, 1 - d)):
        total = dot(grads[0][...], weights[0][...], NT)
        for h in range(1, heads):
            total = total + dot(grads[h][...], weights[h][...], NT)
        at = pl.multiple_of(side * half + j * cols, cols)
        out_ref[:, pl.ds(at, cols)] = total.astype(out_ref.dtype)


def image_term(d, grads, near, far):
    heads = len(near)
    half, width = near[0].shape
    rows = grads[0].shape[0]
    tiles = 4
    side = pl.BlockSpec((half // tiles, width), lambda j, d: (j, 0))
    grad = pl.BlockSpec((rows, width), lambda j, d: (0, 0))
    return pl.pallas_call(
        image_body,
        grid_spec=pltpu.PrefetchScalarGridSpec(
            num_scalar_prefetch=1,
            grid=(tiles,),
            in_specs=[grad] * heads + [side] * (2 * heads),
            out_specs=pl.BlockSpec((rows, 2 * half), lambda j, d: (0, 0)),
        ),
        out_shape=jax.ShapeDtypeStruct((rows, 2 * half), jnp.bfloat16),
        cost_estimate=cost(4 * heads * half * width * rows, 4 * heads * half * width * 2),
        compiler_params=params(),
    )(d, *grads, *near, *far)


def per_device(image_states, place_index, doc_ids, queries, text_kv, kv_weight, d_out):
    ranks = lax.axis_size("ctx")
    mps = lax.axis_size("mp")
    c = lax.axis_index("ctx")
    d = lax.axis_index("dp")
    rows = queries.shape[1]
    states = image_states[0]
    image_rows, feats = states.shape
    images = image_rows // IMGTOK
    per_shard = rows // IMGTOK
    capacity = IMGTOK * ((images + ranks - 1) // ranks)
    weights = kv_weight[0]
    width = weights.shape[1]
    c1 = jnp.reshape(c, (1,)).astype(jnp.int32)
    d1 = jnp.reshape(d, (1,)).astype(jnp.int32)
    place = place_index[0, ::IMGTOK] // IMGTOK

    m = lax.axis_index("mp")
    m1 = jnp.reshape(m, (1,)).astype(jnp.int32)
    steps = range(1, mps)
    mixed = ranks == mps

    x = trade(states, "mp", 1)
    y = trade(states, "mp", 2)
    low = trade(x[: image_rows // 2], "mp", 2)
    high = trade(y[image_rows // 2 :], "mp", 1)
    part, *slabs = project(m1, d1, [states, x, y], weights)

    prior_text = shift(text_kv[0], "ctx", 1)
    docs = doc_ids[0]
    own_docs = lax.dynamic_slice_in_dim(docs, c * rows, rows)
    prior_docs = lax.dynamic_slice_in_dim(docs, jnp.maximum(c - 1, 0) * rows, rows)
    prior_docs = jnp.where(c > 0, prior_docs, -1)
    key_docs = jnp.concatenate([prior_docs, own_docs])
    start = jnp.sum((key_docs[:, None] < own_docs[None, :]).astype(jnp.int32), axis=0)[None]
    low, high, prior_text, start, place = lax.optimization_barrier(
        (low, high, prior_text, start, place)
    )
    packed = pack(
        m1, c1, place, low, high, weights, part, ranks, capacity, per_shard, mixed
    )

    *slabs, _ = lax.optimization_barrier((*slabs, packed[0]))
    slabs, own_slabs = slabs[:3], slabs[3:]
    near = [trade(slabs[0], "mp", 1), None, trade(slabs[2], "mp", 3)]

    if mixed:
        c2, _ = lax.optimization_barrier((c1, packed[0]))
        kept, *moved = slices(m1, c2, [states, x, y, low, high], feats // mps)
        image = [trade(packed[s], "ctx", s) if s else packed[0] for s in range(ranks)]
        both = lax.optimization_barrier((*moved, *image))
        moved, image = both[: len(moved)], both[len(moved) :]
        moved = [trade(moved[s - 1], "ctx", s) for s in range(1, ranks)]
    else:
        image = [exchange(packed[0], "ctx")]
        whole = lax.all_gather(states, "mp", axis=1, tiled=True)
        moved = whole.reshape(image_rows, ranks, mps, -1)
        moved = lax.dynamic_index_in_dim(moved, m, axis=2, keepdims=False).transpose(1, 0, 2)
        moved = [exchange(moved, "ctx").reshape(ranks * image_rows, -1)]

    attn_out, own_grad, prior_grad = attention(
        c1, place, start, queries[0], d_out[0], text_kv[0], prior_text, image,
        images, per_shard, image_rows,
    )
    early = ranks // 2 if mixed else 1
    prior_grad, slabs[1], near[0], near[2], *both = lax.optimization_barrier(
        (prior_grad, slabs[1], near[0], near[2], *moved[:early])
    )
    moved = both + list(moved[early:])
    near[1] = trade(slabs[1], "mp", 2)
    far = [own_slabs[1], swap(near[0], "dp"), None, swap(near[2], "dp")]
    grad = own_grad + shift(prior_grad, "ctx", -1).astype(jnp.float32)
    grad = grad.astype(jnp.bfloat16)
    grad, far[1], far[3] = lax.optimization_barrier((grad, far[1], far[3]))
    if mixed:
        gathered = [trade(grad, "ctx", s) if s else grad for s in range(ranks)]
        base = jnp.concatenate(moved, axis=0)
        cut = base.shape[0] // 2
        base_x = trade(base, "mp", 1)
        base_y = trade(base, "mp", 2)
    else:
        gathered = [exchange(jnp.broadcast_to(grad, (ranks,) + grad.shape), "ctx")]
        all_states = lax.all_gather(moved[0], "mp", axis=0)
    near[1], *gathered = lax.optimization_barrier((near[1], *gathered))
    far[2] = swap(near[1], "dp")
    by_rank, mine = reorder(c1, place, gathered, per_shard, images, ranks)
    head_grad = [mine] + [trade(mine, "mp", s) for s in steps]
    if mixed:
        base_low = trade(base_x[:cut], "mp", 2)
        base_high = trade(base_y[cut:], "mp", 1)
        by_rank, base_low, base_high, far[2], *head_grad = lax.optimization_barrier(
            (by_rank, base_low, base_high, far[2], *head_grad)
        )
    near = [own_slabs[0]] + list(near)
    image_grad = image_term(d1, head_grad, near, far)
    if mixed:
        by_rank = by_rank.reshape(ranks, image_rows, width)
        terms = [
            slice_terms(0, (1, 1, 1), m1, c1, kept, by_rank, [base, base_x, base_y]),
            slice_terms(3, (2,), m1, c1, kept, by_rank, [base_low, base_high]),
        ]
        weight_grad = settle(m1, terms, [swap(a, "dp") for a in terms])
    else:
        term = weight_term(all_states, by_rank)
        weight_grad = term + swap(term, "dp")
    return (attn_out[None], image_grad[None], weight_grad[None])


def solution(mesh):
    in_specs = (
        P("dp", "ctx", "mp"),
        P("dp", None),
        P("dp", None),
        P("dp", "ctx", "mp"),
        P("dp", "ctx", "mp"),
        P("mp", None, None),
        P("dp", "ctx", "mp"),
    )
    out_specs = (P("dp", "ctx", "mp"), P("dp", "ctx", "mp"), P("mp", "ctx", None))
    return jax.shard_map(
        per_device, mesh=mesh, in_specs=in_specs, out_specs=out_specs, check_vma=False
    )
```

```python
import functools

import jax
import jax.numpy as jnp
from jax import lax
from jax.experimental import pallas as pl
from jax.experimental.pallas import tpu as pltpu
from jax.sharding import PartitionSpec as P

IMGTOK = 16
QTILE = 128
SPANS = (2, 3)
LOG2E = 1.4426950408889634
VMEM = 24 * 1024 * 1024

NN = (((1,), (0,)), ((), ()))
NT = (((1,), (1,)), ((), ()))
TN = (((0,), (0,)), ((), ()))


def dot(a, b, dims):
    return lax.dot_general(a, b, dims, preferred_element_type=jnp.float32)


def params():
    return pltpu.CompilerParams(vmem_limit_bytes=VMEM)


def cost(flops, moved):
    return pl.CostEstimate(flops=int(flops), bytes_accessed=int(moved), transcendentals=0)


def shift(block, axis, distance):
    devices = range(lax.axis_size(axis))
    route = [(i - distance, i) for i in devices if i - distance in devices]
    return lax.ppermute(block, axis, route)


def swap(block, axis):
    count = lax.axis_size(axis)
    return lax.ppermute(block, axis, [(i, count - 1 - i) for i in range(count)])


def exchange(blocks, axis):
    return lax.all_to_all(blocks, axis, split_axis=0, concat_axis=0, tiled=True)


def trade(block, axis, step):
    count = lax.axis_size(axis)
    return lax.ppermute(block, axis, [(i, i ^ step) for i in range(count)])


def rows16(start):
    return pl.ds(pl.multiple_of(start * IMGTOK, IMGTOK), IMGTOK)


def project_body(m_ref, d_ref, own_ref, x_ref, y_ref, weight_ref, out_ref, *slab_refs):
    m = m_ref[0]
    d = d_ref[0]
    feats = own_ref.shape[1]
    half = slab_refs[0].shape[0]

    def rows(k, at, count):
        return pl.ds(pl.multiple_of((m ^ k) * feats + at, half), count)

    total = dot(own_ref[...], weight_ref[rows(0, 0, feats), :], NN)
    for k, ref in ((1, x_ref), (2, y_ref)):
        total = total + dot(ref[...], weight_ref[rows(k, 0, feats), :], NN)
    out_ref[...] = total
    for k, side, ref in zip((1, 2, 3, 0, 0), (d, d, d, d, 1 - d), slab_refs):
        ref[...] = weight_ref[rows(k, side * half, half), :]


def project(m, d, blocks, weights):
    rows, feats = blocks[0].shape
    width = weights.shape[1]
    smem = pl.BlockSpec(memory_space=pltpu.SMEM)
    vmem = pl.BlockSpec(memory_space=pltpu.VMEM)
    slab = jax.ShapeDtypeStruct((feats // 2, width), weights.dtype)
    return pl.pallas_call(
        project_body,
        in_specs=[smem, smem] + [vmem] * 4,
        out_specs=[vmem] * 6,
        out_shape=[jax.ShapeDtypeStruct((rows, width), jnp.float32)] + [slab] * 5,
        cost_estimate=cost(6 * rows * feats * width, 4 * weights.size),
        compiler_params=params(),
    )(m, d, *blocks, weights)


def pack_body(per_shard, m_ref, c_ref, place_ref, low_ref, high_ref, weight_ref, part_ref, *refs):
    out_refs = refs[:-3]
    rounded, sorted_ref, count = refs[-3:]
    shards = sorted_ref.shape[0]
    half = low_ref.shape[0]
    for at, ref in ((0, low_ref), (half, high_ref)):
        term = dot(ref[...], weight_ref[...], NN)
        rounded[at : at + half, :] = (part_ref[at : at + half, :] + term).astype(jnp.bfloat16)
    sorted_ref[...] = jnp.zeros_like(sorted_ref)
    for s in range(shards):
        count[s] = 0
    images = rounded.shape[0] // IMGTOK
    c = c_ref[0]

    def step(i, carry):
        dest = place_ref[c * images + i] // per_shard
        slot = count[dest]
        count[dest] = slot + 1
        block = rounded[rows16(i), :]
        sorted_ref[dest, 0, rows16(slot), :] = block

        @pl.when(dest + 1 < shards)
        def _():
            sorted_ref[dest + 1, 1, rows16(slot), :] = block

        return carry

    lax.fori_loop(0, images, step, 0)
    if len(out_refs) == 1:
        out_refs[0][...] = sorted_ref[...]
    else:
        for u, ref in enumerate(out_refs):
            ref[...] = sorted_ref[c ^ u]


def pack(m, c, place, low, high, weights, part, shards, capacity, per_shard, mixed):
    rows, width = part.shape
    feats = low.shape[1]
    whole = lambda a: pl.BlockSpec(a.shape, lambda i, *_: (0,) * len(a.shape))
    shape = (2, capacity, width)
    if mixed:
        out = [jax.ShapeDtypeStruct(shape, jnp.bfloat16)] * shards
    else:
        out = [jax.ShapeDtypeStruct((shards,) + shape, jnp.bfloat16)]
    return pl.pallas_call(
        functools.partial(pack_body, per_shard),
        grid_spec=pltpu.PrefetchScalarGridSpec(
            num_scalar_prefetch=3,
            grid=(1,),
            in_specs=[
                whole(low),
                whole(high),
                pl.BlockSpec((feats, width), lambda i, m, *_: (m[0] ^ 3, 0)),
                whole(part),
            ],
            out_specs=[whole(a) for a in out],
            scratch_shapes=[
                pltpu.VMEM((rows, width), jnp.bfloat16),
                pltpu.VMEM((shards,) + shape, jnp.bfloat16),
                pltpu.SMEM((shards,), jnp.int32),
            ],
        ),
        out_shape=out,
        cost_estimate=cost(2 * rows * feats * width, part.size * 16),
        compiler_params=params(),
    )(m, c, place, low, high, weights, part)


def slices_body(m_ref, c_ref, own_ref, x_ref, y_ref, low_ref, high_ref, kept_ref, *out_refs):
    m = m_ref[0]
    c = c_ref[0]
    sub = out_refs[0].shape[1]
    half = low_ref.shape[0]
    for u, ref in enumerate((kept_ref,) + out_refs):
        at = pl.ds(0, ref.shape[1]) if u == 0 else pl.ds(pl.multiple_of(m * sub, sub), sub)
        which = m ^ c ^ u
        for k, source in enumerate((own_ref, x_ref, y_ref)):

            @pl.when(which == k)
            def _():
                ref[...] = source[:, at]

        @pl.when(which == 3)
        def _():
            ref[:half, :] = low_ref[:, at]
            ref[half:, :] = high_ref[:, at]


def slices(m, c, blocks, sub):
    rows, feats = blocks[0].shape
    smem = pl.BlockSpec(memory_space=pltpu.SMEM)
    vmem = pl.BlockSpec(memory_space=pltpu.VMEM)
    dtype = blocks[0].dtype
    out = [jax.ShapeDtypeStruct((rows, feats), dtype)]
    out += [jax.ShapeDtypeStruct((rows, sub), dtype)] * 3
    return pl.pallas_call(
        slices_body,
        in_specs=[smem, smem] + [vmem] * len(blocks),
        out_specs=[vmem] * len(out),
        out_shape=out,
        cost_estimate=cost(0, rows * feats * 16),
        compiler_params=params(),
    )(m, c, *blocks)


def attention_body(
    per_shard,
    images,
    c_ref,
    place_ref,
    start_ref,
    q_ref,
    g_ref,
    own_ref,
    prior_ref,
    *refs,
):
    image_refs = refs[:-8]
    out_ref, own_grad_ref, prior_grad_ref, window, probs, grads, total, image_ref = refs[-8:]
    t = pl.program_id(0)
    c = c_ref[0]
    rows = own_ref.shape[0]
    hd = own_ref.shape[1] // 2
    blocks = place_ref.shape[0]
    heads = q_ref.shape[1] // hd
    scale = hd ** (-0.5)

    @pl.when(t == 0)
    def _():
        window[:rows, :] = prior_ref[...]
        window[rows:, :] = own_ref[...]
        total[...] = jnp.zeros_like(total)
        if len(image_refs) == 1:
            image_ref[...] = image_refs[0][...]
        else:
            for u, ref in enumerate(image_refs):
                image_ref[c ^ u] = ref[...]

        def step(b, carry):
            n_own, n_prior = carry
            rank = b // images
            fresh = b % images == 0
            n_own = jnp.where(fresh, 0, n_own)
            n_prior = jnp.where(fresh, 0, n_prior)
            at = place_ref[b] - (c - 1) * per_shard
            is_prior = (at >= 0) & (at < per_shard)
            is_own = (at >= per_shard) & (at < 2 * per_shard)

            @pl.when(is_own)
            def _():
                window[rows16(at), :] = image_ref[rank, 0, rows16(n_own), :]

            @pl.when(is_prior)
            def _():
                window[rows16(at), :] = image_ref[rank, 1, rows16(n_prior), :]

            return n_own + is_own.astype(jnp.int32), n_prior + is_prior.astype(jnp.int32)

        lax.fori_loop(0, blocks, step, (jnp.int32(0), jnp.int32(0)))

    first = t * QTILE

    def stack(ref, a, b):
        return jnp.concatenate([ref[:, h * hd : (h + 1) * hd] for h in range(a, b)], axis=0)

    def tile(span):
        base = pl.multiple_of(first + (full - span), QTILE)
        keys = window[pl.ds(base, span), :hd]
        values = window[pl.ds(base, span), hd:]
        values_t = values.T
        key_pos = lax.broadcasted_iota(jnp.int32, (span, QTILE), 0) + base
        query_pos = lax.broadcasted_iota(jnp.int32, (span, QTILE), 1) + (first + rows)
        allowed = (key_pos <= query_pos) & (key_pos >= start_ref[...])
        bias = jnp.where(allowed, 0.0, -1e30)
        bias = jnp.concatenate([bias, bias], axis=1)

        def products(h):
            query = stack(q_ref, h, h + 2)
            grad = stack(g_ref, h, h + 2)
            return dot(keys, query, NT), dot(values, grad, NT)

        def softmax(h, scores):
            scores = scores * (scale * LOG2E) + bias
            top = jnp.max(scores, axis=0, keepdims=True)
            e = jnp.exp2(scores - top)
            p = e * (1.0 / jnp.sum(e, axis=0, keepdims=True))
            low = p.astype(jnp.bfloat16)
            probs[:span, h * QTILE : (h + 2) * QTILE] = low
            return p, dot(values_t, low, NN)

        def backward(h, p, grad_p, context_t):
            grad_t = stack(g_ref, h, h + 2).astype(jnp.float32).T
            delta = jnp.sum(grad_t * context_t, axis=0, keepdims=True)
            ds = (p * (grad_p - delta)).astype(jnp.bfloat16)
            context = context_t.T.astype(jnp.bfloat16)
            out_ref[:, h * hd : (h + 1) * hd] = context[:QTILE]
            out_ref[:, (h + 1) * hd : (h + 2) * hd] = context[QTILE:]
            grads[:span, h * QTILE : (h + 2) * QTILE] = ds

        pairs = heads // 2
        first_stage, second_stage = {}, {}
        for i in range(pairs + 2):
            if i < pairs:
                first_stage[i] = products(2 * i)
            if 1 <= i <= pairs:
                scores, grad_p = first_stage.pop(i - 1)
                second_stage[i - 1] = (grad_p, *softmax(2 * (i - 1), scores))
            if i >= 2:
                grad_p, p, context_t = second_stage.pop(i - 2)
                backward(2 * (i - 2), p, grad_p, context_t)
        total[pl.ds(base, span), :hd] += dot(grads[:span, :], stack(q_ref, 0, heads), NN)
        total[pl.ds(base, span), hd:] += dot(probs[:span, :], stack(g_ref, 0, heads), NN)

    full = rows + QTILE
    need = full - (jnp.min(start_ref[...]) - first)
    below = 0
    for span in sorted({min(b * QTILE, full) for b in SPANS} | {full}):
        lower, below = below, span

        @pl.when((need > lower) & (need <= span))
        def _():
            tile(span)

    @pl.when(t == pl.num_programs(0) - 1)
    def _():
        total[:, :hd] = total[:, :hd] * scale
        prior_grad_ref[...] = jnp.zeros_like(prior_grad_ref)

        def step(b, carry):
            n_own, n_prior = carry
            at = place_ref[b] - (c - 1) * per_shard
            is_prior = (at >= 0) & (at < per_shard)
            is_own = (at >= per_shard) & (at < 2 * per_shard)

            @pl.when(is_own)
            def _():
                own_grad_ref[rows16(n_own), :] = total[rows16(at), :]

            @pl.when(is_prior)
            def _():
                prior_grad_ref[rows16(n_prior), :] = total[rows16(at), :].astype(jnp.bfloat16)

            return n_own + is_own.astype(jnp.int32), n_prior + is_prior.astype(jnp.int32)

        lax.fori_loop(0, blocks, step, (jnp.int32(0), jnp.int32(0)))


def attention(c, place, start, queries, d_out, own, prior, image, images, per_shard, image_rows):
    ranks = len(image) if len(image) > 1 else image[0].shape[0]
    rows, width = own.shape
    cols = queries.shape[1]
    tiles = rows // QTILE
    span = rows + QTILE
    head_rows = cols // (width // 2) * QTILE
    whole = lambda a: pl.BlockSpec(a.shape, lambda t, *_: (0,) * a.ndim)
    tile = pl.BlockSpec((QTILE, cols), lambda t, *_: (t, 0))
    grad = jax.ShapeDtypeStruct((image_rows, width), jnp.float32)
    prior_grad = jax.ShapeDtypeStruct((image_rows, width), jnp.bfloat16)
    return pl.pallas_call(
        functools.partial(attention_body, per_shard, images),
        grid_spec=pltpu.PrefetchScalarGridSpec(
            num_scalar_prefetch=2,
            grid=(tiles,),
            in_specs=[
                pl.BlockSpec((1, QTILE), lambda t, *_: (0, t)),
                tile,
                tile,
                whole(own),
                whole(prior),
                *map(whole, image),
            ],
            out_specs=[tile, whole(grad), whole(grad)],
            scratch_shapes=[
                pltpu.VMEM((2 * rows, width), jnp.bfloat16),
                pltpu.VMEM((span, head_rows), jnp.bfloat16),
                pltpu.VMEM((span, head_rows), jnp.bfloat16),
                pltpu.VMEM((2 * rows, width), jnp.float32),
                pltpu.VMEM((ranks,) + image[0].shape[-3:], jnp.bfloat16),
            ],
        ),
        out_shape=[jax.ShapeDtypeStruct((rows, cols), jnp.bfloat16), grad, prior_grad],
        cost_estimate=cost(2 * 20 * cols * span * rows, 4 * queries.size * 2),
        compiler_params=params(),
    )(c, place, start, queries, d_out, own, prior, *image)


def reorder_body(per_shard, images, c_ref, place_ref, *refs):
    grad_refs = refs[:-4]
    out_ref, mine_ref, g_ref, count = refs[-4:]
    shards = g_ref.shape[0]
    if len(grad_refs) == 1:
        g_ref[...] = grad_refs[0][...]
    else:
        for u, ref in enumerate(grad_refs):
            g_ref[c_ref[0] ^ u] = ref[...]
    for s in range(shards):
        count[s] = 0
    c = c_ref[0]

    def step(b, carry):
        dest = place_ref[b] // per_shard
        slot = count[dest]
        count[dest] = slot + 1
        out_ref[rows16(b), :] = g_ref[dest, rows16(slot), :]
        return carry

    lax.fori_loop(0, place_ref.shape[0], step, 0)
    rows = mine_ref.shape[0]
    mine_ref[...] = out_ref[pl.ds(pl.multiple_of(c * rows, IMGTOK), rows), :]


def reorder(c, place, gathered, per_shard, images, shards):
    rows, width = gathered[0].shape[-2:]
    dtype = gathered[0].dtype
    smem = pl.BlockSpec(memory_space=pltpu.SMEM)
    vmem = pl.BlockSpec(memory_space=pltpu.VMEM)
    return pl.pallas_call(
        functools.partial(reorder_body, per_shard, images),
        in_specs=[smem, smem] + [vmem] * len(gathered),
        out_specs=[vmem, vmem],
        out_shape=[
            jax.ShapeDtypeStruct((shards * rows, width), dtype),
            jax.ShapeDtypeStruct((rows, width), dtype),
        ],
        scratch_shapes=[
            pltpu.VMEM((shards, rows, width), dtype),
            pltpu.SMEM((shards,), jnp.int32),
        ],
        cost_estimate=cost(0, shards * rows * width * 8),
        compiler_params=params(),
    )(c, place, *gathered)


def weight_body(s_ref, g_ref, out_ref):
    out_ref[...] = dot(s_ref[0], g_ref[...], TN)


def weight_term(states, grad):
    parts, rows, cols = states.shape
    width = grad.shape[1]
    return pl.pallas_call(
        weight_body,
        grid=(parts,),
        in_specs=[
            pl.BlockSpec((1, rows, cols), lambda k: (k, 0, 0)),
            pl.BlockSpec(grad.shape, lambda k: (0, 0)),
        ],
        out_specs=pl.BlockSpec((cols, width), lambda k: (k, 0)),
        out_shape=jax.ShapeDtypeStruct((parts * cols, width), jnp.float32),
        cost_estimate=cost(2 * states.size * width, states.size * 4),
        compiler_params=params(),
    )(states, grad)


def slice_body(first, groups, m_ref, c_ref, kept_ref, g_ref, *refs):
    out_ref = refs[-1]
    ranks, rows, width = g_ref.shape
    m = m_ref[0]
    c = c_ref[0]
    grad = jnp.concatenate([g_ref[c ^ u] for u in range(1, ranks)], axis=0)
    cols = refs[0].shape[1]
    state_refs = list(refs[:-1])
    for k, count in enumerate(groups):
        at = pl.multiple_of((m ^ (first + k)) * cols, cols)
        total = dot(kept_ref[:, pl.ds(at, cols)], g_ref[c], TN)
        done = 0
        for ref in state_refs[:count]:
            total = total + dot(ref[...], grad[done : done + ref.shape[0]], TN)
            done += ref.shape[0]
        state_refs = state_refs[count:]
        out_ref[k] = total


def slice_terms(first, groups, m, c, kept, grad, states):
    cols = states[0].shape[1]
    width = grad.shape[2]
    smem = pl.BlockSpec(memory_space=pltpu.SMEM)
    vmem = pl.BlockSpec(memory_space=pltpu.VMEM)
    rows = grad.shape[0] * grad.shape[1]
    return pl.pallas_call(
        functools.partial(slice_body, first, groups),
        in_specs=[smem, smem] + [vmem] * (2 + len(states)),
        out_specs=vmem,
        out_shape=jax.ShapeDtypeStruct((len(groups), cols, width), jnp.float32),
        cost_estimate=cost(2 * rows * cols * width * len(groups), rows * cols * len(groups) * 4),
        compiler_params=params(),
    )(m, c, kept, grad, *states)


def settle_body(m_ref, *refs):
    out_ref = refs[-1]
    m = m_ref[0]
    half = (len(refs) - 1) // 2
    k = 0
    for own, other in zip(refs[:half], refs[half:-1]):
        for i in range(own.shape[0]):
            cols = own.shape[1]
            at = pl.ds(pl.multiple_of((m ^ k) * cols, cols), cols)
            out_ref[at, :] = own[i] + other[i]
            k += 1


def settle(m, own, other):
    count = sum(a.shape[0] for a in own)
    _, cols, width = own[0].shape
    vmem = pl.BlockSpec(memory_space=pltpu.VMEM)
    return pl.pallas_call(
        settle_body,
        in_specs=[pl.BlockSpec(memory_space=pltpu.SMEM)] + [vmem] * (2 * len(own)),
        out_specs=vmem,
        out_shape=jax.ShapeDtypeStruct((count * cols, width), jnp.float32),
        cost_estimate=cost(0, count * cols * width * 12),
        compiler_params=params(),
    )(m, *own, *other)


def image_body(d_ref, *refs):
    out_ref = refs[-1]
    heads = (len(refs) - 1) // 3
    grads, near, far = refs[:heads], refs[heads : 2 * heads], refs[2 * heads : -1]
    j = pl.program_id(0)
    cols = near[0].shape[0]
    half = out_ref.shape[1] // 2
    d = d_ref[0]
    for weights, side in ((near, d), (far, 1 - d)):
        total = dot(grads[0][...], weights[0][...], NT)
        for h in range(1, heads):
            total = total + dot(grads[h][...], weights[h][...], NT)
        at = pl.multiple_of(side * half + j * cols, cols)
        out_ref[:, pl.ds(at, cols)] = total.astype(out_ref.dtype)


def image_term(d, grads, near, far):
    heads = len(near)
    half, width = near[0].shape
    rows = grads[0].shape[0]
    tiles = 4
    side = pl.BlockSpec((half // tiles, width), lambda j, d: (j, 0))
    grad = pl.BlockSpec((rows, width), lambda j, d: (0, 0))
    return pl.pallas_call(
        image_body,
        grid_spec=pltpu.PrefetchScalarGridSpec(
            num_scalar_prefetch=1,
            grid=(tiles,),
            in_specs=[grad] * heads + [side] * (2 * heads),
            out_specs=pl.BlockSpec((rows, 2 * half), lambda j, d: (0, 0)),
        ),
        out_shape=jax.ShapeDtypeStruct((rows, 2 * half), jnp.bfloat16),
        cost_estimate=cost(4 * heads * half * width * rows, 4 * heads * half * width * 2),
        compiler_params=params(),
    )(d, *grads, *near, *far)


def per_device(image_states, place_index, doc_ids, queries, text_kv, kv_weight, d_out):
    ranks = lax.axis_size("ctx")
    mps = lax.axis_size("mp")
    c = lax.axis_index("ctx")
    d = lax.axis_index("dp")
    rows = queries.shape[1]
    states = image_states[0]
    image_rows, feats = states.shape
    images = image_rows // IMGTOK
    per_shard = rows // IMGTOK
    capacity = IMGTOK * ((images + ranks - 1) // ranks)
    weights = kv_weight[0]
    width = weights.shape[1]
    c1 = jnp.reshape(c, (1,)).astype(jnp.int32)
    d1 = jnp.reshape(d, (1,)).astype(jnp.int32)
    place = place_index[0, ::IMGTOK] // IMGTOK

    m = lax.axis_index("mp")
    m1 = jnp.reshape(m, (1,)).astype(jnp.int32)
    steps = range(1, mps)
    mixed = ranks == mps

    x = trade(states, "mp", 1)
    y = trade(states, "mp", 2)
    low = trade(x[: image_rows // 2], "mp", 2)
    high = trade(y[image_rows // 2 :], "mp", 1)
    part, *slabs = project(m1, d1, [states, x, y], weights)

    prior_text = shift(text_kv[0], "ctx", 1)
    docs = doc_ids[0]
    own_docs = lax.dynamic_slice_in_dim(docs, c * rows, rows)
    prior_docs = lax.dynamic_slice_in_dim(docs, jnp.maximum(c - 1, 0) * rows, rows)
    prior_docs = jnp.where(c > 0, prior_docs, -1)
    key_docs = jnp.concatenate([prior_docs, own_docs])
    start = jnp.sum((key_docs[:, None] < own_docs[None, :]).astype(jnp.int32), axis=0)[None]
    low, high, prior_text, start, place = lax.optimization_barrier(
        (low, high, prior_text, start, place)
    )
    packed = pack(
        m1, c1, place, low, high, weights, part, ranks, capacity, per_shard, mixed
    )

    *slabs, _ = lax.optimization_barrier((*slabs, packed[0]))
    slabs, own_slabs = slabs[:3], slabs[3:]
    near = [trade(slabs[0], "mp", 1), None, trade(slabs[2], "mp", 3)]

    if mixed:
        c2, _ = lax.optimization_barrier((c1, packed[0]))
        kept, *moved = slices(m1, c2, [states, x, y, low, high], feats // mps)
        image = [trade(packed[s], "ctx", s) if s else packed[0] for s in range(ranks)]
        both = lax.optimization_barrier((*moved, *image))
        moved, image = both[: len(moved)], both[len(moved) :]
        moved = [trade(moved[s - 1], "ctx", s) for s in range(1, ranks)]
    else:
        image = [exchange(packed[0], "ctx")]
        whole = lax.all_gather(states, "mp", axis=1, tiled=True)
        moved = whole.reshape(image_rows, ranks, mps, -1)
        moved = lax.dynamic_index_in_dim(moved, m, axis=2, keepdims=False).transpose(1, 0, 2)
        moved = [exchange(moved, "ctx").reshape(ranks * image_rows, -1)]

    attn_out, own_grad, prior_grad = attention(
        c1, place, start, queries[0], d_out[0], text_kv[0], prior_text, image,
        images, per_shard, image_rows,
    )
    prior_grad, near[0], near[2], *moved = lax.optimization_barrier(
        (prior_grad, near[0], near[2], *moved)
    )
    far = [own_slabs[1], swap(near[0], "dp"), None, swap(near[2], "dp")]
    grad = own_grad + shift(prior_grad, "ctx", -1).astype(jnp.float32)
    grad = grad.astype(jnp.bfloat16)
    if mixed:
        gathered = [trade(grad, "ctx", s) if s else grad for s in range(ranks)]
        base = jnp.concatenate(moved, axis=0)
        cut = base.shape[0] // 2
        base_x = trade(base, "mp", 1)
        base_y = trade(base, "mp", 2)
    else:
        gathered = [exchange(jnp.broadcast_to(grad, (ranks,) + grad.shape), "ctx")]
        all_states = lax.all_gather(moved[0], "mp", axis=0)
        base_x = base_y = all_states
    slabs[1], base_x, base_y, *gathered = lax.optimization_barrier(
        (slabs[1], base_x, base_y, *gathered)
    )
    near[1] = trade(slabs[1], "mp", 2)
    by_rank, mine = reorder(c1, place, gathered, per_shard, images, ranks)
    head_grad = [mine] + [trade(mine, "mp", s) for s in steps]
    if mixed:
        base_low = trade(base_x[:cut], "mp", 2)
        base_high = trade(base_y[cut:], "mp", 1)
        by_rank, base_low, base_high, near[1], *head_grad = lax.optimization_barrier(
            (by_rank, base_low, base_high, near[1], *head_grad)
        )
    far[2] = swap(near[1], "dp")
    near = [own_slabs[0]] + list(near)
    image_grad = image_term(d1, head_grad, near, far)
    if mixed:
        by_rank = by_rank.reshape(ranks, image_rows, width)
        terms = [
            slice_terms(0, (1, 1, 1), m1, c1, kept, by_rank, [base, base_x, base_y]),
            slice_terms(3, (2,), m1, c1, kept, by_rank, [base_low, base_high]),
        ]
        weight_grad = settle(m1, terms, [swap(a, "dp") for a in terms])
    else:
        term = weight_term(all_states, by_rank)
        weight_grad = term + swap(term, "dp")
    return (attn_out[None], image_grad[None], weight_grad[None])


def solution(mesh):
    in_specs = (
        P("dp", "ctx", "mp"),
        P("dp", None),
        P("dp", None),
        P("dp", "ctx", "mp"),
        P("dp", "ctx", "mp"),
        P("mp", None, None),
        P("dp", "ctx", "mp"),
    )
    out_specs = (P("dp", "ctx", "mp"), P("dp", "ctx", "mp"), P("mp", "ctx", None))
    return jax.shard_map(
        per_device, mesh=mesh, in_specs=in_specs, out_specs=out_specs, check_vma=False
    )
```

```python
import functools

import jax
import jax.numpy as jnp
from jax import lax
from jax.experimental import pallas as pl
from jax.experimental.pallas import tpu as pltpu
from jax.sharding import PartitionSpec as P

IMGTOK = 16
QTILE = 128
SPANS = (2, 3)
LOG2E = 1.4426950408889634
VMEM = 24 * 1024 * 1024

NN = (((1,), (0,)), ((), ()))
NT = (((1,), (1,)), ((), ()))
TN = (((0,), (0,)), ((), ()))


def dot(a, b, dims):
    return lax.dot_general(a, b, dims, preferred_element_type=jnp.float32)


def params():
    return pltpu.CompilerParams(vmem_limit_bytes=VMEM)


def cost(flops, moved):
    return pl.CostEstimate(flops=int(flops), bytes_accessed=int(moved), transcendentals=0)


def shift(block, axis, distance):
    devices = range(lax.axis_size(axis))
    route = [(i - distance, i) for i in devices if i - distance in devices]
    return lax.ppermute(block, axis, route)


def swap(block, axis):
    count = lax.axis_size(axis)
    return lax.ppermute(block, axis, [(i, count - 1 - i) for i in range(count)])


def exchange(blocks, axis):
    return lax.all_to_all(blocks, axis, split_axis=0, concat_axis=0, tiled=True)


def trade(block, axis, step):
    count = lax.axis_size(axis)
    return lax.ppermute(block, axis, [(i, i ^ step) for i in range(count)])


def rows16(start):
    return pl.ds(pl.multiple_of(start * IMGTOK, IMGTOK), IMGTOK)


def project_body(m_ref, d_ref, own_ref, x_ref, y_ref, weight_ref, out_ref, *slab_refs):
    m = m_ref[0]
    d = d_ref[0]
    feats = own_ref.shape[1]
    half = slab_refs[1].shape[0]

    def rows(k, at, count):
        return pl.ds(pl.multiple_of((m ^ k) * feats + at, half), count)

    total = dot(own_ref[...], weight_ref[rows(0, 0, feats), :], NN)
    for k, ref in ((1, x_ref), (2, y_ref)):
        total = total + dot(ref[...], weight_ref[rows(k, 0, feats), :], NN)
    out_ref[...] = total
    for k, at, ref in zip((1 + d, 3, 0), (0, d * half, 0), slab_refs):
        ref[...] = weight_ref[rows(k, at, ref.shape[0]), :]


def project(m, d, blocks, weights):
    rows, feats = blocks[0].shape
    width = weights.shape[1]
    smem = pl.BlockSpec(memory_space=pltpu.SMEM)
    vmem = pl.BlockSpec(memory_space=pltpu.VMEM)
    slabs = [jax.ShapeDtypeStruct((r, width), weights.dtype) for r in (feats, feats // 2, feats)]
    return pl.pallas_call(
        project_body,
        in_specs=[smem, smem] + [vmem] * 4,
        out_specs=[vmem] * 4,
        out_shape=[jax.ShapeDtypeStruct((rows, width), jnp.float32)] + slabs,
        cost_estimate=cost(6 * rows * feats * width, 4 * weights.size),
        compiler_params=params(),
    )(m, d, *blocks, weights)


def pack_body(per_shard, m_ref, c_ref, place_ref, low_ref, high_ref, weight_ref, part_ref, *refs):
    out_refs = refs[:-3]
    rounded, sorted_ref, count = refs[-3:]
    shards = sorted_ref.shape[0]
    half = low_ref.shape[0]
    for at, ref in ((0, low_ref), (half, high_ref)):
        term = dot(ref[...], weight_ref[...], NN)
        rounded[at : at + half, :] = (part_ref[at : at + half, :] + term).astype(jnp.bfloat16)
    sorted_ref[...] = jnp.zeros_like(sorted_ref)
    for s in range(shards):
        count[s] = 0
    images = rounded.shape[0] // IMGTOK
    c = c_ref[0]

    def step(i, carry):
        dest = place_ref[c * images + i] // per_shard
        slot = count[dest]
        count[dest] = slot + 1
        block = rounded[rows16(i), :]
        sorted_ref[dest, 0, rows16(slot), :] = block

        @pl.when(dest + 1 < shards)
        def _():
            sorted_ref[dest + 1, 1, rows16(slot), :] = block

        return carry

    lax.fori_loop(0, images, step, 0)
    if len(out_refs) == 1:
        out_refs[0][...] = sorted_ref[...]
    else:
        for u, ref in enumerate(out_refs):
            ref[...] = sorted_ref[c ^ u]


def pack(m, c, place, low, high, weights, part, shards, capacity, per_shard, mixed):
    rows, width = part.shape
    feats = low.shape[1]
    whole = lambda a: pl.BlockSpec(a.shape, lambda i, *_: (0,) * len(a.shape))
    shape = (2, capacity, width)
    if mixed:
        out = [jax.ShapeDtypeStruct(shape, jnp.bfloat16)] * shards
    else:
        out = [jax.ShapeDtypeStruct((shards,) + shape, jnp.bfloat16)]
    return pl.pallas_call(
        functools.partial(pack_body, per_shard),
        grid_spec=pltpu.PrefetchScalarGridSpec(
            num_scalar_prefetch=3,
            grid=(1,),
            in_specs=[
                whole(low),
                whole(high),
                pl.BlockSpec((feats, width), lambda i, m, *_: (m[0] ^ 3, 0)),
                whole(part),
            ],
            out_specs=[whole(a) for a in out],
            scratch_shapes=[
                pltpu.VMEM((rows, width), jnp.bfloat16),
                pltpu.VMEM((shards,) + shape, jnp.bfloat16),
                pltpu.SMEM((shards,), jnp.int32),
            ],
        ),
        out_shape=out,
        cost_estimate=cost(2 * rows * feats * width, part.size * 16),
        compiler_params=params(),
    )(m, c, place, low, high, weights, part)


def slices_body(m_ref, c_ref, own_ref, x_ref, y_ref, low_ref, high_ref, kept_ref, *out_refs):
    m = m_ref[0]
    c = c_ref[0]
    sub = out_refs[0].shape[1]
    half = low_ref.shape[0]
    for u, ref in enumerate((kept_ref,) + out_refs):
        at = pl.ds(0, ref.shape[1]) if u == 0 else pl.ds(pl.multiple_of(m * sub, sub), sub)
        which = m ^ c ^ u
        for k, source in enumerate((own_ref, x_ref, y_ref)):

            @pl.when(which == k)
            def _():
                ref[...] = source[:, at]

        @pl.when(which == 3)
        def _():
            ref[:half, :] = low_ref[:, at]
            ref[half:, :] = high_ref[:, at]


def slices(m, c, blocks, sub):
    rows, feats = blocks[0].shape
    smem = pl.BlockSpec(memory_space=pltpu.SMEM)
    vmem = pl.BlockSpec(memory_space=pltpu.VMEM)
    dtype = blocks[0].dtype
    out = [jax.ShapeDtypeStruct((rows, feats), dtype)]
    out += [jax.ShapeDtypeStruct((rows, sub), dtype)] * 3
    return pl.pallas_call(
        slices_body,
        in_specs=[smem, smem] + [vmem] * len(blocks),
        out_specs=[vmem] * len(out),
        out_shape=out,
        cost_estimate=cost(0, rows * feats * 16),
        compiler_params=params(),
    )(m, c, *blocks)


def attention_body(
    per_shard,
    images,
    c_ref,
    place_ref,
    start_ref,
    q_ref,
    g_ref,
    own_ref,
    prior_ref,
    *refs,
):
    image_refs = refs[:-8]
    out_ref, own_grad_ref, prior_grad_ref, window, probs, grads, total, image_ref = refs[-8:]
    t = pl.program_id(0)
    c = c_ref[0]
    rows = own_ref.shape[0]
    hd = own_ref.shape[1] // 2
    blocks = place_ref.shape[0]
    heads = q_ref.shape[1] // hd
    scale = hd ** (-0.5)

    @pl.when(t == 0)
    def _():
        window[:rows, :] = prior_ref[...]
        window[rows:, :] = own_ref[...]
        total[...] = jnp.zeros_like(total)
        if len(image_refs) == 1:
            image_ref[...] = image_refs[0][...]
        else:
            for u, ref in enumerate(image_refs):
                image_ref[c ^ u] = ref[...]

        def step(b, carry):
            n_own, n_prior = carry
            rank = b // images
            fresh = b % images == 0
            n_own = jnp.where(fresh, 0, n_own)
            n_prior = jnp.where(fresh, 0, n_prior)
            at = place_ref[b] - (c - 1) * per_shard
            is_prior = (at >= 0) & (at < per_shard)
            is_own = (at >= per_shard) & (at < 2 * per_shard)

            @pl.when(is_own)
            def _():
                window[rows16(at), :] = image_ref[rank, 0, rows16(n_own), :]

            @pl.when(is_prior)
            def _():
                window[rows16(at), :] = image_ref[rank, 1, rows16(n_prior), :]

            return n_own + is_own.astype(jnp.int32), n_prior + is_prior.astype(jnp.int32)

        lax.fori_loop(0, blocks, step, (jnp.int32(0), jnp.int32(0)))

    first = t * QTILE

    def stack(ref, a, b):
        return jnp.concatenate([ref[:, h * hd : (h + 1) * hd] for h in range(a, b)], axis=0)

    def tile(span):
        base = pl.multiple_of(first + (full - span), QTILE)
        keys = window[pl.ds(base, span), :hd]
        values = window[pl.ds(base, span), hd:]
        values_t = values.T
        key_pos = lax.broadcasted_iota(jnp.int32, (span, QTILE), 0) + base
        query_pos = lax.broadcasted_iota(jnp.int32, (span, QTILE), 1) + (first + rows)
        allowed = (key_pos <= query_pos) & (key_pos >= start_ref[...])
        bias = jnp.where(allowed, 0.0, -1e30)
        bias = jnp.concatenate([bias, bias], axis=1)

        def products(h):
            query = stack(q_ref, h, h + 2)
            grad = stack(g_ref, h, h + 2)
            return dot(keys, query, NT), dot(values, grad, NT)

        def softmax(h, scores):
            scores = scores * (scale * LOG2E) + bias
            top = jnp.max(scores, axis=0, keepdims=True)
            e = jnp.exp2(scores - top)
            p = e * (1.0 / jnp.sum(e, axis=0, keepdims=True))
            low = p.astype(jnp.bfloat16)
            probs[:span, h * QTILE : (h + 2) * QTILE] = low
            return p, dot(values_t, low, NN)

        def backward(h, p, grad_p, context_t):
            grad_t = stack(g_ref, h, h + 2).astype(jnp.float32).T
            delta = jnp.sum(grad_t * context_t, axis=0, keepdims=True)
            ds = (p * (grad_p - delta)).astype(jnp.bfloat16)
            context = context_t.T.astype(jnp.bfloat16)
            out_ref[:, h * hd : (h + 1) * hd] = context[:QTILE]
            out_ref[:, (h + 1) * hd : (h + 2) * hd] = context[QTILE:]
            grads[:span, h * QTILE : (h + 2) * QTILE] = ds

        pairs = heads // 2
        first_stage, second_stage = {}, {}
        for i in range(pairs + 2):
            if i < pairs:
                first_stage[i] = products(2 * i)
            if 1 <= i <= pairs:
                scores, grad_p = first_stage.pop(i - 1)
                second_stage[i - 1] = (grad_p, *softmax(2 * (i - 1), scores))
            if i >= 2:
                grad_p, p, context_t = second_stage.pop(i - 2)
                backward(2 * (i - 2), p, grad_p, context_t)
        total[pl.ds(base, span), :hd] += dot(grads[:span, :], stack(q_ref, 0, heads), NN)
        total[pl.ds(base, span), hd:] += dot(probs[:span, :], stack(g_ref, 0, heads), NN)

    full = rows + QTILE
    need = full - (jnp.min(start_ref[...]) - first)
    below = 0
    for span in sorted({min(b * QTILE, full) for b in SPANS} | {full}):
        lower, below = below, span

        @pl.when((need > lower) & (need <= span))
        def _():
            tile(span)

    @pl.when(t == pl.num_programs(0) - 1)
    def _():
        total[:, :hd] = total[:, :hd] * scale
        prior_grad_ref[...] = jnp.zeros_like(prior_grad_ref)

        def step(b, carry):
            n_own, n_prior = carry
            at = place_ref[b] - (c - 1) * per_shard
            is_prior = (at >= 0) & (at < per_shard)
            is_own = (at >= per_shard) & (at < 2 * per_shard)

            @pl.when(is_own)
            def _():
                own_grad_ref[rows16(n_own), :] = total[rows16(at), :]

            @pl.when(is_prior)
            def _():
                prior_grad_ref[rows16(n_prior), :] = total[rows16(at), :].astype(jnp.bfloat16)

            return n_own + is_own.astype(jnp.int32), n_prior + is_prior.astype(jnp.int32)

        lax.fori_loop(0, blocks, step, (jnp.int32(0), jnp.int32(0)))


def attention(c, place, start, queries, d_out, own, prior, image, images, per_shard, image_rows):
    ranks = len(image) if len(image) > 1 else image[0].shape[0]
    rows, width = own.shape
    cols = queries.shape[1]
    tiles = rows // QTILE
    span = rows + QTILE
    head_rows = cols // (width // 2) * QTILE
    whole = lambda a: pl.BlockSpec(a.shape, lambda t, *_: (0,) * a.ndim)
    tile = pl.BlockSpec((QTILE, cols), lambda t, *_: (t, 0))
    grad = jax.ShapeDtypeStruct((image_rows, width), jnp.float32)
    prior_grad = jax.ShapeDtypeStruct((image_rows, width), jnp.bfloat16)
    return pl.pallas_call(
        functools.partial(attention_body, per_shard, images),
        grid_spec=pltpu.PrefetchScalarGridSpec(
            num_scalar_prefetch=2,
            grid=(tiles,),
            in_specs=[
                pl.BlockSpec((1, QTILE), lambda t, *_: (0, t)),
                tile,
                tile,
                whole(own),
                whole(prior),
                *map(whole, image),
            ],
            out_specs=[tile, whole(grad), whole(grad)],
            scratch_shapes=[
                pltpu.VMEM((2 * rows, width), jnp.bfloat16),
                pltpu.VMEM((span, head_rows), jnp.bfloat16),
                pltpu.VMEM((span, head_rows), jnp.bfloat16),
                pltpu.VMEM((2 * rows, width), jnp.float32),
                pltpu.VMEM((ranks,) + image[0].shape[-3:], jnp.bfloat16),
            ],
        ),
        out_shape=[jax.ShapeDtypeStruct((rows, cols), jnp.bfloat16), grad, prior_grad],
        cost_estimate=cost(2 * 20 * cols * span * rows, 4 * queries.size * 2),
        compiler_params=params(),
    )(c, place, start, queries, d_out, own, prior, *image)


def reorder_body(per_shard, images, c_ref, place_ref, *refs):
    grad_refs = refs[:-4]
    out_ref, mine_ref, g_ref, count = refs[-4:]
    shards = g_ref.shape[0]
    if len(grad_refs) == 1:
        g_ref[...] = grad_refs[0][...]
    else:
        for u, ref in enumerate(grad_refs):
            g_ref[c_ref[0] ^ u] = ref[...]
    for s in range(shards):
        count[s] = 0
    c = c_ref[0]

    def step(b, carry):
        dest = place_ref[b] // per_shard
        slot = count[dest]
        count[dest] = slot + 1
        out_ref[rows16(b), :] = g_ref[dest, rows16(slot), :]
        return carry

    lax.fori_loop(0, place_ref.shape[0], step, 0)
    rows = mine_ref.shape[0]
    mine_ref[...] = out_ref[pl.ds(pl.multiple_of(c * rows, IMGTOK), rows), :]


def reorder(c, place, gathered, per_shard, images, shards):
    rows, width = gathered[0].shape[-2:]
    dtype = gathered[0].dtype
    smem = pl.BlockSpec(memory_space=pltpu.SMEM)
    vmem = pl.BlockSpec(memory_space=pltpu.VMEM)
    return pl.pallas_call(
        functools.partial(reorder_body, per_shard, images),
        in_specs=[smem, smem] + [vmem] * len(gathered),
        out_specs=[vmem, vmem],
        out_shape=[
            jax.ShapeDtypeStruct((shards * rows, width), dtype),
            jax.ShapeDtypeStruct((rows, width), dtype),
        ],
        scratch_shapes=[
            pltpu.VMEM((shards, rows, width), dtype),
            pltpu.SMEM((shards,), jnp.int32),
        ],
        cost_estimate=cost(0, shards * rows * width * 8),
        compiler_params=params(),
    )(c, place, *gathered)


def weight_body(s_ref, g_ref, out_ref):
    out_ref[...] = dot(s_ref[0], g_ref[...], TN)


def weight_term(states, grad):
    parts, rows, cols = states.shape
    width = grad.shape[1]
    return pl.pallas_call(
        weight_body,
        grid=(parts,),
        in_specs=[
            pl.BlockSpec((1, rows, cols), lambda k: (k, 0, 0)),
            pl.BlockSpec(grad.shape, lambda k: (0, 0)),
        ],
        out_specs=pl.BlockSpec((cols, width), lambda k: (k, 0)),
        out_shape=jax.ShapeDtypeStruct((parts * cols, width), jnp.float32),
        cost_estimate=cost(2 * states.size * width, states.size * 4),
        compiler_params=params(),
    )(states, grad)


def slice_body(first, groups, m_ref, c_ref, kept_ref, g_ref, *refs):
    out_ref = refs[-1]
    ranks, rows, width = g_ref.shape
    m = m_ref[0]
    c = c_ref[0]
    grad = jnp.concatenate([g_ref[c ^ u] for u in range(1, ranks)], axis=0)
    cols = refs[0].shape[1]
    state_refs = list(refs[:-1])
    for k, count in enumerate(groups):
        at = pl.multiple_of((m ^ (first + k)) * cols, cols)
        total = dot(kept_ref[:, pl.ds(at, cols)], g_ref[c], TN)
        done = 0
        for ref in state_refs[:count]:
            total = total + dot(ref[...], grad[done : done + ref.shape[0]], TN)
            done += ref.shape[0]
        state_refs = state_refs[count:]
        out_ref[k] = total


def slice_terms(first, groups, m, c, kept, grad, states):
    cols = states[0].shape[1]
    width = grad.shape[2]
    smem = pl.BlockSpec(memory_space=pltpu.SMEM)
    vmem = pl.BlockSpec(memory_space=pltpu.VMEM)
    rows = grad.shape[0] * grad.shape[1]
    return pl.pallas_call(
        functools.partial(slice_body, first, groups),
        in_specs=[smem, smem] + [vmem] * (2 + len(states)),
        out_specs=vmem,
        out_shape=jax.ShapeDtypeStruct((len(groups), cols, width), jnp.float32),
        cost_estimate=cost(2 * rows * cols * width * len(groups), rows * cols * len(groups) * 4),
        compiler_params=params(),
    )(m, c, kept, grad, *states)


def settle_body(m_ref, *refs):
    out_ref = refs[-1]
    m = m_ref[0]
    half = (len(refs) - 1) // 2
    k = 0
    for own, other in zip(refs[:half], refs[half:-1]):
        for i in range(own.shape[0]):
            cols = own.shape[1]
            at = pl.ds(pl.multiple_of((m ^ k) * cols, cols), cols)
            out_ref[at, :] = own[i] + other[i]
            k += 1


def settle(m, own, other):
    count = sum(a.shape[0] for a in own)
    _, cols, width = own[0].shape
    vmem = pl.BlockSpec(memory_space=pltpu.VMEM)
    return pl.pallas_call(
        settle_body,
        in_specs=[pl.BlockSpec(memory_space=pltpu.SMEM)] + [vmem] * (2 * len(own)),
        out_specs=vmem,
        out_shape=jax.ShapeDtypeStruct((count * cols, width), jnp.float32),
        cost_estimate=cost(0, count * cols * width * 12),
        compiler_params=params(),
    )(m, *own, *other)


def image_body(d_ref, g0, g1, g2, g3, own_ref, first_ref, second_ref, near_ref, far_ref, out_ref):
    half = near_ref.shape[0]
    tile = half // 4
    d = d_ref[0]
    first = jnp.where(d == 0, g1[...], g2[...])
    second = jnp.where(d == 0, g2[...], g1[...])
    for ref, side in ((near_ref, d), (far_ref, 1 - d)):
        for j in range(0, half, tile):
            at = pl.ds(pl.multiple_of(side * half + j, tile), tile)
            total = dot(g0[...], own_ref[at, :], NT) + dot(first, first_ref[at, :], NT)
            total = total + dot(second, second_ref[at, :], NT)
            total = total + dot(g3[...], ref[j : j + tile, :], NT)
            out_ref[:, at] = total.astype(out_ref.dtype)


def image_term(d, grads, weights):
    feats, width = weights[0].shape
    rows = grads[0].shape[0]
    vmem = pl.BlockSpec(memory_space=pltpu.VMEM)
    return pl.pallas_call(
        image_body,
        in_specs=[pl.BlockSpec(memory_space=pltpu.SMEM)] + [vmem] * 9,
        out_specs=vmem,
        out_shape=jax.ShapeDtypeStruct((rows, feats), jnp.bfloat16),
        cost_estimate=cost(8 * feats * width * rows, 8 * feats * width),
        compiler_params=params(),
    )(d, *grads, *weights)


def per_device(image_states, place_index, doc_ids, queries, text_kv, kv_weight, d_out):
    ranks = lax.axis_size("ctx")
    mps = lax.axis_size("mp")
    c = lax.axis_index("ctx")
    d = lax.axis_index("dp")
    rows = queries.shape[1]
    states = image_states[0]
    image_rows, feats = states.shape
    images = image_rows // IMGTOK
    per_shard = rows // IMGTOK
    capacity = IMGTOK * ((images + ranks - 1) // ranks)
    weights = kv_weight[0]
    width = weights.shape[1]
    c1 = jnp.reshape(c, (1,)).astype(jnp.int32)
    d1 = jnp.reshape(d, (1,)).astype(jnp.int32)
    place = place_index[0, ::IMGTOK] // IMGTOK

    m = lax.axis_index("mp")
    m1 = jnp.reshape(m, (1,)).astype(jnp.int32)
    steps = range(1, mps)
    mixed = ranks == mps

    x = trade(states, "mp", 1)
    y = trade(states, "mp", 2)
    low = trade(x[: image_rows // 2], "mp", 2)
    high = trade(y[image_rows // 2 :], "mp", 1)
    part, *slabs = project(m1, d1, [states, x, y], weights)

    prior_text = shift(text_kv[0], "ctx", 1)
    docs = doc_ids[0]
    own_docs = lax.dynamic_slice_in_dim(docs, c * rows, rows)
    prior_docs = lax.dynamic_slice_in_dim(docs, jnp.maximum(c - 1, 0) * rows, rows)
    prior_docs = jnp.where(c > 0, prior_docs, -1)
    key_docs = jnp.concatenate([prior_docs, own_docs])
    start = jnp.sum((key_docs[:, None] < own_docs[None, :]).astype(jnp.int32), axis=0)[None]
    low, high, prior_text, start, place = lax.optimization_barrier(
        (low, high, prior_text, start, place)
    )
    packed = pack(
        m1, c1, place, low, high, weights, part, ranks, capacity, per_shard, mixed
    )

    *slabs, own_slab, _ = lax.optimization_barrier((*slabs, packed[0]))
    cores = lax.axis_size("dp")
    route = [
        (i * mps + j, i * mps + (j ^ (1 + i))) for i in range(cores) for j in range(mps)
    ]
    near = [lax.ppermute(slabs[0], ("dp", "mp"), route), trade(slabs[1], "mp", 3)]

    if mixed:
        c2, _ = lax.optimization_barrier((c1, packed[0]))
        kept, *moved = slices(m1, c2, [states, x, y, low, high], feats // mps)
        image = [trade(packed[s], "ctx", s) if s else packed[0] for s in range(ranks)]
        both = lax.optimization_barrier((*moved, *image))
        moved, image = both[: len(moved)], both[len(moved) :]
        moved = [trade(moved[s - 1], "ctx", s) for s in range(1, ranks)]
    else:
        image = [exchange(packed[0], "ctx")]
        whole = lax.all_gather(states, "mp", axis=1, tiled=True)
        moved = whole.reshape(image_rows, ranks, mps, -1)
        moved = lax.dynamic_index_in_dim(moved, m, axis=2, keepdims=False).transpose(1, 0, 2)
        moved = [exchange(moved, "ctx").reshape(ranks * image_rows, -1)]

    attn_out, own_grad, prior_grad = attention(
        c1, place, start, queries[0], d_out[0], text_kv[0], prior_text, image,
        images, per_shard, image_rows,
    )
    prior_grad, near[0], near[1], *moved = lax.optimization_barrier(
        (prior_grad, near[0], near[1], *moved)
    )
    far = [swap(w, "dp") for w in near]
    grad = own_grad + shift(prior_grad, "ctx", -1).astype(jnp.float32)
    grad = grad.astype(jnp.bfloat16)
    if mixed:
        gathered = [trade(grad, "ctx", s) if s else grad for s in range(ranks)]
        base = jnp.concatenate(moved, axis=0)
        cut = base.shape[0] // 2
        base_x = trade(base, "mp", 1)
        base_y = trade(base, "mp", 2)
    else:
        gathered = [exchange(jnp.broadcast_to(grad, (ranks,) + grad.shape), "ctx")]
        all_states = lax.all_gather(moved[0], "mp", axis=0)
        base_x = base_y = all_states
    base_x, base_y, *gathered = lax.optimization_barrier((base_x, base_y, *gathered))
    by_rank, mine = reorder(c1, place, gathered, per_shard, images, ranks)
    head_grad = [mine] + [trade(mine, "mp", s) for s in steps]
    if mixed:
        base_low = trade(base_x[:cut], "mp", 2)
        base_high = trade(base_y[cut:], "mp", 1)
        by_rank, base_low, base_high, *head_grad = lax.optimization_barrier(
            (by_rank, base_low, base_high, *head_grad)
        )
    image_grad = image_term(d1, head_grad, [own_slab, near[0], far[0], near[1], far[1]])
    if mixed:
        by_rank = by_rank.reshape(ranks, image_rows, width)
        terms = [
            slice_terms(0, (1, 1, 1), m1, c1, kept, by_rank, [base, base_x, base_y]),
            slice_terms(3, (2,), m1, c1, kept, by_rank, [base_low, base_high]),
        ]
        weight_grad = settle(m1, terms, [swap(a, "dp") for a in terms])
    else:
        term = weight_term(all_states, by_rank)
        weight_grad = term + swap(term, "dp")
    return (attn_out[None], image_grad[None], weight_grad[None])


def solution(mesh):
    in_specs = (
        P("dp", "ctx", "mp"),
        P("dp", None),
        P("dp", None),
        P("dp", "ctx", "mp"),
        P("dp", "ctx", "mp"),
        P("mp", None, None),
        P("dp", "ctx", "mp"),
    )
    out_specs = (P("dp", "ctx", "mp"), P("dp", "ctx", "mp"), P("mp", "ctx", None))
    return jax.shard_map(
        per_device, mesh=mesh, in_specs=in_specs, out_specs=out_specs, check_vma=False
    )
```

```python
import functools

import jax
import jax.numpy as jnp
from jax import lax
from jax.experimental import pallas as pl
from jax.experimental.pallas import tpu as pltpu
from jax.sharding import PartitionSpec as P

IMGTOK = 16
QTILE = 128
SPANS = (2, 3, 4)
LOG2E = 1.4426950408889634
VMEM = 24 * 1024 * 1024

NN = (((1,), (0,)), ((), ()))
NT = (((1,), (1,)), ((), ()))
TN = (((0,), (0,)), ((), ()))


def dot(a, b, dims):
    return lax.dot_general(a, b, dims, preferred_element_type=jnp.float32)


def params():
    return pltpu.CompilerParams(vmem_limit_bytes=VMEM)


def cost(flops, moved):
    return pl.CostEstimate(flops=int(flops), bytes_accessed=int(moved), transcendentals=0)


def shift(block, axis, distance):
    devices = range(lax.axis_size(axis))
    route = [(i - distance, i) for i in devices if i - distance in devices]
    return lax.ppermute(block, axis, route)


def swap(block, axis):
    count = lax.axis_size(axis)
    return lax.ppermute(block, axis, [(i, count - 1 - i) for i in range(count)])


def exchange(blocks, axis):
    return lax.all_to_all(blocks, axis, split_axis=0, concat_axis=0, tiled=True)


def trade(block, axis, step):
    count = lax.axis_size(axis)
    return lax.ppermute(block, axis, [(i, i ^ step) for i in range(count)])


def rows16(start):
    return pl.ds(pl.multiple_of(start * IMGTOK, IMGTOK), IMGTOK)


def project_body(m_ref, d_ref, own_ref, x_ref, y_ref, weight_ref, out_ref, *slab_refs):
    m = m_ref[0]
    d = d_ref[0]
    feats = own_ref.shape[1]
    half = slab_refs[1].shape[0]

    def rows(k, at, count):
        return pl.ds(pl.multiple_of((m ^ k) * feats + at, half), count)

    total = dot(own_ref[...], weight_ref[rows(0, 0, feats), :], NN)
    for k, ref in ((1, x_ref), (2, y_ref)):
        total = total + dot(ref[...], weight_ref[rows(k, 0, feats), :], NN)
    out_ref[...] = total
    for k, at, ref in zip((1 + d, 3, 0), (0, d * half, 0), slab_refs):
        ref[...] = weight_ref[rows(k, at, ref.shape[0]), :]


def project(m, d, blocks, weights):
    rows, feats = blocks[0].shape
    width = weights.shape[1]
    smem = pl.BlockSpec(memory_space=pltpu.SMEM)
    vmem = pl.BlockSpec(memory_space=pltpu.VMEM)
    slabs = [jax.ShapeDtypeStruct((r, width), weights.dtype) for r in (feats, feats // 2, feats)]
    return pl.pallas_call(
        project_body,
        in_specs=[smem, smem] + [vmem] * 4,
        out_specs=[vmem] * 4,
        out_shape=[jax.ShapeDtypeStruct((rows, width), jnp.float32)] + slabs,
        cost_estimate=cost(6 * rows * feats * width, 4 * weights.size),
        compiler_params=params(),
    )(m, d, *blocks, weights)


def pack_body(per_shard, m_ref, c_ref, place_ref, low_ref, high_ref, weight_ref, part_ref, *refs):
    out_refs = refs[:-3]
    rounded, sorted_ref, count = refs[-3:]
    shards = sorted_ref.shape[0]
    half = low_ref.shape[0]
    for at, ref in ((0, low_ref), (half, high_ref)):
        term = dot(ref[...], weight_ref[...], NN)
        rounded[at : at + half, :] = (part_ref[at : at + half, :] + term).astype(jnp.bfloat16)
    sorted_ref[...] = jnp.zeros_like(sorted_ref)
    for s in range(shards):
        count[s] = 0
    images = rounded.shape[0] // IMGTOK
    c = c_ref[0]

    def step(i, carry):
        dest = place_ref[c * images + i] // per_shard
        slot = count[dest]
        count[dest] = slot + 1
        block = rounded[rows16(i), :]
        sorted_ref[dest, 0, rows16(slot), :] = block

        @pl.when(dest + 1 < shards)
        def _():
            sorted_ref[dest + 1, 1, rows16(slot), :] = block

        return carry

    lax.fori_loop(0, images, step, 0)
    if len(out_refs) == 1:
        out_refs[0][...] = sorted_ref[...]
    else:
        for u, ref in enumerate(out_refs):
            ref[...] = sorted_ref[c ^ u]


def pack(m, c, place, low, high, weights, part, shards, capacity, per_shard, mixed):
    rows, width = part.shape
    feats = low.shape[1]
    whole = lambda a: pl.BlockSpec(a.shape, lambda i, *_: (0,) * len(a.shape))
    shape = (2, capacity, width)
    if mixed:
        out = [jax.ShapeDtypeStruct(shape, jnp.bfloat16)] * shards
    else:
        out = [jax.ShapeDtypeStruct((shards,) + shape, jnp.bfloat16)]
    return pl.pallas_call(
        functools.partial(pack_body, per_shard),
        grid_spec=pltpu.PrefetchScalarGridSpec(
            num_scalar_prefetch=3,
            grid=(1,),
            in_specs=[
                whole(low),
                whole(high),
                pl.BlockSpec((feats, width), lambda i, m, *_: (m[0] ^ 3, 0)),
                whole(part),
            ],
            out_specs=[whole(a) for a in out],
            scratch_shapes=[
                pltpu.VMEM((rows, width), jnp.bfloat16),
                pltpu.VMEM((shards,) + shape, jnp.bfloat16),
                pltpu.SMEM((shards,), jnp.int32),
            ],
        ),
        out_shape=out,
        cost_estimate=cost(2 * rows * feats * width, part.size * 16),
        compiler_params=params(),
    )(m, c, place, low, high, weights, part)


def slices_body(m_ref, c_ref, own_ref, x_ref, y_ref, low_ref, high_ref, kept_ref, *out_refs):
    m = m_ref[0]
    c = c_ref[0]
    sub = out_refs[0].shape[1]
    half = low_ref.shape[0]
    for u, ref in enumerate((kept_ref,) + out_refs):
        at = pl.ds(0, ref.shape[1]) if u == 0 else pl.ds(pl.multiple_of(m * sub, sub), sub)
        which = m ^ c ^ u
        for k, source in enumerate((own_ref, x_ref, y_ref)):

            @pl.when(which == k)
            def _():
                ref[...] = source[:, at]

        @pl.when(which == 3)
        def _():
            ref[:half, :] = low_ref[:, at]
            ref[half:, :] = high_ref[:, at]


def slices(m, c, blocks, sub):
    rows, feats = blocks[0].shape
    smem = pl.BlockSpec(memory_space=pltpu.SMEM)
    vmem = pl.BlockSpec(memory_space=pltpu.VMEM)
    dtype = blocks[0].dtype
    out = [jax.ShapeDtypeStruct((rows, feats), dtype)]
    out += [jax.ShapeDtypeStruct((rows, sub), dtype)] * 3
    return pl.pallas_call(
        slices_body,
        in_specs=[smem, smem] + [vmem] * len(blocks),
        out_specs=[vmem] * len(out),
        out_shape=out,
        cost_estimate=cost(0, rows * feats * 16),
        compiler_params=params(),
    )(m, c, *blocks)


def attention_body(
    per_shard,
    images,
    c_ref,
    place_ref,
    start_ref,
    q_ref,
    g_ref,
    own_ref,
    prior_ref,
    *refs,
):
    image_refs = refs[:-8]
    out_ref, own_grad_ref, prior_grad_ref, window, probs, grads, total, image_ref = refs[-8:]
    t = pl.program_id(0)
    c = c_ref[0]
    rows = own_ref.shape[0]
    hd = own_ref.shape[1] // 2
    blocks = place_ref.shape[0]
    heads = q_ref.shape[1] // hd
    scale = hd ** (-0.5)

    @pl.when(t == 0)
    def _():
        window[:rows, :] = prior_ref[...]
        window[rows:, :] = own_ref[...]
        total[...] = jnp.zeros_like(total)
        if len(image_refs) == 1:
            image_ref[...] = image_refs[0][...]
        else:
            for u, ref in enumerate(image_refs):
                image_ref[c ^ u] = ref[...]

        def step(b, carry):
            n_own, n_prior = carry
            rank = b // images
            fresh = b % images == 0
            n_own = jnp.where(fresh, 0, n_own)
            n_prior = jnp.where(fresh, 0, n_prior)
            at = place_ref[b] - (c - 1) * per_shard
            is_prior = (at >= 0) & (at < per_shard)
            is_own = (at >= per_shard) & (at < 2 * per_shard)

            @pl.when(is_own)
            def _():
                window[rows16(at), :] = image_ref[rank, 0, rows16(n_own), :]

            @pl.when(is_prior)
            def _():
                window[rows16(at), :] = image_ref[rank, 1, rows16(n_prior), :]

            return n_own + is_own.astype(jnp.int32), n_prior + is_prior.astype(jnp.int32)

        lax.fori_loop(0, blocks, step, (jnp.int32(0), jnp.int32(0)))

    first = t * QTILE

    def stack(ref, a, b):
        return jnp.concatenate([ref[:, h * hd : (h + 1) * hd] for h in range(a, b)], axis=0)

    def tile(span):
        base = pl.multiple_of(first + (full - span), QTILE)
        keys = window[pl.ds(base, span), :hd]
        values = window[pl.ds(base, span), hd:]
        values_t = values.T
        key_pos = lax.broadcasted_iota(jnp.int32, (span, QTILE), 0) + base
        query_pos = lax.broadcasted_iota(jnp.int32, (span, QTILE), 1) + (first + rows)
        allowed = (key_pos <= query_pos) & (key_pos >= start_ref[...])
        bias = jnp.where(allowed, 0.0, -1e30)
        bias = jnp.concatenate([bias, bias], axis=1)

        def products(h):
            query = stack(q_ref, h, h + 2)
            grad = stack(g_ref, h, h + 2)
            return dot(keys, query, NT), dot(values, grad, NT)

        def softmax(h, scores):
            scores = scores * (scale * LOG2E) + bias
            top = jnp.max(scores, axis=0, keepdims=True)
            e = jnp.exp2(scores - top)
            p = e * (1.0 / jnp.sum(e, axis=0, keepdims=True))
            low = p.astype(jnp.bfloat16)
            probs[:span, h * QTILE : (h + 2) * QTILE] = low
            return p, dot(values_t, low, NN)

        def backward(h, p, grad_p, context_t):
            grad_t = stack(g_ref, h, h + 2).astype(jnp.float32).T
            delta = jnp.sum(grad_t * context_t, axis=0, keepdims=True)
            ds = (p * (grad_p - delta)).astype(jnp.bfloat16)
            context = context_t.T.astype(jnp.bfloat16)
            out_ref[:, h * hd : (h + 1) * hd] = context[:QTILE]
            out_ref[:, (h + 1) * hd : (h + 2) * hd] = context[QTILE:]
            grads[:span, h * QTILE : (h + 2) * QTILE] = ds

        pairs = heads // 2
        first_stage, second_stage = {}, {}
        for i in range(pairs + 2):
            if i < pairs:
                first_stage[i] = products(2 * i)
            if 1 <= i <= pairs:
                scores, grad_p = first_stage.pop(i - 1)
                second_stage[i - 1] = (grad_p, *softmax(2 * (i - 1), scores))
            if i >= 2:
                grad_p, p, context_t = second_stage.pop(i - 2)
                backward(2 * (i - 2), p, grad_p, context_t)
        total[pl.ds(base, span), :hd] += dot(grads[:span, :], stack(q_ref, 0, heads), NN)
        total[pl.ds(base, span), hd:] += dot(probs[:span, :], stack(g_ref, 0, heads), NN)

    full = rows + QTILE
    need = full - (jnp.min(start_ref[...]) - first)
    below = 0
    for span in sorted({min(b * QTILE, full) for b in SPANS} | {full}):
        lower, below = below, span

        @pl.when((need > lower) & (need <= span))
        def _():
            tile(span)

    @pl.when(t == pl.num_programs(0) - 1)
    def _():
        total[:, :hd] = total[:, :hd] * scale
        prior_grad_ref[...] = jnp.zeros_like(prior_grad_ref)

        def step(b, carry):
            n_own, n_prior = carry
            at = place_ref[b] - (c - 1) * per_shard
            is_prior = (at >= 0) & (at < per_shard)
            is_own = (at >= per_shard) & (at < 2 * per_shard)

            @pl.when(is_own)
            def _():
                own_grad_ref[rows16(n_own), :] = total[rows16(at), :]

            @pl.when(is_prior)
            def _():
                prior_grad_ref[rows16(n_prior), :] = total[rows16(at), :].astype(jnp.bfloat16)

            return n_own + is_own.astype(jnp.int32), n_prior + is_prior.astype(jnp.int32)

        lax.fori_loop(0, blocks, step, (jnp.int32(0), jnp.int32(0)))


def attention(c, place, start, queries, d_out, own, prior, image, images, per_shard, image_rows):
    ranks = len(image) if len(image) > 1 else image[0].shape[0]
    rows, width = own.shape
    cols = queries.shape[1]
    tiles = rows // QTILE
    span = rows + QTILE
    head_rows = cols // (width // 2) * QTILE
    whole = lambda a: pl.BlockSpec(a.shape, lambda t, *_: (0,) * a.ndim)
    tile = pl.BlockSpec((QTILE, cols), lambda t, *_: (t, 0))
    grad = jax.ShapeDtypeStruct((image_rows, width), jnp.float32)
    prior_grad = jax.ShapeDtypeStruct((image_rows, width), jnp.bfloat16)
    return pl.pallas_call(
        functools.partial(attention_body, per_shard, images),
        grid_spec=pltpu.PrefetchScalarGridSpec(
            num_scalar_prefetch=2,
            grid=(tiles,),
            in_specs=[
                pl.BlockSpec((1, QTILE), lambda t, *_: (0, t)),
                tile,
                tile,
                whole(own),
                whole(prior),
                *map(whole, image),
            ],
            out_specs=[tile, whole(grad), whole(grad)],
            scratch_shapes=[
                pltpu.VMEM((2 * rows, width), jnp.bfloat16),
                pltpu.VMEM((span, head_rows), jnp.bfloat16),
                pltpu.VMEM((span, head_rows), jnp.bfloat16),
                pltpu.VMEM((2 * rows, width), jnp.float32),
                pltpu.VMEM((ranks,) + image[0].shape[-3:], jnp.bfloat16),
            ],
        ),
        out_shape=[jax.ShapeDtypeStruct((rows, cols), jnp.bfloat16), grad, prior_grad],
        cost_estimate=cost(2 * 20 * cols * span * rows, 4 * queries.size * 2),
        compiler_params=params(),
    )(c, place, start, queries, d_out, own, prior, *image)


def reorder_body(per_shard, images, c_ref, place_ref, *refs):
    grad_refs = refs[:-4]
    out_ref, mine_ref, g_ref, count = refs[-4:]
    shards = g_ref.shape[0]
    if len(grad_refs) == 1:
        g_ref[...] = grad_refs[0][...]
    else:
        for u, ref in enumerate(grad_refs):
            g_ref[c_ref[0] ^ u] = ref[...]
    for s in range(shards):
        count[s] = 0
    c = c_ref[0]

    def step(b, carry):
        dest = place_ref[b] // per_shard
        slot = count[dest]
        count[dest] = slot + 1
        out_ref[rows16(b), :] = g_ref[dest, rows16(slot), :]
        return carry

    lax.fori_loop(0, place_ref.shape[0], step, 0)
    rows = mine_ref.shape[0]
    mine_ref[...] = out_ref[pl.ds(pl.multiple_of(c * rows, IMGTOK), rows), :]


def reorder(c, place, gathered, per_shard, images, shards):
    rows, width = gathered[0].shape[-2:]
    dtype = gathered[0].dtype
    smem = pl.BlockSpec(memory_space=pltpu.SMEM)
    vmem = pl.BlockSpec(memory_space=pltpu.VMEM)
    return pl.pallas_call(
        functools.partial(reorder_body, per_shard, images),
        in_specs=[smem, smem] + [vmem] * len(gathered),
        out_specs=[vmem, vmem],
        out_shape=[
            jax.ShapeDtypeStruct((shards * rows, width), dtype),
            jax.ShapeDtypeStruct((rows, width), dtype),
        ],
        scratch_shapes=[
            pltpu.VMEM((shards, rows, width), dtype),
            pltpu.SMEM((shards,), jnp.int32),
        ],
        cost_estimate=cost(0, shards * rows * width * 8),
        compiler_params=params(),
    )(c, place, *gathered)


def weight_body(s_ref, g_ref, out_ref):
    out_ref[...] = dot(s_ref[0], g_ref[...], TN)


def weight_term(states, grad):
    parts, rows, cols = states.shape
    width = grad.shape[1]
    return pl.pallas_call(
        weight_body,
        grid=(parts,),
        in_specs=[
            pl.BlockSpec((1, rows, cols), lambda k: (k, 0, 0)),
            pl.BlockSpec(grad.shape, lambda k: (0, 0)),
        ],
        out_specs=pl.BlockSpec((cols, width), lambda k: (k, 0)),
        out_shape=jax.ShapeDtypeStruct((parts * cols, width), jnp.float32),
        cost_estimate=cost(2 * states.size * width, states.size * 4),
        compiler_params=params(),
    )(states, grad)


def slice_body(first, groups, m_ref, c_ref, kept_ref, g_ref, *refs):
    out_ref = refs[-1]
    ranks, rows, width = g_ref.shape
    m = m_ref[0]
    c = c_ref[0]
    grad = jnp.concatenate([g_ref[c ^ u] for u in range(1, ranks)], axis=0)
    cols = refs[0].shape[1]
    state_refs = list(refs[:-1])
    for k, count in enumerate(groups):
        at = pl.multiple_of((m ^ (first + k)) * cols, cols)
        total = dot(kept_ref[:, pl.ds(at, cols)], g_ref[c], TN)
        done = 0
        for ref in state_refs[:count]:
            total = total + dot(ref[...], grad[done : done + ref.shape[0]], TN)
            done += ref.shape[0]
        state_refs = state_refs[count:]
        out_ref[k] = total


def slice_terms(first, groups, m, c, kept, grad, states):
    cols = states[0].shape[1]
    width = grad.shape[2]
    smem = pl.BlockSpec(memory_space=pltpu.SMEM)
    vmem = pl.BlockSpec(memory_space=pltpu.VMEM)
    rows = grad.shape[0] * grad.shape[1]
    return pl.pallas_call(
        functools.partial(slice_body, first, groups),
        in_specs=[smem, smem] + [vmem] * (2 + len(states)),
        out_specs=vmem,
        out_shape=jax.ShapeDtypeStruct((len(groups), cols, width), jnp.float32),
        cost_estimate=cost(2 * rows * cols * width * len(groups), rows * cols * len(groups) * 4),
        compiler_params=params(),
    )(m, c, kept, grad, *states)


def settle_body(m_ref, *refs):
    out_ref = refs[-1]
    m = m_ref[0]
    half = (len(refs) - 1) // 2
    k = 0
    for own, other in zip(refs[:half], refs[half:-1]):
        for i in range(own.shape[0]):
            cols = own.shape[1]
            at = pl.ds(pl.multiple_of((m ^ k) * cols, cols), cols)
            out_ref[at, :] = own[i] + other[i]
            k += 1


def settle(m, own, other):
    count = sum(a.shape[0] for a in own)
    _, cols, width = own[0].shape
    vmem = pl.BlockSpec(memory_space=pltpu.VMEM)
    return pl.pallas_call(
        settle_body,
        in_specs=[pl.BlockSpec(memory_space=pltpu.SMEM)] + [vmem] * (2 * len(own)),
        out_specs=vmem,
        out_shape=jax.ShapeDtypeStruct((count * cols, width), jnp.float32),
        cost_estimate=cost(0, count * cols * width * 12),
        compiler_params=params(),
    )(m, *own, *other)


def image_body(d_ref, g0, g1, g2, g3, own_ref, first_ref, second_ref, near_ref, far_ref, out_ref):
    half = near_ref.shape[0]
    tile = half // 4
    d = d_ref[0]
    first = jnp.where(d == 0, g1[...], g2[...])
    second = jnp.where(d == 0, g2[...], g1[...])
    for ref, side in ((near_ref, d), (far_ref, 1 - d)):
        for j in range(0, half, tile):
            at = pl.ds(pl.multiple_of(side * half + j, tile), tile)
            total = dot(g0[...], own_ref[at, :], NT) + dot(first, first_ref[at, :], NT)
            total = total + dot(second, second_ref[at, :], NT)
            total = total + dot(g3[...], ref[j : j + tile, :], NT)
            out_ref[:, at] = total.astype(out_ref.dtype)


def image_term(d, grads, weights):
    feats, width = weights[0].shape
    rows = grads[0].shape[0]
    vmem = pl.BlockSpec(memory_space=pltpu.VMEM)
    return pl.pallas_call(
        image_body,
        in_specs=[pl.BlockSpec(memory_space=pltpu.SMEM)] + [vmem] * 9,
        out_specs=vmem,
        out_shape=jax.ShapeDtypeStruct((rows, feats), jnp.bfloat16),
        cost_estimate=cost(8 * feats * width * rows, 8 * feats * width),
        compiler_params=params(),
    )(d, *grads, *weights)


def per_device(image_states, place_index, doc_ids, queries, text_kv, kv_weight, d_out):
    ranks = lax.axis_size("ctx")
    mps = lax.axis_size("mp")
    c = lax.axis_index("ctx")
    d = lax.axis_index("dp")
    rows = queries.shape[1]
    states = image_states[0]
    image_rows, feats = states.shape
    images = image_rows // IMGTOK
    per_shard = rows // IMGTOK
    capacity = IMGTOK * ((images + ranks - 1) // ranks)
    weights = kv_weight[0]
    width = weights.shape[1]
    c1 = jnp.reshape(c, (1,)).astype(jnp.int32)
    d1 = jnp.reshape(d, (1,)).astype(jnp.int32)
    place = place_index[0, ::IMGTOK] // IMGTOK

    m = lax.axis_index("mp")
    m1 = jnp.reshape(m, (1,)).astype(jnp.int32)
    steps = range(1, mps)
    mixed = ranks == mps

    x = trade(states, "mp", 1)
    y = trade(states, "mp", 2)
    low = trade(x[: image_rows // 2], "mp", 2)
    high = trade(y[image_rows // 2 :], "mp", 1)
    part, *slabs = project(m1, d1, [states, x, y], weights)

    prior_text = shift(text_kv[0], "ctx", 1)
    docs = doc_ids[0]
    own_docs = lax.dynamic_slice_in_dim(docs, c * rows, rows)
    prior_docs = lax.dynamic_slice_in_dim(docs, jnp.maximum(c - 1, 0) * rows, rows)
    prior_docs = jnp.where(c > 0, prior_docs, -1)
    key_docs = jnp.concatenate([prior_docs, own_docs])
    start = jnp.sum((key_docs[:, None] < own_docs[None, :]).astype(jnp.int32), axis=0)[None]
    low, high, prior_text, start, place = lax.optimization_barrier(
        (low, high, prior_text, start, place)
    )
    packed = pack(
        m1, c1, place, low, high, weights, part, ranks, capacity, per_shard, mixed
    )

    *slabs, own_slab, _ = lax.optimization_barrier((*slabs, packed[0]))
    cores = lax.axis_size("dp")
    route = [
        (i * mps + j, i * mps + (j ^ (1 + i))) for i in range(cores) for j in range(mps)
    ]
    near = [lax.ppermute(slabs[0], ("dp", "mp"), route), trade(slabs[1], "mp", 3)]

    if mixed:
        c2, _ = lax.optimization_barrier((c1, packed[0]))
        kept, *moved = slices(m1, c2, [states, x, y, low, high], feats // mps)
        image = [trade(packed[s], "ctx", s) if s else packed[0] for s in range(ranks)]
        both = lax.optimization_barrier((*moved, *image))
        moved, image = both[: len(moved)], both[len(moved) :]
        moved = [trade(moved[s - 1], "ctx", s) for s in range(1, ranks)]
    else:
        image = [exchange(packed[0], "ctx")]
        whole = lax.all_gather(states, "mp", axis=1, tiled=True)
        moved = whole.reshape(image_rows, ranks, mps, -1)
        moved = lax.dynamic_index_in_dim(moved, m, axis=2, keepdims=False).transpose(1, 0, 2)
        moved = [exchange(moved, "ctx").reshape(ranks * image_rows, -1)]

    attn_out, own_grad, prior_grad = attention(
        c1, place, start, queries[0], d_out[0], text_kv[0], prior_text, image,
        images, per_shard, image_rows,
    )
    prior_grad, near[0], near[1], *moved = lax.optimization_barrier(
        (prior_grad, near[0], near[1], *moved)
    )
    grad = own_grad + shift(prior_grad, "ctx", -1).astype(jnp.float32)
    grad = grad.astype(jnp.bfloat16)
    far = [swap(w, "dp") for w in near]
    grad, far[0] = lax.optimization_barrier((grad, far[0]))
    if mixed:
        gathered = [trade(grad, "ctx", s) if s else grad for s in range(ranks)]
        base = jnp.concatenate(moved, axis=0)
        cut = base.shape[0] // 2
        base_x = trade(base, "mp", 1)
        base_y = trade(base, "mp", 2)
    else:
        gathered = [exchange(jnp.broadcast_to(grad, (ranks,) + grad.shape), "ctx")]
        all_states = lax.all_gather(moved[0], "mp", axis=0)
        base_x = base_y = all_states
    base_x, base_y, *gathered = lax.optimization_barrier((base_x, base_y, *gathered))
    by_rank, mine = reorder(c1, place, gathered, per_shard, images, ranks)
    head_grad = [mine] + [trade(mine, "mp", s) for s in steps]
    if mixed:
        base_low = trade(base_x[:cut], "mp", 2)
        base_high = trade(base_y[cut:], "mp", 1)
        by_rank, base_low, base_high, *head_grad = lax.optimization_barrier(
            (by_rank, base_low, base_high, *head_grad)
        )
    image_grad = image_term(d1, head_grad, [own_slab, near[0], far[0], near[1], far[1]])
    if mixed:
        by_rank = by_rank.reshape(ranks, image_rows, width)
        terms = [
            slice_terms(0, (1, 1, 1), m1, c1, kept, by_rank, [base, base_x, base_y]),
            slice_terms(3, (2,), m1, c1, kept, by_rank, [base_low, base_high]),
        ]
        weight_grad = settle(m1, terms, [swap(a, "dp") for a in terms])
    else:
        term = weight_term(all_states, by_rank)
        weight_grad = term + swap(term, "dp")
    return (attn_out[None], image_grad[None], weight_grad[None])


def solution(mesh):
    in_specs = (
        P("dp", "ctx", "mp"),
        P("dp", None),
        P("dp", None),
        P("dp", "ctx", "mp"),
        P("dp", "ctx", "mp"),
        P("mp", None, None),
        P("dp", "ctx", "mp"),
    )
    out_specs = (P("dp", "ctx", "mp"), P("dp", "ctx", "mp"), P("mp", "ctx", None))
    return jax.shard_map(
        per_device, mesh=mesh, in_specs=in_specs, out_specs=out_specs, check_vma=False
    )
```

```python
import functools

import jax
import jax.numpy as jnp
from jax import lax
from jax.experimental import pallas as pl
from jax.experimental.pallas import tpu as pltpu
from jax.sharding import PartitionSpec as P

IMGTOK = 16
QTILE = 128
SPANS = (2, 3, 4)
LOG2E = 1.4426950408889634
VMEM = 24 * 1024 * 1024

NN = (((1,), (0,)), ((), ()))
NT = (((1,), (1,)), ((), ()))
TN = (((0,), (0,)), ((), ()))


def dot(a, b, dims):
    return lax.dot_general(a, b, dims, preferred_element_type=jnp.float32)


def params():
    return pltpu.CompilerParams(vmem_limit_bytes=VMEM)


def cost(flops, moved):
    return pl.CostEstimate(flops=int(flops), bytes_accessed=int(moved), transcendentals=0)


def shift(block, axis, distance):
    devices = range(lax.axis_size(axis))
    route = [(i - distance, i) for i in devices if i - distance in devices]
    return lax.ppermute(block, axis, route)


def swap(block, axis):
    count = lax.axis_size(axis)
    return lax.ppermute(block, axis, [(i, count - 1 - i) for i in range(count)])


def exchange(blocks, axis):
    return lax.all_to_all(blocks, axis, split_axis=0, concat_axis=0, tiled=True)


def trade(block, axis, step):
    count = lax.axis_size(axis)
    return lax.ppermute(block, axis, [(i, i ^ step) for i in range(count)])


def rows16(start):
    return pl.ds(pl.multiple_of(start * IMGTOK, IMGTOK), IMGTOK)


def project_body(m_ref, d_ref, own_ref, x_ref, y_ref, weight_ref, out_ref, *slab_refs):
    m = m_ref[0]
    d = d_ref[0]
    feats = own_ref.shape[1]
    half = slab_refs[1].shape[0]

    def rows(k, at, count):
        return pl.ds(pl.multiple_of((m ^ k) * feats + at, half), count)

    total = dot(own_ref[...], weight_ref[rows(0, 0, feats), :], NN)
    for k, ref in ((1, x_ref), (2, y_ref)):
        total = total + dot(ref[...], weight_ref[rows(k, 0, feats), :], NN)
    out_ref[...] = total
    for k, at, ref in zip((1 + d, 3, 0), (0, d * half, 0), slab_refs):
        ref[...] = weight_ref[rows(k, at, ref.shape[0]), :]


def project(m, d, blocks, weights):
    rows, feats = blocks[0].shape
    width = weights.shape[1]
    smem = pl.BlockSpec(memory_space=pltpu.SMEM)
    vmem = pl.BlockSpec(memory_space=pltpu.VMEM)
    slabs = [jax.ShapeDtypeStruct((r, width), weights.dtype) for r in (feats, feats // 2, feats)]
    return pl.pallas_call(
        project_body,
        in_specs=[smem, smem] + [vmem] * 4,
        out_specs=[vmem] * 4,
        out_shape=[jax.ShapeDtypeStruct((rows, width), jnp.float32)] + slabs,
        cost_estimate=cost(6 * rows * feats * width, 4 * weights.size),
        compiler_params=params(),
    )(m, d, *blocks, weights)


def pack_body(per_shard, m_ref, c_ref, place_ref, low_ref, high_ref, weight_ref, part_ref, *refs):
    out_refs = refs[:-3]
    rounded, sorted_ref, count = refs[-3:]
    shards = sorted_ref.shape[0]
    half = low_ref.shape[0]
    for at, ref in ((0, low_ref), (half, high_ref)):
        term = dot(ref[...], weight_ref[...], NN)
        rounded[at : at + half, :] = (part_ref[at : at + half, :] + term).astype(jnp.bfloat16)
    sorted_ref[...] = jnp.zeros_like(sorted_ref)
    for s in range(shards):
        count[s] = 0
    images = rounded.shape[0] // IMGTOK
    c = c_ref[0]

    def step(i, carry):
        dest = place_ref[c * images + i] // per_shard
        slot = count[dest]
        count[dest] = slot + 1
        block = rounded[rows16(i), :]
        sorted_ref[dest, 0, rows16(slot), :] = block

        @pl.when(dest + 1 < shards)
        def _():
            sorted_ref[dest + 1, 1, rows16(slot), :] = block

        return carry

    lax.fori_loop(0, images, step, 0)
    if len(out_refs) == 1:
        out_refs[0][...] = sorted_ref[...]
    else:
        for u, ref in enumerate(out_refs):
            ref[...] = sorted_ref[c ^ u]


def pack(m, c, place, low, high, weights, part, shards, capacity, per_shard, mixed):
    rows, width = part.shape
    feats = low.shape[1]
    whole = lambda a: pl.BlockSpec(a.shape, lambda i, *_: (0,) * len(a.shape))
    shape = (2, capacity, width)
    if mixed:
        out = [jax.ShapeDtypeStruct(shape, jnp.bfloat16)] * shards
    else:
        out = [jax.ShapeDtypeStruct((shards,) + shape, jnp.bfloat16)]
    return pl.pallas_call(
        functools.partial(pack_body, per_shard),
        grid_spec=pltpu.PrefetchScalarGridSpec(
            num_scalar_prefetch=3,
            grid=(1,),
            in_specs=[
                whole(low),
                whole(high),
                pl.BlockSpec((feats, width), lambda i, m, *_: (m[0] ^ 3, 0)),
                whole(part),
            ],
            out_specs=[whole(a) for a in out],
            scratch_shapes=[
                pltpu.VMEM((rows, width), jnp.bfloat16),
                pltpu.VMEM((shards,) + shape, jnp.bfloat16),
                pltpu.SMEM((shards,), jnp.int32),
            ],
        ),
        out_shape=out,
        cost_estimate=cost(2 * rows * feats * width, part.size * 16),
        compiler_params=params(),
    )(m, c, place, low, high, weights, part)


def slices_body(m_ref, c_ref, own_ref, x_ref, y_ref, low_ref, high_ref, kept_ref, *out_refs):
    m = m_ref[0]
    c = c_ref[0]
    sub = out_refs[0].shape[1]
    half = low_ref.shape[0]
    for u, ref in enumerate((kept_ref,) + out_refs):
        at = pl.ds(0, ref.shape[1]) if u == 0 else pl.ds(pl.multiple_of(m * sub, sub), sub)
        which = m ^ c ^ u
        for k, source in enumerate((own_ref, x_ref, y_ref)):

            @pl.when(which == k)
            def _():
                ref[...] = source[:, at]

        @pl.when(which == 3)
        def _():
            ref[:half, :] = low_ref[:, at]
            ref[half:, :] = high_ref[:, at]


def slices(m, c, blocks, sub):
    rows, feats = blocks[0].shape
    smem = pl.BlockSpec(memory_space=pltpu.SMEM)
    vmem = pl.BlockSpec(memory_space=pltpu.VMEM)
    dtype = blocks[0].dtype
    out = [jax.ShapeDtypeStruct((rows, feats), dtype)]
    out += [jax.ShapeDtypeStruct((rows, sub), dtype)] * 3
    return pl.pallas_call(
        slices_body,
        in_specs=[smem, smem] + [vmem] * len(blocks),
        out_specs=[vmem] * len(out),
        out_shape=out,
        cost_estimate=cost(0, rows * feats * 16),
        compiler_params=params(),
    )(m, c, *blocks)


def attention_body(
    per_shard,
    images,
    c_ref,
    place_ref,
    start_ref,
    q_ref,
    g_ref,
    own_ref,
    prior_ref,
    *refs,
):
    image_refs = refs[:-8]
    out_ref, own_grad_ref, prior_grad_ref, window, probs, grads, total, image_ref = refs[-8:]
    t = pl.program_id(0)
    c = c_ref[0]
    rows = own_ref.shape[0]
    hd = own_ref.shape[1] // 2
    blocks = place_ref.shape[0]
    heads = q_ref.shape[1] // hd
    scale = hd ** (-0.5)

    @pl.when(t == 0)
    def _():
        window[:rows, :] = prior_ref[...]
        window[rows:, :] = own_ref[...]
        total[...] = jnp.zeros_like(total)
        if len(image_refs) == 1:
            image_ref[...] = image_refs[0][...]
        else:
            for u, ref in enumerate(image_refs):
                image_ref[c ^ u] = ref[...]

        def step(b, carry):
            n_own, n_prior = carry
            rank = b // images
            fresh = b % images == 0
            n_own = jnp.where(fresh, 0, n_own)
            n_prior = jnp.where(fresh, 0, n_prior)
            at = place_ref[b] - (c - 1) * per_shard
            is_prior = (at >= 0) & (at < per_shard)
            is_own = (at >= per_shard) & (at < 2 * per_shard)

            @pl.when(is_own)
            def _():
                window[rows16(at), :] = image_ref[rank, 0, rows16(n_own), :]

            @pl.when(is_prior)
            def _():
                window[rows16(at), :] = image_ref[rank, 1, rows16(n_prior), :]

            return n_own + is_own.astype(jnp.int32), n_prior + is_prior.astype(jnp.int32)

        lax.fori_loop(0, blocks, step, (jnp.int32(0), jnp.int32(0)))

    first = t * QTILE

    def stack(ref, a, b):
        return jnp.concatenate([ref[:, h * hd : (h + 1) * hd] for h in range(a, b)], axis=0)

    def tile(span):
        base = pl.multiple_of(first + (full - span), QTILE)
        keys = window[pl.ds(base, span), :hd]
        values = window[pl.ds(base, span), hd:]
        values_t = values.T
        key_pos = lax.broadcasted_iota(jnp.int32, (span, QTILE), 0) + base
        query_pos = lax.broadcasted_iota(jnp.int32, (span, QTILE), 1) + (first + rows)
        allowed = (key_pos <= query_pos) & (key_pos >= start_ref[...])
        bias = jnp.where(allowed, 0.0, -1e30)
        bias = jnp.concatenate([bias, bias], axis=1)

        def products(h):
            query = stack(q_ref, h, h + 2)
            grad = stack(g_ref, h, h + 2)
            return dot(keys, query, NT), dot(values, grad, NT)

        def softmax(h, scores):
            scores = scores * (scale * LOG2E) + bias
            top = jnp.max(scores, axis=0, keepdims=True)
            e = jnp.exp2(scores - top)
            p = e * (1.0 / jnp.sum(e, axis=0, keepdims=True))
            low = p.astype(jnp.bfloat16)
            probs[:span, h * QTILE : (h + 2) * QTILE] = low
            return p, dot(values_t, low, NN)

        def backward(h, p, grad_p, context_t):
            grad_t = stack(g_ref, h, h + 2).astype(jnp.float32).T
            delta = jnp.sum(grad_t * context_t, axis=0, keepdims=True)
            ds = (p * (grad_p - delta)).astype(jnp.bfloat16)
            context = context_t.T.astype(jnp.bfloat16)
            out_ref[:, h * hd : (h + 1) * hd] = context[:QTILE]
            out_ref[:, (h + 1) * hd : (h + 2) * hd] = context[QTILE:]
            grads[:span, h * QTILE : (h + 2) * QTILE] = ds

        pairs = heads // 2
        first_stage, second_stage = {}, {}
        for i in range(pairs + 2):
            if i < pairs:
                first_stage[i] = products(2 * i)
            if 1 <= i <= pairs:
                scores, grad_p = first_stage.pop(i - 1)
                second_stage[i - 1] = (grad_p, *softmax(2 * (i - 1), scores))
            if i >= 2:
                grad_p, p, context_t = second_stage.pop(i - 2)
                backward(2 * (i - 2), p, grad_p, context_t)
        total[pl.ds(base, span), :hd] += dot(grads[:span, :], stack(q_ref, 0, heads), NN)
        total[pl.ds(base, span), hd:] += dot(probs[:span, :], stack(g_ref, 0, heads), NN)

    full = rows + QTILE
    need = full - (jnp.min(start_ref[...]) - first)
    below = 0
    for span in sorted({min(b * QTILE, full) for b in SPANS} | {full}):
        lower, below = below, span

        @pl.when((need > lower) & (need <= span))
        def _():
            tile(span)

    @pl.when(t == pl.num_programs(0) - 1)
    def _():
        total[:, :hd] = total[:, :hd] * scale
        prior_grad_ref[...] = jnp.zeros_like(prior_grad_ref)

        def step(b, carry):
            n_own, n_prior = carry
            at = place_ref[b] - (c - 1) * per_shard
            is_prior = (at >= 0) & (at < per_shard)
            is_own = (at >= per_shard) & (at < 2 * per_shard)

            @pl.when(is_own)
            def _():
                own_grad_ref[rows16(n_own), :] = total[rows16(at), :]

            @pl.when(is_prior)
            def _():
                prior_grad_ref[rows16(n_prior), :] = total[rows16(at), :].astype(jnp.bfloat16)

            return n_own + is_own.astype(jnp.int32), n_prior + is_prior.astype(jnp.int32)

        lax.fori_loop(0, blocks, step, (jnp.int32(0), jnp.int32(0)))


def attention(c, place, start, queries, d_out, own, prior, image, images, per_shard, image_rows):
    ranks = len(image) if len(image) > 1 else image[0].shape[0]
    rows, width = own.shape
    cols = queries.shape[1]
    tiles = rows // QTILE
    span = rows + QTILE
    head_rows = cols // (width // 2) * QTILE
    whole = lambda a: pl.BlockSpec(a.shape, lambda t, *_: (0,) * a.ndim)
    tile = pl.BlockSpec((QTILE, cols), lambda t, *_: (t, 0))
    grad = jax.ShapeDtypeStruct((image_rows, width), jnp.float32)
    prior_grad = jax.ShapeDtypeStruct((image_rows, width), jnp.bfloat16)
    return pl.pallas_call(
        functools.partial(attention_body, per_shard, images),
        grid_spec=pltpu.PrefetchScalarGridSpec(
            num_scalar_prefetch=2,
            grid=(tiles,),
            in_specs=[
                pl.BlockSpec((1, QTILE), lambda t, *_: (0, t)),
                tile,
                tile,
                whole(own),
                whole(prior),
                *map(whole, image),
            ],
            out_specs=[tile, whole(grad), whole(grad)],
            scratch_shapes=[
                pltpu.VMEM((2 * rows, width), jnp.bfloat16),
                pltpu.VMEM((span, head_rows), jnp.bfloat16),
                pltpu.VMEM((span, head_rows), jnp.bfloat16),
                pltpu.VMEM((2 * rows, width), jnp.float32),
                pltpu.VMEM((ranks,) + image[0].shape[-3:], jnp.bfloat16),
            ],
        ),
        out_shape=[jax.ShapeDtypeStruct((rows, cols), jnp.bfloat16), grad, prior_grad],
        cost_estimate=cost(2 * 20 * cols * span * rows, 4 * queries.size * 2),
        compiler_params=params(),
    )(c, place, start, queries, d_out, own, prior, *image)


def reorder_body(per_shard, images, c_ref, place_ref, *refs):
    grad_refs = refs[:-4]
    out_ref, mine_ref, g_ref, count = refs[-4:]
    shards = g_ref.shape[0]
    if len(grad_refs) == 1:
        g_ref[...] = grad_refs[0][...]
    else:
        for u, ref in enumerate(grad_refs):
            g_ref[c_ref[0] ^ u] = ref[...]
    for s in range(shards):
        count[s] = 0
    c = c_ref[0]

    def step(b, carry):
        dest = place_ref[b] // per_shard
        slot = count[dest]
        count[dest] = slot + 1
        out_ref[rows16(b), :] = g_ref[dest, rows16(slot), :]
        return carry

    lax.fori_loop(0, place_ref.shape[0], step, 0)
    rows = mine_ref.shape[0]
    mine_ref[...] = out_ref[pl.ds(pl.multiple_of(c * rows, IMGTOK), rows), :]


def reorder(c, place, gathered, per_shard, images, shards):
    rows, width = gathered[0].shape[-2:]
    dtype = gathered[0].dtype
    smem = pl.BlockSpec(memory_space=pltpu.SMEM)
    vmem = pl.BlockSpec(memory_space=pltpu.VMEM)
    return pl.pallas_call(
        functools.partial(reorder_body, per_shard, images),
        in_specs=[smem, smem] + [vmem] * len(gathered),
        out_specs=[vmem, vmem],
        out_shape=[
            jax.ShapeDtypeStruct((shards * rows, width), dtype),
            jax.ShapeDtypeStruct((rows, width), dtype),
        ],
        scratch_shapes=[
            pltpu.VMEM((shards, rows, width), dtype),
            pltpu.SMEM((shards,), jnp.int32),
        ],
        cost_estimate=cost(0, shards * rows * width * 8),
        compiler_params=params(),
    )(c, place, *gathered)


def weight_body(s_ref, g_ref, out_ref):
    out_ref[...] = dot(s_ref[0], g_ref[...], TN)


def weight_term(states, grad):
    parts, rows, cols = states.shape
    width = grad.shape[1]
    return pl.pallas_call(
        weight_body,
        grid=(parts,),
        in_specs=[
            pl.BlockSpec((1, rows, cols), lambda k: (k, 0, 0)),
            pl.BlockSpec(grad.shape, lambda k: (0, 0)),
        ],
        out_specs=pl.BlockSpec((cols, width), lambda k: (k, 0)),
        out_shape=jax.ShapeDtypeStruct((parts * cols, width), jnp.float32),
        cost_estimate=cost(2 * states.size * width, states.size * 4),
        compiler_params=params(),
    )(states, grad)


def slice_body(first, groups, m_ref, c_ref, kept_ref, g_ref, *refs):
    out_ref = refs[-1]
    ranks, rows, width = g_ref.shape
    m = m_ref[0]
    c = c_ref[0]
    grad = jnp.concatenate([g_ref[c ^ u] for u in range(1, ranks)], axis=0)
    cols = refs[0].shape[1]
    state_refs = list(refs[:-1])
    for k, count in enumerate(groups):
        at = pl.multiple_of((m ^ (first + k)) * cols, cols)
        total = dot(kept_ref[:, pl.ds(at, cols)], g_ref[c], TN)
        done = 0
        for ref in state_refs[:count]:
            total = total + dot(ref[...], grad[done : done + ref.shape[0]], TN)
            done += ref.shape[0]
        state_refs = state_refs[count:]
        out_ref[k] = total


def slice_terms(first, groups, m, c, kept, grad, states):
    cols = states[0].shape[1]
    width = grad.shape[2]
    smem = pl.BlockSpec(memory_space=pltpu.SMEM)
    vmem = pl.BlockSpec(memory_space=pltpu.VMEM)
    rows = grad.shape[0] * grad.shape[1]
    return pl.pallas_call(
        functools.partial(slice_body, first, groups),
        in_specs=[smem, smem] + [vmem] * (2 + len(states)),
        out_specs=vmem,
        out_shape=jax.ShapeDtypeStruct((len(groups), cols, width), jnp.float32),
        cost_estimate=cost(2 * rows * cols * width * len(groups), rows * cols * len(groups) * 4),
        compiler_params=params(),
    )(m, c, kept, grad, *states)


def settle_body(m_ref, *refs):
    out_ref = refs[-1]
    m = m_ref[0]
    half = (len(refs) - 1) // 2
    k = 0
    for own, other in zip(refs[:half], refs[half:-1]):
        for i in range(own.shape[0]):
            cols = own.shape[1]
            at = pl.ds(pl.multiple_of((m ^ k) * cols, cols), cols)
            out_ref[at, :] = own[i] + other[i]
            k += 1


def settle(m, own, other):
    count = sum(a.shape[0] for a in own)
    _, cols, width = own[0].shape
    vmem = pl.BlockSpec(memory_space=pltpu.VMEM)
    return pl.pallas_call(
        settle_body,
        in_specs=[pl.BlockSpec(memory_space=pltpu.SMEM)] + [vmem] * (2 * len(own)),
        out_specs=vmem,
        out_shape=jax.ShapeDtypeStruct((count * cols, width), jnp.float32),
        cost_estimate=cost(0, count * cols * width * 12),
        compiler_params=params(),
    )(m, *own, *other)


def image_body(d_ref, g0, g1, g2, g3, own_ref, first_ref, second_ref, near_ref, far_ref, out_ref):
    half = near_ref.shape[0]
    tile = half // 4
    d = d_ref[0]
    first = jnp.where(d == 0, g1[...], g2[...])
    second = jnp.where(d == 0, g2[...], g1[...])
    for ref, side in ((near_ref, d), (far_ref, 1 - d)):
        for j in range(0, half, tile):
            at = pl.ds(pl.multiple_of(side * half + j, tile), tile)
            total = dot(g0[...], own_ref[at, :], NT) + dot(first, first_ref[at, :], NT)
            total = total + dot(second, second_ref[at, :], NT)
            total = total + dot(g3[...], ref[j : j + tile, :], NT)
            out_ref[:, at] = total.astype(out_ref.dtype)


def image_term(d, grads, weights):
    feats, width = weights[0].shape
    rows = grads[0].shape[0]
    vmem = pl.BlockSpec(memory_space=pltpu.VMEM)
    return pl.pallas_call(
        image_body,
        in_specs=[pl.BlockSpec(memory_space=pltpu.SMEM)] + [vmem] * 9,
        out_specs=vmem,
        out_shape=jax.ShapeDtypeStruct((rows, feats), jnp.bfloat16),
        cost_estimate=cost(8 * feats * width * rows, 8 * feats * width),
        compiler_params=params(),
    )(d, *grads, *weights)


def per_device(image_states, place_index, doc_ids, queries, text_kv, kv_weight, d_out):
    ranks = lax.axis_size("ctx")
    mps = lax.axis_size("mp")
    c = lax.axis_index("ctx")
    d = lax.axis_index("dp")
    rows = queries.shape[1]
    states = image_states[0]
    image_rows, feats = states.shape
    images = image_rows // IMGTOK
    per_shard = rows // IMGTOK
    capacity = IMGTOK * ((images + ranks - 1) // ranks)
    weights = kv_weight[0]
    width = weights.shape[1]
    c1 = jnp.reshape(c, (1,)).astype(jnp.int32)
    d1 = jnp.reshape(d, (1,)).astype(jnp.int32)
    place = place_index[0, ::IMGTOK] // IMGTOK

    m = lax.axis_index("mp")
    m1 = jnp.reshape(m, (1,)).astype(jnp.int32)
    steps = range(1, mps)
    mixed = ranks == mps

    x = trade(states, "mp", 1)
    y = trade(states, "mp", 2)
    low = trade(x[: image_rows // 2], "mp", 2)
    high = trade(y[image_rows // 2 :], "mp", 1)
    part, *slabs = project(m1, d1, [states, x, y], weights)

    prior_text = shift(text_kv[0], "ctx", 1)
    docs = doc_ids[0]
    own_docs = lax.dynamic_slice_in_dim(docs, c * rows, rows)
    prior_docs = lax.dynamic_slice_in_dim(docs, jnp.maximum(c - 1, 0) * rows, rows)
    prior_docs = jnp.where(c > 0, prior_docs, -1)
    key_docs = jnp.concatenate([prior_docs, own_docs])
    start = jnp.sum((key_docs[:, None] < own_docs[None, :]).astype(jnp.int32), axis=0)[None]
    low, high, prior_text, start, place = lax.optimization_barrier(
        (low, high, prior_text, start, place)
    )
    packed = pack(
        m1, c1, place, low, high, weights, part, ranks, capacity, per_shard, mixed
    )

    *slabs, own_slab, _ = lax.optimization_barrier((*slabs, packed[0]))
    cores = lax.axis_size("dp")
    route = [
        (i * mps + j, i * mps + (j ^ (1 + i))) for i in range(cores) for j in range(mps)
    ]
    near = [lax.ppermute(slabs[0], ("dp", "mp"), route), trade(slabs[1], "mp", 3)]

    if mixed:
        c2, _ = lax.optimization_barrier((c1, packed[0]))
        kept, *moved = slices(m1, c2, [states, x, y, low, high], feats // mps)
        image = [trade(packed[s], "ctx", s) if s else packed[0] for s in range(ranks)]
        both = lax.optimization_barrier((*moved, *image))
        moved, image = both[: len(moved)], both[len(moved) :]
        moved = [trade(moved[s - 1], "ctx", s) for s in range(1, ranks)]
    else:
        image = [exchange(packed[0], "ctx")]
        whole = lax.all_gather(states, "mp", axis=1, tiled=True)
        moved = whole.reshape(image_rows, ranks, mps, -1)
        moved = lax.dynamic_index_in_dim(moved, m, axis=2, keepdims=False).transpose(1, 0, 2)
        moved = [exchange(moved, "ctx").reshape(ranks * image_rows, -1)]

    attn_out, own_grad, prior_grad = attention(
        c1, place, start, queries[0], d_out[0], text_kv[0], prior_text, image,
        images, per_shard, image_rows,
    )
    prior_grad, near[0], near[1], *moved = lax.optimization_barrier(
        (prior_grad, near[0], near[1], *moved)
    )
    far = [swap(w, "dp") for w in near]
    grad = own_grad + shift(prior_grad, "ctx", -1).astype(jnp.float32)
    grad = grad.astype(jnp.bfloat16)
    if mixed:
        gathered = [trade(grad, "ctx", s) if s else grad for s in range(ranks)]
        base = jnp.concatenate(moved, axis=0)
        cut = base.shape[0] // 2
        base_x = trade(base, "mp", 1)
        base_y = trade(base, "mp", 2)
    else:
        gathered = [exchange(jnp.broadcast_to(grad, (ranks,) + grad.shape), "ctx")]
        all_states = lax.all_gather(moved[0], "mp", axis=0)
        base_x = base_y = all_states
    base_x, base_y, *gathered = lax.optimization_barrier((base_x, base_y, *gathered))
    by_rank, mine = reorder(c1, place, gathered, per_shard, images, ranks)
    head_grad = [mine] + [trade(mine, "mp", s) for s in steps]
    if mixed:
        base_low = trade(base_x[:cut], "mp", 2)
        base_high = trade(base_y[cut:], "mp", 1)
        by_rank, base_low, base_high, *head_grad = lax.optimization_barrier(
            (by_rank, base_low, base_high, *head_grad)
        )
    image_grad = image_term(d1, head_grad, [own_slab, near[0], far[0], near[1], far[1]])
    if mixed:
        by_rank = by_rank.reshape(ranks, image_rows, width)
        terms = [
            slice_terms(0, (1, 1, 1), m1, c1, kept, by_rank, [base, base_x, base_y]),
            slice_terms(3, (2,), m1, c1, kept, by_rank, [base_low, base_high]),
        ]
        weight_grad = settle(m1, terms, [swap(a, "dp") for a in terms])
    else:
        term = weight_term(all_states, by_rank)
        weight_grad = term + swap(term, "dp")
    return (attn_out[None], image_grad[None], weight_grad[None])


def solution(mesh):
    in_specs = (
        P("dp", "ctx", "mp"),
        P("dp", None),
        P("dp", None),
        P("dp", "ctx", "mp"),
        P("dp", "ctx", "mp"),
        P("mp", None, None),
        P("dp", "ctx", "mp"),
    )
    out_specs = (P("dp", "ctx", "mp"), P("dp", "ctx", "mp"), P("mp", "ctx", None))
    return jax.shard_map(
        per_device, mesh=mesh, in_specs=in_specs, out_specs=out_specs, check_vma=False
    )
```
